32 devices in a mesh: gx: 8 (over y, x, core), gy: 4 (over z).
Axes of the slice: x: 2, y: 2, z: 4, core: 2. Of those that a mesh axis runs over, the one named last changes fastest.
Arguments:
- src_coef: bfloat16 [512, 16384], P(None, ('gx', 'gy')), may hold values from -6 to 6
- point_slot: int32 [1024, 1024], P(None, ('gx', 'gy')), may hold values from 0 to 3
- tgt_owner: int32 [1024, 4], P(('gx', 'gy')), may hold values from 0 to 31, all different within a row; in each aligned block of 32 rows (0 to 31, 32 to 63, ...) at most 8 rows name the same one
- tgt_local: int32 [1024, 4], P(('gx', 'gy')), may hold values from 0 to 31
- vander: bfloat16 [1024, 512], replicated, may hold values from -0.25 to 0.25
- test_fn: bfloat16 [1024, 512], replicated, may hold values from -0.375 to 0.375
- inv_mass: float32 [512, 512], replicated, may hold values from -0.02 to 0.8, as said below
- jacobian: float32 [1024], P(('gx', 'gy')), may hold values from 0.5 to 2
- trace_tab: float32 [512, 128], replicated, may hold values from -0.25 to 0.25
- lift_tab: float32 [128, 512], replicated, may hold values from -0.5 to 0.5
- wave_speed: float32 [16], replicated, may hold values from 0.1 to 0.5
Outputs:
- remapped: float32 [1024, 16, 512], P(('gx', 'gy'))
The draws below stay inside these ranges and needn't reach their ends.
Inputs may be any that keep to these rules, and one draw needn't show every extreme that they name: `tgt_owner`: each source element's 4 intersections have 4 different owners; among the source elements of one device at most 8 intersections have the same owner, and that many in every draw. `inv_mass`: symmetric positive definite.
All inputs are finite; a program needn't handle non-finite values.
Results may differ from the reference program's by a relative error of at most 0.0041.
Values may be sent and summed in bfloat16 or wider, within the bound.
A program may use at most 64 MiB of HBM per device.

```python
import math
import jax
import jax.numpy as jnp
import numpy as np
from jax import lax

P_SIZE = 512
F = 16
Q = 1024
K = 4
FQ = 32
TX = 8
E_DEV = 32
TY = 4
CAP = 8
ELEMS = 1024
N_GX = 8
N_GY = 4


def draw_inv_mass(key, part):
    first_key, second_key = jax.random.split(jax.random.fold_in(key, 7))
    diagonal = jax.random.uniform(first_key, (P_SIZE,), jnp.float32, 0.4, 0.8)
    raw = jax.random.uniform(second_key, (P_SIZE, P_SIZE), jnp.float32, -0.014, 0.014)
    symmetric = (raw + raw.T) * 0.5
    rows = lax_rows = jnp.arange(P_SIZE, dtype=jnp.int32)
    on_diag = (rows[:, None] == lax_rows[None, :]).astype(jnp.float32)
    return symmetric * (1.0 - on_diag) + on_diag * diagonal[:, None]


def with_ends(array, rng, least, largest):
    extent = array.shape
    index_at = [jax.random.randint(jax.random.fold_in(rng, axis), (), 0, extent[axis]) for axis in range(len(extent))]
    array = array.at[tuple(index_at)].set(least)
    longest = extent.index(max(extent))
    index_at[longest] = (index_at[longest] + 1) % extent[longest]
    return array.at[tuple(index_at)].set(largest)


def block_scale(key, extent, cuts, low, high):
    gain, own = 1.0, jax.random.fold_in(key, 6)
    for dim, shards_of in cuts:
        steps = jnp.exp(jax.random.uniform(jax.random.fold_in(own, dim), (shards_of,), jnp.float32, low / len(cuts), high / len(cuts)))
        gain = gain * jnp.repeat(steps, extent[dim] // shards_of).reshape([-1 if axis == dim else 1 for axis in range(len(extent))])
    return gain


def deal_out(stream_key, own, number, rows, count, top, limit, lean):
    order = jax.random.permutation(stream_key, count)
    heavy_load, usual = shares(count, rows * top, limit, lean, True), shares(count, rows * top, limit, lean, False)
    places = jnp.arange(count)

    def named(lengths, offset_by):
        used = int((lengths > 0).sum())
        fixed = max(1, used // 4)
        shifted = fixed + (places - fixed + offset_by * (used - fixed)) % max(1, count - fixed)
        return jnp.zeros((count,), jnp.int32).at[order[jnp.where(places < fixed, places, shifted)]].set(jnp.asarray(lengths, jnp.int32))

    lengths = jnp.where(number % 4 == 0, named(heavy_load, number // 4), named(usual, number - number // 4 - 1))
    mixed = jax.random.permutation(jax.random.fold_in(own, 3), count)
    donor, sink = mixed[0:count // 2 * 2:2], mixed[1:count // 2 * 2:2]
    room = jnp.minimum(lengths[donor] - 1, limit - lengths[sink]) // 2
    room = jnp.where((donor == order[0]) | (sink == order[0]) | (lengths[sink] == 0), 0, jnp.maximum(room, 0))
    shifted = jax.random.randint(jax.random.fold_in(own, 4), (count // 2,), 0, 1 << 20) % (room + 1)
    lengths = lengths.at[donor].add(-shifted).at[sink].add(shifted)
    labels = jnp.searchsorted(jnp.cumsum(lengths), jnp.arange(rows * top), side="right").astype(jnp.int32)
    grid = labels.reshape(top, rows).T
    grid = grid[jax.random.permutation(jax.random.fold_in(own, 1), rows)]
    offset_by = jax.random.randint(jax.random.fold_in(own, 2), (rows, 1), 0, top)
    return jnp.take_along_axis(grid, (jnp.arange(top)[None, :] + offset_by) % top, axis=1)


def shares(amount, total, bound, lean, full):
    weights = [(1 << 20) // math.isqrt(standing ** lean) + 1 for standing in range(1, amount + 1)]
    largest = bound if full else min(bound, max(-(-total // amount), total * weights[0] // sum(weights)))
    least = 1 if total - largest >= amount - 1 else 0
    counts, rest = [largest] + [least] * (amount - 1), total - largest - least * (amount - 1)
    while rest > 0:
        free = [i for i in range(1, amount) if counts[i] < largest] or [i for i in range(1, amount) if counts[i] < bound]
        whole, remaining = sum([weights[i] for i in free]), rest
        for i in free:
            more = min(bound - counts[i], max(1, remaining * weights[i] // whole), rest)
            counts[i] = counts[i] + more
            rest = rest - more
    return np.array(counts)


def scatter_about(rng, dims, scale, limit, cuts=(), kind=jnp.bfloat16):
    drawn = scale * jax.random.normal(rng, dims, jnp.float32)
    if cuts:
        drawn = drawn * block_scale(rng, dims, cuts, -0.22, 0.18)
    return jnp.clip(drawn, -limit, limit).astype(kind)


def setup_inputs(seed: int = 0) -> dict:
    streams_of = jax.random.split(jax.random.key(seed), 12)
    src_coef = scatter_about(streams_of[0], (P_SIZE, ELEMS * F), 1.0, 6.0, ((1, 32),))
    point_slot = with_ends(jax.random.randint(streams_of[1], (Q, ELEMS), 0, K), jax.random.fold_in(streams_of[1], 1), 0, K - 1).astype(jnp.int32)
    tgt_owner_keys = jax.random.split(jax.random.fold_in(streams_of[2], 1), ELEMS // E_DEV)
    tgt_owner_turns = jax.random.permutation(jax.random.fold_in(streams_of[2], 3), ELEMS // E_DEV)
    tgt_owner = jax.vmap(lambda own, number: deal_out(jax.random.fold_in(streams_of[2], 2), own, number, E_DEV, N_GX * N_GY, K, CAP, 2))(tgt_owner_keys, tgt_owner_turns).reshape((ELEMS, K))
    tgt_local = with_ends(jax.random.randint(streams_of[3], (ELEMS, K), 0, E_DEV), jax.random.fold_in(streams_of[3], 1), 0, E_DEV - 1).astype(jnp.int32)
    vander = scatter_about(streams_of[4], (Q, P_SIZE), P_SIZE ** -0.5, 0.25)
    test_fn = scatter_about(streams_of[5], (Q, P_SIZE), (Q // K) ** -0.5, 0.375)
    inv_mass = draw_inv_mass(jax.random.fold_in(streams_of[11], 71), 0)
    jacobian = jnp.clip(jnp.exp(math.log(2.0) - 1.3862944 * jax.random.uniform(streams_of[7], (ELEMS,), jnp.float32) ** block_scale(streams_of[7], (ELEMS,), ((0, 32),), -0.2, 0.2)), 0.5, 2.0)
    trace_tab = scatter_about(streams_of[8], (P_SIZE, 4 * FQ), P_SIZE ** -0.5, 0.25, (), jnp.float32)
    lift_tab = scatter_about(streams_of[9], (4 * FQ, P_SIZE), (4 * FQ) ** -0.5, 0.5, (), jnp.float32)
    wave_speed = jnp.clip(jnp.exp(jax.random.uniform(streams_of[10], (F,), jnp.float32, math.log(0.1), math.log(0.5))), 0.1, 0.5)
    return {"src_coef": src_coef, "point_slot": point_slot, "tgt_owner": tgt_owner, "tgt_local": tgt_local, "vander": vander, "test_fn": test_fn, "inv_mass": inv_mass, "jacobian": jacobian, "trace_tab": trace_tab, "lift_tab": lift_tab, "wave_speed": wave_speed}


def block_pieces(operands, test_fn, slot_count):
    point_vals, slot_ids = operands
    points, members = slot_ids.shape
    fields = point_vals.shape[1] // members
    shaped = point_vals.reshape(points, members, 1, fields)
    chosen = slot_ids[:, :, None] == jnp.arange(slot_count, dtype=jnp.int32)[None, None, :]
    masked = jnp.where(chosen[..., None], shaped, jnp.zeros_like(shaped)).reshape(points, -1)
    moments = lax.dot_general(masked, test_fn, (((0,), (0,)), ((), ())), preferred_element_type=jnp.float32)
    return moments.astype(jnp.bfloat16)


def face_jumps(extended):
    center = extended[1:-1, 1:-1]
    west_jump = extended[:-2, 1:-1, :, 1] - center[:, :, :, 0]
    east_jump = extended[2:, 1:-1, :, 0] - center[:, :, :, 1]
    south_jump = extended[1:-1, :-2, :, 3] - center[:, :, :, 2]
    north_jump = extended[1:-1, 2:, :, 2] - center[:, :, :, 3]
    return jnp.stack([west_jump, east_jump, south_jump, north_jump], axis=3)


def reference(src_coef, point_slot, tgt_owner, tgt_local, vander, test_fn, inv_mass, jacobian, trace_tab, lift_tab, wave_speed):
    highest = lax.Precision.HIGHEST
    devices = N_GX * N_GY
    elements = E_DEV * devices
    coef_blocks = src_coef.reshape(P_SIZE, devices, E_DEV * F).transpose(1, 0, 2)
    slot_blocks = point_slot.reshape(Q, devices, E_DEV).transpose(1, 0, 2)
    target_ids = (tgt_owner * E_DEV + tgt_local).astype(jnp.int32).reshape(devices, E_DEV * K)

    def accumulate(summed, operands):
        coef_part, slot_part, id_part = operands
        point_vals = jnp.dot(vander, coef_part, preferred_element_type=jnp.float32).astype(jnp.bfloat16)
        pieces = block_pieces((point_vals, slot_part), test_fn, K).reshape(E_DEV * K, F * P_SIZE)
        return summed.at[id_part].add(pieces.astype(jnp.float32)), None

    summed, unused = lax.scan(accumulate, jnp.zeros((elements, F * P_SIZE), jnp.float32), (coef_blocks, slot_blocks, target_ids))
    coeffs = jnp.dot(summed.reshape(elements * F, P_SIZE), inv_mass, precision=highest, preferred_element_type=jnp.float32).reshape(elements, F, P_SIZE) / jacobian[:, None, None]
    traces = jnp.dot(coeffs.reshape(elements * F, P_SIZE), trace_tab, precision=highest, preferred_element_type=jnp.float32)
    traces = traces.reshape(N_GX, N_GY, TX, TY, F, 4, FQ).transpose(0, 2, 1, 3, 4, 5, 6).reshape(N_GX * TX, N_GY * TY, F, 4, FQ)
    extended = jnp.pad(traces, ((1, 1), (1, 1), (0, 0), (0, 0), (0, 0)))
    jumps = face_jumps(extended).reshape(N_GX, TX, N_GY, TY, F, 4, FQ).transpose(0, 2, 1, 3, 4, 5, 6).reshape(elements * F, 4 * FQ)
    lifted = jnp.dot(jumps, lift_tab, precision=highest, preferred_element_type=jnp.float32)
    update = jnp.dot(lifted, inv_mass, precision=highest, preferred_element_type=jnp.float32).reshape(elements, F, P_SIZE)
    update = update * wave_speed[None, :, None] / jacobian[:, None, None]
    return coeffs + update
```

```python
import functools

import jax
import jax.numpy as jnp
from jax import lax
from jax.experimental import pallas as pl
from jax.experimental.pallas import tpu as pltpu
from jax.sharding import Mesh, PartitionSpec as P

TX = 8
MESH = pl.DeviceIdType.MESH
GROUP = ("hi", "lo")
WORLD = ("hi", "rep", "lo")


def dot(a, b, dims, precision=None):
    return lax.dot_general(
        a, b, (dims, ((), ())), precision=precision, preferred_element_type=jnp.float32
    )


def neighbour_traces(traces, gx, gy, tx, ty):
    face_cols = traces.shape[1]
    pts = face_cols // 4
    grid = traces.reshape(gx, gy, tx, ty, face_cols).transpose(0, 2, 1, 3, 4)
    grid = grid.reshape(gx * tx, gy * ty, face_cols)
    face = lambda k: grid[:, :, k * pts : (k + 1) * pts]
    west = jnp.pad(face(1)[:-1], ((1, 0), (0, 0), (0, 0)))
    east = jnp.pad(face(0)[1:], ((0, 1), (0, 0), (0, 0)))
    south = jnp.pad(face(3)[:, :-1], ((0, 0), (1, 0), (0, 0)))
    north = jnp.pad(face(2)[:, 1:], ((0, 0), (0, 1), (0, 0)))
    joined = jnp.concatenate([west, east, south, north], axis=2) - grid
    joined = joined.reshape(gx, tx, gy, ty, face_cols).transpose(0, 2, 1, 3, 4)
    return joined.reshape(gx * gy * tx * ty, face_cols)


def peer_at(sizes, offset):
    return tuple(
        lax.rem(lax.axis_index(name) + step, size) if step else lax.axis_index(name)
        for name, size, step in zip(WORLD, sizes, offset)
    )


def offsets(sizes):
    hi, rep, lo = sizes
    every = [(a, b, c) for a in range(hi) for b in range(rep) for c in range(lo)]
    return every[1:]


def greet(peers):
    barrier = pltpu.get_barrier_semaphore()
    for peer in peers:
        pl.semaphore_signal(barrier, inc=1, device_id=peer, device_id_type=MESH)
    pl.semaphore_wait(barrier, len(peers))


def push(src, dst, send, recv, peer):
    copy = pltpu.make_async_remote_copy(
        src_ref=src, dst_ref=dst, send_sem=send, recv_sem=recv, device_id=peer, device_id_type=MESH
    )
    copy.start()
    return copy


def enter_kernel(
    sizes,
    blocks,
    slot_rows,
    meta,
    vander,
    test_fn,
    part,
    metas,
    mine,
    slots,
    onehot,
    pieces,
    block_sems,
    slot_sems,
    relay_sems,
    meta_sems,
    local_sems,
):
    hi, rep, lo = sizes
    h, r, l = (lax.axis_index(name) for name in WORLD)
    me = h * lo + l
    device = (h * rep + r) * lo + l
    everyone = offsets(sizes)
    group = [o for o in everyone if o[1] == 0]
    local = [
        pltpu.make_async_copy(slot_rows, slots.at[me], local_sems.at[0]),
        pltpu.make_async_copy(blocks.at[me], mine.at[me], local_sems.at[1]),
        pltpu.make_async_copy(meta, metas.at[device], local_sems.at[2]),
    ]
    for copy in local:
        copy.start()
    greet([peer_at(sizes, o) for o in everyone])

    along, relays = [], []
    for c in range(1, lo):
        peer = peer_at(sizes, (0, 0, c))
        along.append(
            push(slot_rows, slots.at[me], slot_sems.at[0, c], slot_sems.at[1, c], peer)
        )
    for a in range(1, hi):
        peer = peer_at(sizes, (a, 0, 0))
        k = a * lo
        relays.append(
            push(slot_rows, slots.at[me], relay_sems.at[0, k], relay_sems.at[1, k], peer)
        )
    arrive, labels = [], []
    for k, o in enumerate(group):
        to_h, _, to_l = peer = peer_at(sizes, o)
        arrive.append(
            push(
                blocks.at[to_h * lo + to_l],
                mine.at[me],
                block_sems.at[0, k],
                block_sems.at[1, k],
                peer,
            )
        )
    for k, o in enumerate(everyone):
        labels.append(
            push(
                meta, metas.at[device], meta_sems.at[0, k], meta_sems.at[1, k], peer_at(sizes, o)
            )
        )
    for c in range(1, lo):
        along[c - 1].wait_recv()
        place = h * lo + lax.rem(l + lo - c, lo)
        for a in range(1, hi):
            k = a * lo + c
            relays.append(
                push(
                    slots.at[place],
                    slots.at[place],
                    relay_sems.at[0, k],
                    relay_sems.at[1, k],
                    peer_at(sizes, (a, 0, 0)),
                )
            )
    for copy in local:
        copy.wait()
    for copy in labels:
        copy.wait_recv()

    width = meta.shape[1]
    rows = 128

    @pl.loop(0, part.shape[0] // rows)
    def _(i):
        start = pl.multiple_of(i * rows, rows)
        target = (lax.broadcasted_iota(jnp.int32, (rows, width), 0) + start).astype(jnp.float32)
        for g in range(hi * lo):
            ids = metas[(g // lo * rep + r) * lo + g % lo][0:1, :]
            onehot[pl.ds(start, rows), g * width : (g + 1) * width] = jnp.where(
                target == ids, 1.0, 0.0
            ).astype(onehot.dtype)

    members = slot_rows.shape[0]
    slot_count = width // members
    for a in range(hi):
        for c in range(lo):
            if a or c:
                arrive[a * lo + c - 1].wait_recv()
            if a:
                relays[(a - 1) if c == 0 else (hi - 1) * c + a - 1].wait_recv()
        from_h = lax.rem(h + hi - a, hi)
        first = from_h * lo
        source = mine[pl.ds(first, lo)].reshape(lo * members, -1)
        values = dot(source, vander[...], ((1,), (1,)))
        parts = []
        for c in range(lo):
            where = slots[first + c].astype(jnp.float32)
            value = values[c * members : (c + 1) * members]
            for s in range(slot_count):
                parts.append(jnp.where(where == s, value, 0.0).astype(jnp.bfloat16))
        masked = jnp.concatenate(parts, axis=0)
        pieces[from_h] = dot(masked, test_fn[...], ((1,), (0,))).astype(jnp.bfloat16)

    every = pieces.shape[0] * pieces.shape[1]
    block = 256

    @pl.loop(0, part.shape[0] // block)
    def _(i):
        start = pl.multiple_of(i * block, block)
        summed = dot(
            onehot[pl.ds(start, block), :], pieces[...].reshape(every, -1), ((1,), (0,))
        )
        part[pl.ds(start, block), :] = summed.astype(part.dtype)

    for copy in along + relays + arrive + labels:
        copy.wait_send()


def enter(sizes, blocks, slot_rows, meta, vander, test_fn):
    hi, rep, lo = sizes
    world = hi * rep * lo
    _, members, modes = blocks.shape
    vmem = pl.BlockSpec(memory_space=pltpu.VMEM)
    dma = pltpu.SemaphoreType.DMA
    return pl.pallas_call(
        functools.partial(enter_kernel, sizes),
        out_shape=(
            jax.ShapeDtypeStruct((world * members, modes), jnp.bfloat16),
            jax.ShapeDtypeStruct((world, *meta.shape), meta.dtype),
        ),
        in_specs=[vmem] * 5,
        out_specs=(vmem,) * 2,
        scratch_shapes=[
            pltpu.VMEM(blocks.shape, blocks.dtype),
            pltpu.VMEM((hi * lo, *slot_rows.shape), slot_rows.dtype),
            pltpu.VMEM((world * members, hi * lo * meta.shape[1]), jnp.bfloat16),
            pltpu.VMEM((hi, lo * meta.shape[1], modes), jnp.bfloat16),
            dma((2, hi * lo)),
            dma((2, lo)),
            dma((2, hi * lo)),
            dma((2, world)),
            dma((3,)),
        ],
        compiler_params=pltpu.CompilerParams(
            collective_id=0, has_side_effects=True, vmem_limit_bytes=44 << 20
        ),
        name="enter",
    )(blocks, slot_rows, meta, vander, test_fn)


def leave_kernel(sizes, blocks, mine, sems, local_sem):
    hi, rep, lo = sizes
    me = lax.axis_index("hi") * lo + lax.axis_index("lo")
    group = [o for o in offsets(sizes) if o[1] == 0]
    local = pltpu.make_async_copy(blocks.at[me], mine.at[me], local_sem)
    local.start()
    greet([peer_at(sizes, o) for o in group])
    copies = []
    for k, o in enumerate(group):
        to_h, _, to_l = peer = peer_at(sizes, o)
        copies.append(
            push(blocks.at[to_h * lo + to_l], mine.at[me], sems.at[0, k], sems.at[1, k], peer)
        )
    for copy in copies:
        copy.wait()
    local.wait()


def leave(sizes, blocks):
    vmem = pl.BlockSpec(memory_space=pltpu.VMEM)
    dma = pltpu.SemaphoreType.DMA
    return pl.pallas_call(
        functools.partial(leave_kernel, sizes),
        out_shape=jax.ShapeDtypeStruct(blocks.shape, blocks.dtype),
        in_specs=[vmem],
        out_specs=vmem,
        scratch_shapes=[dma((2, sizes[0] * sizes[2])), dma],
        compiler_params=pltpu.CompilerParams(
            collective_id=1, has_side_effects=True, vmem_limit_bytes=8 << 20
        ),
        name="leave",
    )(blocks)


def per_device(
    gx,
    gy,
    src_coef,
    point_slot,
    tgt_owner,
    tgt_local,
    vander,
    test_fn,
    inv_mass,
    jacobian,
    trace_tab,
    lift_tab,
    wave_speed,
):
    bf16 = jnp.bfloat16
    high = lax.Precision.HIGH
    modes, columns = src_coef.shape
    members = point_slot.shape[1]
    fields = wave_speed.shape[0]
    reps = lax.axis_size("rep")
    my_rep = lax.axis_index("rep")
    my_field = lax.axis_index("hi") * lax.axis_size("lo") + lax.axis_index("lo")

    row = jnp.arange(columns, dtype=jnp.int32)
    wanted = (row % members) * fields + row // members
    perm = (wanted[:, None] == row[None, :]).astype(bf16)
    by_field = dot(perm, src_coef, ((1,), (1,))).astype(bf16)
    sizes = tuple(lax.axis_size(name) for name in WORLD)
    holders = sizes[0] * sizes[2]
    ids = (tgt_owner * members + tgt_local).T.reshape(1, -1).astype(jnp.float32)
    jac = jnp.pad(jacobian[None, :], ((0, 0), (0, ids.shape[1] - members)))
    meta = jnp.pad(jnp.concatenate([ids, jac], axis=0), ((0, 6), (0, 0)))
    part, metas = enter(
        sizes,
        by_field.reshape(holders, members, modes),
        point_slot.T.astype(bf16),
        meta,
        vander,
        test_fn,
    )
    jac = metas[:, 1, :members].reshape(-1, 1)
    if reps == 2:
        other = lax.ppermute(part, "rep", [(0, 1), (1, 0)])
        moments = part.astype(jnp.float32) + other.astype(jnp.float32)
    else:
        moments = lax.psum(part.astype(jnp.float32), "rep")

    coeffs = dot(moments, inv_mass, ((1,), (0,)), high) / jac
    traces = dot(coeffs, trace_tab, ((1,), (0,)), high)
    jumps = neighbour_traces(traces, gx, gy, TX, members // TX)
    own = lambda x: lax.dynamic_index_in_dim(
        x.reshape(-1, reps, gy * members, x.shape[-1]), my_rep, 1, keepdims=False
    ).reshape(-1, x.shape[-1])
    lift = dot(lift_tab, inv_mass, ((1,), (0,)), high)
    speed = lax.dynamic_index_in_dim(wave_speed, my_field, 0, keepdims=False)
    update = dot(own(jumps), lift, ((1,), (0,)), high) * (speed / own(jac))
    result = (own(coeffs) + update).astype(bf16)
    back = leave(sizes, result.reshape(holders, members, modes))
    back = back.transpose(1, 0, 2)
    return back.astype(jnp.float32)


def nt(a, b):
    return dot(a, b, ((1,), (1,)))


def nn(a, b):
    return dot(a, b, ((1,), (0,)))


def split(x):
    high = x.astype(jnp.bfloat16)
    return high, (x - high.astype(jnp.float32)).astype(jnp.bfloat16)


def nn3(a, b):
    (ah, al), (bh, bl) = split(a), split(b)
    return nn(ah, bh) + nn(al, bh) + nn(ah, bl)


def fused_kernel(
    sizes,
    gy,
    src,
    slot_rows,
    owner,
    local_id,
    jac,
    vander_hbm,
    test_hbm,
    inv_hbm,
    trace_hbm,
    lift_hbm,
    speeds,
    out,
    coef,
    slot_in,
    vander,
    test_fn,
    inv,
    trace,
    lift,
    inv_hi,
    inv_lo,
    table,
    lift_inv,
    blocks,
    mine,
    slots,
    meta,
    metas,
    onehot,
    acc,
    part,
    part_in,
    edge,
    edge_in,
    beside,
    result,
    back,
    load_sems,
    slot_send,
    slot_recv,
    block_send,
    block_recv,
    meta_send,
    meta_recv,
    core_send,
    core_recv,
    back_send,
    back_recv,
):
    hi, rep, lo = sizes
    bf16, f32 = jnp.bfloat16, jnp.float32
    h, r, l = (lax.axis_index(name) for name in WORLD)
    me = h * lo + l
    group = hi * lo
    members, points = slot_rows.shape
    modes, columns = src.shape
    slot_count = owner.shape[0]
    fields = columns // members
    ty = members // TX
    width = slot_count * members
    strip = gy * members
    half = hi * strip
    unit = lo * width

    loads = []
    for k, (a, b) in enumerate(
        [
            (src, coef),
            (slot_rows, slot_in),
            (vander_hbm, vander),
            (test_hbm, test_fn),
            (inv_hbm, inv),
            (trace_hbm, trace),
            (lift_hbm, lift),
        ]
    ):
        copy = pltpu.make_async_copy(a, b, load_sems.at[k])
        copy.start()
        loads.append(copy)

    y, x = h // 2, h % 2
    flip_x = y * 2 + (1 - x)
    flip_y = (1 - y) * 2 + x
    flip_xy = (1 - y) * 2 + (1 - x)
    near = [h, flip_x, flip_y, flip_xy]
    core = (h, 1 - r, l)

    barrier = pltpu.get_barrier_semaphore()
    for o in offsets((hi, 1, lo)):
        pl.semaphore_signal(
            barrier, inc=1, device_id=peer_at((hi, 1, lo), o), device_id_type=MESH
        )
    pl.semaphore_signal(barrier, inc=1, device_id=core, device_id_type=MESH)

    meta[...] = jnp.zeros_like(meta)
    meta[0:slot_count, 0:members] = (owner[...] * members + local_id[...]).astype(f32)
    meta[slot_count : slot_count + 1, 0:members] = jac[...]
    packed = meta[...]
    row = lax.broadcasted_iota(jnp.int32, packed.shape, 0)
    lane = lax.broadcasted_iota(jnp.int32, packed.shape, 1)
    ids = jnp.zeros_like(packed)
    for s in range(slot_count):
        turned = pltpu.roll(packed, s * members, 1) if s else packed
        ids = jnp.where((row == s) & (lane // members == s), turned, ids)
    ids = jnp.sum(ids, axis=0, keepdims=True)
    jacs = jnp.zeros_like(packed)
    for c in range(lo):
        turned = pltpu.roll(packed, c * members, 1) if c else packed
        here = (row == slot_count) & (lane // members == c) & (lane // members == l)
        jacs = jnp.where(here, turned, jacs)
    jacs = jnp.sum(jacs, axis=0, keepdims=True)
    packed = jnp.where(row == 0, ids, jnp.where(row == 1, jacs, 0.0))
    meta[...] = packed
    metas[me] = packed

    loads[1].wait()
    slots[me] = slot_in[...].astype(f32).astype(bf16)
    loads[0].wait()
    rows = lo * members
    r_iota = lax.broadcasted_iota(jnp.int32, (rows, columns), 0)
    c_iota = lax.broadcasted_iota(jnp.int32, (rows, columns), 1)
    for k in range(hi):
        wanted = (r_iota % members) * fields + r_iota // members + k * lo
        perm = (wanted == c_iota).astype(f32).astype(bf16)
        moved = nt(perm, coef[...]).astype(bf16)
        blocks[k * lo : (k + 1) * lo] = moved.reshape(lo, members, modes)
    mine[me] = blocks[me]

    pl.semaphore_wait(barrier, group)

    sent = []

    def slot_copy(at, k, to):
        return pltpu.make_async_remote_copy(
            src_ref=slots.at[at],
            dst_ref=slots.at[at],
            send_sem=slot_send.at[k],
            recv_sem=slot_recv.at[at],
            device_id=to,
            device_id_type=MESH,
        )

    def send_slot(at, to, when=None):
        copy = slot_copy(at, len(sent), to)
        sent.append((copy, when))
        if when is None:
            copy.start()
        else:
            pl.when(when)(copy.start)

    def wait_slot(at):
        slot_copy(at, 0, core).wait_recv()

    up, down = jnp.minimum(l + 1, lo - 1), jnp.maximum(l - 1, 0)
    send_slot(me, (h, r, up), l + 1 < lo)
    send_slot(me, (h, r, down), l > 0)
    send_slot(me, (flip_x, r, l))
    send_slot(me, (flip_y, r, l))

    others = []
    for k, to_h in enumerate(near):
        for c in range(1 if k == 0 else 0, lo):
            to_l = (l + c) % lo
            copy = pltpu.make_async_remote_copy(
                src_ref=blocks.at[to_h * lo + to_l],
                dst_ref=mine.at[me],
                send_sem=block_send.at[k * lo + c],
                recv_sem=block_recv.at[me],
                device_id=(to_h, r, to_l),
                device_id_type=MESH,
            )
            copy.start()
            others.append(copy)
    for k, to_h in enumerate(near):
        for c in range(1 if k == 0 else 0, lo):
            to_l = (l + c) % lo
            copy = pltpu.make_async_remote_copy(
                src_ref=meta,
                dst_ref=metas.at[me],
                send_sem=meta_send.at[k * lo + c],
                recv_sem=meta_recv.at[me],
                device_id=(to_h, r, to_l),
                device_id_type=MESH,
            )
            copy.start()
            others.append(copy)

    def wait_block(at):
        pltpu.make_async_remote_copy(
            src_ref=mine.at[at],
            dst_ref=mine.at[at],
            send_sem=block_send.at[0],
            recv_sem=block_recv.at[at],
            device_id=core,
            device_id_type=MESH,
        ).wait_recv()
        pltpu.make_async_remote_copy(
            src_ref=metas.at[at],
            dst_ref=metas.at[at],
            send_sem=meta_send.at[0],
            recv_sem=meta_recv.at[at],
            device_id=core,
            device_id_type=MESH,
        ).wait_recv()

    for copy in loads[2:]:
        copy.wait()
    high, low = split(inv[...])
    inv_hi[...] = high
    inv_lo[...] = low
    traced = nn3(inv[...], trace[...])
    pts = trace.shape[1] // 4
    table[:, : 4 * pts] = traced.astype(bf16)
    face = lax.broadcasted_iota(jnp.int32, traced.shape, 1) // pts
    swapped = jnp.where(
        face % 2 == 0, pltpu.roll(traced, 3 * pts, 1), pltpu.roll(traced, pts, 1)
    )
    table[:, 4 * pts :] = swapped.astype(bf16)
    lift_inv[...] = nn3(lift[...], inv[...]).astype(bf16)

    def relay(z, ok, to, forward):
        z = jnp.clip(z, 0, lo - 1)

        @pl.when(ok)
        def _():
            wait_slot(h * lo + z)

        send_slot(h * lo + z, (h, r, to), ok & forward)
        send_slot(h * lo + z, (flip_x, r, l), ok)
        send_slot(h * lo + z, (flip_y, r, l), ok)

    def turn(z, ok):
        z = jnp.clip(z, 0, lo - 1)

        @pl.when(ok)
        def _():
            wait_slot(flip_x * lo + z)
            wait_slot(flip_y * lo + z)

        send_slot(flip_x * lo + z, (flip_y, r, l), ok & (z % 2 == 0))
        send_slot(flip_y * lo + z, (flip_x, r, l), ok & (z % 2 == 1))

    def relays(k):
        relay(l - k, l >= k, up, l + 1 < lo)
        relay(l + k, l + k < lo, down, l > 0)

    def turns(k):
        if k:
            turn(l - k, l >= k)
            turn(l + k, l + k < lo)
        else:
            turn(l, l >= 0)

    place = lax.broadcasted_iota(jnp.int32, (half, width), 0)
    place = (place // strip) * (2 * strip) + place % strip

    def gather(from_h, k):
        first = from_h * lo
        source = mine[pl.ds(first, lo)].reshape(lo * members, modes)
        values = nt(source, vander[...]).astype(bf16).astype(f32)
        parts = []
        for c in range(lo):
            where = slots[first + c].astype(f32)
            value = values[c * members : (c + 1) * members]
            for s in range(slot_count):
                parts.append(jnp.where(where == s, value, 0.0).astype(bf16))
        pieces = nn(jnp.concatenate(parts, axis=0), test_fn[...]).astype(bf16)
        for side in range(2):
            shift = (1 - r if side == 0 else r) * strip
            for c in range(lo):
                targets = (metas[first + c][0:1, :]).astype(jnp.int32) - shift
                onehot[side, :, c * width : (c + 1) * width] = (
                    jnp.where(place == targets, 1.0, 0.0).astype(bf16)
                )
        return pieces

    def scatter(pieces, side, first):
        summed = nn(onehot[side], pieces)
        return summed if first else acc[side] + summed

    for k in range(1, lo):
        relays(k)
        turns(k - 1)
    for k in range(hi):
        from_h = near[k]
        if k == 1:
            turns(lo - 1)
        if k == 3:
            for c in range(lo):
                wait_slot(from_h * lo + c)
        for c in range(1 if k == 0 else 0, lo):
            wait_block(from_h * lo + (l + c) % lo)
        pieces = gather(from_h, k)
        if k < hi - 1:
            for side in range(2):
                acc[side] = scatter(pieces, side, k == 0)

    def core_copy(a, b, k):
        return pltpu.make_async_remote_copy(
            src_ref=a,
            dst_ref=b,
            send_sem=core_send.at[k],
            recv_sem=core_recv.at[k],
            device_id=core,
            device_id_type=MESH,
        )

    theirs = scatter(pieces, 0, False).astype(bf16)
    part[...] = theirs
    part_copy = core_copy(part, part_in, 0)
    part_copy.start()
    ours = scatter(pieces, 1, False)
    acc[1] = ours
    swap = table[:, 4 * pts :]
    seen = nn(ours.astype(bf16), swap)
    eye_r = lax.broadcasted_iota(jnp.int32, (strip, strip), 0)
    eye_c = lax.broadcasted_iota(jnp.int32, (strip, strip), 1)
    lanes = lax.broadcasted_iota(jnp.int32, (strip, 4 * pts), 1)
    inverse = []
    for k in range(hi):
        jac_row = metas[k * lo][1:2, :]
        for c in range(1, lo):
            jac_row = jac_row + metas[k * lo + c][1:2, :]
        column = jnp.sum(jnp.where(eye_r == eye_c, jac_row, 0.0), axis=1, keepdims=True)
        column = 1.0 / column
        inverse.append(column)
        edge[k * strip : (k + 1) * strip, :] = jnp.where(
            lanes == 4 * pts - 1, column, seen[k * strip : (k + 1) * strip]
        )
    edge_copy = core_copy(edge, edge_in, 1)
    edge_copy.start()
    seen = nn(theirs, swap)
    beside[0:strip, :] = jnp.zeros((strip, 4 * pts), f32)
    beside[(hi + 1) * strip :, :] = jnp.zeros((strip, 4 * pts), f32)
    part_copy.wait_recv()
    edge_copy.wait_recv()
    for k in range(hi):
        got = edge_in[k * strip : (k + 1) * strip, :]
        column = got[:, 4 * pts - 1 : 4 * pts]
        beside[(k + 1) * strip : (k + 2) * strip, :] = (
            seen[k * strip : (k + 1) * strip] + got
        ) * column

    speed = speeds[me]
    t_row = lax.broadcasted_iota(jnp.int32, (strip, 4 * pts), 0)
    d_row, a_row, b_row = t_row // members, (t_row % members) // ty, t_row % ty
    face = lanes // pts
    moved = lambda v, n: pltpu.roll(v, n % strip, 0)
    for k in range(hi):
        own = slice(k * strip, (k + 1) * strip)
        moments = acc[1, own, :] + part_in[own, :].astype(f32)
        m_hi, m_lo = split(moments)
        both = nn(m_hi, table[...]) * inverse[k]
        mine_t, cur = both[:, : 4 * pts], both[:, 4 * pts :]
        prev = beside[pl.ds(pl.multiple_of((k + r) * strip, strip), strip), :]
        after = beside[pl.ds(pl.multiple_of((k + r + 1) * strip, strip), strip), :]
        last = (TX - 1) * ty
        west = jnp.where(a_row > 0, moved(cur, ty), moved(prev, -last))
        east = jnp.where(a_row < TX - 1, moved(cur, -ty), moved(after, last))
        jump = members - (ty - 1)
        south = jnp.where(b_row > 0, moved(cur, 1), moved(cur, jump))
        south = jnp.where((b_row == 0) & (d_row == 0), 0.0, south)
        north = jnp.where(b_row < ty - 1, moved(cur, -1), moved(cur, -jump))
        north = jnp.where((b_row == ty - 1) & (d_row == gy - 1), 0.0, north)
        other = jnp.where(
            face < 2, jnp.where(face == 0, west, east), jnp.where(face == 2, south, north)
        )
        jumps = ((other - mine_t) * speed).astype(bf16)
        solved = nn(m_hi, inv_hi[...]) + nn(m_lo, inv_hi[...]) + nn(m_hi, inv_lo[...])
        solved = (solved + nn(jumps, lift_inv[...])) * inverse[k]
        result[k * lo : (k + 1) * lo] = solved.astype(bf16).reshape(lo, members, modes)
        for c in range(lo):
            to_l = (l + c) % lo

            def back_copy():
                return pltpu.make_async_remote_copy(
                    src_ref=result.at[k * lo + to_l],
                    dst_ref=back.at[me],
                    send_sem=back_send.at[k * lo + c],
                    recv_sem=back_recv.at[me],
                    device_id=(k, r, to_l),
                    device_id_type=MESH,
                )

            if c == 0:
                pl.when(h != k)(lambda: back_copy().start())
            else:
                back_copy().start()
    back[me] = result[me]

    for at in range(group):

        @pl.when(me != at)
        def _():
            pltpu.make_async_remote_copy(
                src_ref=back.at[at],
                dst_ref=back.at[at],
                send_sem=back_send.at[0],
                recv_sem=back_recv.at[at],
                device_id=core,
                device_id_type=MESH,
            ).wait_recv()

    for at in range(group):
        out[:, at, :] = back[at].astype(f32)

    for copy, when in sent:
        if when is None:
            copy.wait_send()
        else:
            pl.when(when)(copy.wait_send)
    for copy in others + [part_copy, edge_copy]:
        copy.wait_send()
    for k in range(hi):
        for c in range(lo):

            def leave_wait():
                pltpu.make_async_remote_copy(
                    src_ref=result.at[k * lo],
                    dst_ref=back.at[me],
                    send_sem=back_send.at[k * lo + c],
                    recv_sem=back_recv.at[me],
                    device_id=core,
                    device_id_type=MESH,
                ).wait_send()

            if c == 0:
                pl.when(h != k)(leave_wait)
            else:
                leave_wait()


def fused(sizes, gy, *args):
    src, slot_rows, owner, _, _, vander, test_fn, inv, trace, lift, speeds = args
    hi, rep, lo = sizes
    members, points = slot_rows.shape
    modes, columns = src.shape
    slot_count = owner.shape[0]
    group = hi * lo
    strip = gy * members
    half = hi * strip
    faces = trace.shape[1]
    width = slot_count * members
    bf16, f32 = jnp.bfloat16, jnp.float32
    any_, vmem = pl.BlockSpec(memory_space=pl.ANY), pl.BlockSpec(memory_space=pltpu.VMEM)
    smem = pl.BlockSpec(memory_space=pltpu.SMEM)
    dma = pltpu.SemaphoreType.DMA
    like = lambda a: pltpu.VMEM(a.shape, a.dtype)
    slot_sends = 4 + (lo - 1) * 6 + 2 + (lo - 1) * 4
    return pl.pallas_call(
        functools.partial(fused_kernel, sizes, gy),
        out_shape=jax.ShapeDtypeStruct((members, columns // members, modes), f32),
        in_specs=[any_, any_, vmem, vmem, vmem, any_, any_, any_, any_, any_, smem],
        out_specs=vmem,
        scratch_shapes=[
            like(src),
            like(slot_rows),
            like(vander),
            like(test_fn),
            like(inv),
            like(trace),
            like(lift),
            pltpu.VMEM(inv.shape, bf16),
            pltpu.VMEM(inv.shape, bf16),
            pltpu.VMEM((modes, 2 * faces), bf16),
            pltpu.VMEM(lift.shape, bf16),
            pltpu.VMEM((group, members, modes), bf16),
            pltpu.VMEM((group, members, modes), bf16),
            pltpu.VMEM((group, members, points), bf16),
            pltpu.VMEM((8, width), f32),
            pltpu.VMEM((group, 8, width), f32),
            pltpu.VMEM((2, half, lo * width), bf16),
            pltpu.VMEM((2, half, modes), f32),
            pltpu.VMEM((half, modes), bf16),
            pltpu.VMEM((half, modes), bf16),
            pltpu.VMEM((half, faces), f32),
            pltpu.VMEM((half, faces), f32),
            pltpu.VMEM((half + 2 * strip, faces), f32),
            pltpu.VMEM((group, members, modes), bf16),
            pltpu.VMEM((group, members, modes), bf16),
            dma((7,)),
            dma((slot_sends,)),
            dma((group,)),
            dma((group,)),
            dma((group,)),
            dma((group,)),
            dma((group,)),
            dma((2,)),
            dma((2,)),
            dma((group,)),
            dma((group,)),
        ],
        compiler_params=pltpu.CompilerParams(
            collective_id=2, has_side_effects=True, vmem_limit_bytes=56 << 20
        ),
        name="remap",
    )(*args)


def fused_device(sizes, gy, src_coef, point_slot, tgt_owner, tgt_local, vander, test_fn, inv_mass, jacobian, trace_tab, lift_tab, wave_speed):
    return fused(
        sizes,
        gy,
        src_coef,
        point_slot.T,
        tgt_owner.T,
        tgt_local.T,
        jacobian[None, :],
        vander,
        test_fn,
        inv_mass,
        trace_tab,
        lift_tab,
        wave_speed,
    )


def solution(mesh):
    gx, gy = mesh.shape["gx"], mesh.shape["gy"]
    devices = gx * gy

    def call(*args):
        fields = args[-1].shape[0]
        sizes = (fields // gy, devices // fields, gy)
        body = functools.partial(per_device, gx, gy)
        if sizes[:2] == (4, 2):
            body = functools.partial(fused_device, sizes, gy)
        return jax.shard_map(
            body,
            mesh=Mesh(mesh.devices.reshape(sizes), WORLD),
            in_specs=(
                P(None, WORLD),
                P(None, WORLD),
                P(WORLD, None),
                P(WORLD, None),
                P(),
                P(),
                P(),
                P(WORLD),
                P(),
                P(),
                P(),
            ),
            out_specs=P(WORLD, None, None),
            check_vma=False,
        )(*args)

    return call
```

```python
import functools

import jax
import jax.numpy as jnp
from jax import lax
from jax.experimental import pallas as pl
from jax.experimental.pallas import tpu as pltpu
from jax.sharding import Mesh, PartitionSpec as P

TX = 8
MESH = pl.DeviceIdType.MESH
GROUP = ("hi", "lo")
WORLD = ("hi", "rep", "lo")


def dot(a, b, dims, precision=None):
    return lax.dot_general(
        a, b, (dims, ((), ())), precision=precision, preferred_element_type=jnp.float32
    )


def neighbour_traces(traces, gx, gy, tx, ty):
    face_cols = traces.shape[1]
    pts = face_cols // 4
    grid = traces.reshape(gx, gy, tx, ty, face_cols).transpose(0, 2, 1, 3, 4)
    grid = grid.reshape(gx * tx, gy * ty, face_cols)
    face = lambda k: grid[:, :, k * pts : (k + 1) * pts]
    west = jnp.pad(face(1)[:-1], ((1, 0), (0, 0), (0, 0)))
    east = jnp.pad(face(0)[1:], ((0, 1), (0, 0), (0, 0)))
    south = jnp.pad(face(3)[:, :-1], ((0, 0), (1, 0), (0, 0)))
    north = jnp.pad(face(2)[:, 1:], ((0, 0), (0, 1), (0, 0)))
    joined = jnp.concatenate([west, east, south, north], axis=2) - grid
    joined = joined.reshape(gx, tx, gy, ty, face_cols).transpose(0, 2, 1, 3, 4)
    return joined.reshape(gx * gy * tx * ty, face_cols)


def peer_at(sizes, offset):
    return tuple(
        lax.rem(lax.axis_index(name) + step, size) if step else lax.axis_index(name)
        for name, size, step in zip(WORLD, sizes, offset)
    )


def offsets(sizes):
    hi, rep, lo = sizes
    every = [(a, b, c) for a in range(hi) for b in range(rep) for c in range(lo)]
    return every[1:]


def greet(peers):
    barrier = pltpu.get_barrier_semaphore()
    for peer in peers:
        pl.semaphore_signal(barrier, inc=1, device_id=peer, device_id_type=MESH)
    pl.semaphore_wait(barrier, len(peers))


def push(src, dst, send, recv, peer):
    copy = pltpu.make_async_remote_copy(
        src_ref=src, dst_ref=dst, send_sem=send, recv_sem=recv, device_id=peer, device_id_type=MESH
    )
    copy.start()
    return copy


def enter_kernel(
    sizes,
    blocks,
    slot_rows,
    meta,
    vander,
    test_fn,
    part,
    metas,
    mine,
    slots,
    onehot,
    pieces,
    block_sems,
    slot_sems,
    relay_sems,
    meta_sems,
    local_sems,
):
    hi, rep, lo = sizes
    h, r, l = (lax.axis_index(name) for name in WORLD)
    me = h * lo + l
    device = (h * rep + r) * lo + l
    everyone = offsets(sizes)
    group = [o for o in everyone if o[1] == 0]
    local = [
        pltpu.make_async_copy(slot_rows, slots.at[me], local_sems.at[0]),
        pltpu.make_async_copy(blocks.at[me], mine.at[me], local_sems.at[1]),
        pltpu.make_async_copy(meta, metas.at[device], local_sems.at[2]),
    ]
    for copy in local:
        copy.start()
    greet([peer_at(sizes, o) for o in everyone])

    along, relays = [], []
    for c in range(1, lo):
        peer = peer_at(sizes, (0, 0, c))
        along.append(
            push(slot_rows, slots.at[me], slot_sems.at[0, c], slot_sems.at[1, c], peer)
        )
    for a in range(1, hi):
        peer = peer_at(sizes, (a, 0, 0))
        k = a * lo
        relays.append(
            push(slot_rows, slots.at[me], relay_sems.at[0, k], relay_sems.at[1, k], peer)
        )
    arrive, labels = [], []
    for k, o in enumerate(group):
        to_h, _, to_l = peer = peer_at(sizes, o)
        arrive.append(
            push(
                blocks.at[to_h * lo + to_l],
                mine.at[me],
                block_sems.at[0, k],
                block_sems.at[1, k],
                peer,
            )
        )
    for k, o in enumerate(everyone):
        labels.append(
            push(
                meta, metas.at[device], meta_sems.at[0, k], meta_sems.at[1, k], peer_at(sizes, o)
            )
        )
    for c in range(1, lo):
        along[c - 1].wait_recv()
        place = h * lo + lax.rem(l + lo - c, lo)
        for a in range(1, hi):
            k = a * lo + c
            relays.append(
                push(
                    slots.at[place],
                    slots.at[place],
                    relay_sems.at[0, k],
                    relay_sems.at[1, k],
                    peer_at(sizes, (a, 0, 0)),
                )
            )
    for copy in local:
        copy.wait()
    for copy in labels:
        copy.wait_recv()

    width = meta.shape[1]
    rows = 128

    @pl.loop(0, part.shape[0] // rows)
    def _(i):
        start = pl.multiple_of(i * rows, rows)
        target = (lax.broadcasted_iota(jnp.int32, (rows, width), 0) + start).astype(jnp.float32)
        for g in range(hi * lo):
            ids = metas[(g // lo * rep + r) * lo + g % lo][0:1, :]
            onehot[pl.ds(start, rows), g * width : (g + 1) * width] = jnp.where(
                target == ids, 1.0, 0.0
            ).astype(onehot.dtype)

    members = slot_rows.shape[0]
    slot_count = width // members
    for a in range(hi):
        for c in range(lo):
            if a or c:
                arrive[a * lo + c - 1].wait_recv()
            if a:
                relays[(a - 1) if c == 0 else (hi - 1) * c + a - 1].wait_recv()
        from_h = lax.rem(h + hi - a, hi)
        first = from_h * lo
        source = mine[pl.ds(first, lo)].reshape(lo * members, -1)
        values = dot(source, vander[...], ((1,), (1,)))
        parts = []
        for c in range(lo):
            where = slots[first + c].astype(jnp.float32)
            value = values[c * members : (c + 1) * members]
            for s in range(slot_count):
                parts.append(jnp.where(where == s, value, 0.0).astype(jnp.bfloat16))
        masked = jnp.concatenate(parts, axis=0)
        pieces[from_h] = dot(masked, test_fn[...], ((1,), (0,))).astype(jnp.bfloat16)

    every = pieces.shape[0] * pieces.shape[1]
    block = 256

    @pl.loop(0, part.shape[0] // block)
    def _(i):
        start = pl.multiple_of(i * block, block)
        summed = dot(
            onehot[pl.ds(start, block), :], pieces[...].reshape(every, -1), ((1,), (0,))
        )
        part[pl.ds(start, block), :] = summed.astype(part.dtype)

    for copy in along + relays + arrive + labels:
        copy.wait_send()


def enter(sizes, blocks, slot_rows, meta, vander, test_fn):
    hi, rep, lo = sizes
    world = hi * rep * lo
    _, members, modes = blocks.shape
    vmem = pl.BlockSpec(memory_space=pltpu.VMEM)
    dma = pltpu.SemaphoreType.DMA
    return pl.pallas_call(
        functools.partial(enter_kernel, sizes),
        out_shape=(
            jax.ShapeDtypeStruct((world * members, modes), jnp.bfloat16),
            jax.ShapeDtypeStruct((world, *meta.shape), meta.dtype),
        ),
        in_specs=[vmem] * 5,
        out_specs=(vmem,) * 2,
        scratch_shapes=[
            pltpu.VMEM(blocks.shape, blocks.dtype),
            pltpu.VMEM((hi * lo, *slot_rows.shape), slot_rows.dtype),
            pltpu.VMEM((world * members, hi * lo * meta.shape[1]), jnp.bfloat16),
            pltpu.VMEM((hi, lo * meta.shape[1], modes), jnp.bfloat16),
            dma((2, hi * lo)),
            dma((2, lo)),
            dma((2, hi * lo)),
            dma((2, world)),
            dma((3,)),
        ],
        compiler_params=pltpu.CompilerParams(
            collective_id=0, has_side_effects=True, vmem_limit_bytes=44 << 20
        ),
        name="enter",
    )(blocks, slot_rows, meta, vander, test_fn)


def leave_kernel(sizes, blocks, mine, sems, local_sem):
    hi, rep, lo = sizes
    me = lax.axis_index("hi") * lo + lax.axis_index("lo")
    group = [o for o in offsets(sizes) if o[1] == 0]
    local = pltpu.make_async_copy(blocks.at[me], mine.at[me], local_sem)
    local.start()
    greet([peer_at(sizes, o) for o in group])
    copies = []
    for k, o in enumerate(group):
        to_h, _, to_l = peer = peer_at(sizes, o)
        copies.append(
            push(blocks.at[to_h * lo + to_l], mine.at[me], sems.at[0, k], sems.at[1, k], peer)
        )
    for copy in copies:
        copy.wait()
    local.wait()


def leave(sizes, blocks):
    vmem = pl.BlockSpec(memory_space=pltpu.VMEM)
    dma = pltpu.SemaphoreType.DMA
    return pl.pallas_call(
        functools.partial(leave_kernel, sizes),
        out_shape=jax.ShapeDtypeStruct(blocks.shape, blocks.dtype),
        in_specs=[vmem],
        out_specs=vmem,
        scratch_shapes=[dma((2, sizes[0] * sizes[2])), dma],
        compiler_params=pltpu.CompilerParams(
            collective_id=1, has_side_effects=True, vmem_limit_bytes=8 << 20
        ),
        name="leave",
    )(blocks)


def per_device(
    gx,
    gy,
    src_coef,
    point_slot,
    tgt_owner,
    tgt_local,
    vander,
    test_fn,
    inv_mass,
    jacobian,
    trace_tab,
    lift_tab,
    wave_speed,
):
    bf16 = jnp.bfloat16
    high = lax.Precision.HIGH
    modes, columns = src_coef.shape
    members = point_slot.shape[1]
    fields = wave_speed.shape[0]
    reps = lax.axis_size("rep")
    my_rep = lax.axis_index("rep")
    my_field = lax.axis_index("hi") * lax.axis_size("lo") + lax.axis_index("lo")

    row = jnp.arange(columns, dtype=jnp.int32)
    wanted = (row % members) * fields + row // members
    perm = (wanted[:, None] == row[None, :]).astype(bf16)
    by_field = dot(perm, src_coef, ((1,), (1,))).astype(bf16)
    sizes = tuple(lax.axis_size(name) for name in WORLD)
    holders = sizes[0] * sizes[2]
    ids = (tgt_owner * members + tgt_local).T.reshape(1, -1).astype(jnp.float32)
    jac = jnp.pad(jacobian[None, :], ((0, 0), (0, ids.shape[1] - members)))
    meta = jnp.pad(jnp.concatenate([ids, jac], axis=0), ((0, 6), (0, 0)))
    part, metas = enter(
        sizes,
        by_field.reshape(holders, members, modes),
        point_slot.T.astype(bf16),
        meta,
        vander,
        test_fn,
    )
    jac = metas[:, 1, :members].reshape(-1, 1)
    if reps == 2:
        other = lax.ppermute(part, "rep", [(0, 1), (1, 0)])
        moments = part.astype(jnp.float32) + other.astype(jnp.float32)
    else:
        moments = lax.psum(part.astype(jnp.float32), "rep")

    coeffs = dot(moments, inv_mass, ((1,), (0,)), high) / jac
    traces = dot(coeffs, trace_tab, ((1,), (0,)), high)
    jumps = neighbour_traces(traces, gx, gy, TX, members // TX)
    own = lambda x: lax.dynamic_index_in_dim(
        x.reshape(-1, reps, gy * members, x.shape[-1]), my_rep, 1, keepdims=False
    ).reshape(-1, x.shape[-1])
    lift = dot(lift_tab, inv_mass, ((1,), (0,)), high)
    speed = lax.dynamic_index_in_dim(wave_speed, my_field, 0, keepdims=False)
    update = dot(own(jumps), lift, ((1,), (0,)), high) * (speed / own(jac))
    result = (own(coeffs) + update).astype(bf16)
    back = leave(sizes, result.reshape(holders, members, modes))
    back = back.transpose(1, 0, 2)
    return back.astype(jnp.float32)


def nt(a, b):
    return dot(a, b, ((1,), (1,)))


def nn(a, b):
    return dot(a, b, ((1,), (0,)))


def split(x):
    high = x.astype(jnp.bfloat16)
    return high, (x - high.astype(jnp.float32)).astype(jnp.bfloat16)


def nn3(a, b):
    (ah, al), (bh, bl) = split(a), split(b)
    return nn(ah, bh) + nn(al, bh) + nn(ah, bl)


def fused_kernel(
    sizes,
    gy,
    src,
    slot_rows,
    owner,
    local_id,
    jac,
    vander_hbm,
    test_hbm,
    inv_hbm,
    trace_hbm,
    lift_hbm,
    speeds,
    out,
    coef,
    slot_in,
    vander,
    test_fn,
    inv,
    trace,
    lift,
    inv_hi,
    inv_lo,
    table,
    lift_inv,
    blocks,
    mine,
    slots,
    meta,
    metas,
    onehot,
    acc,
    part,
    part_in,
    edge,
    edge_in,
    beside,
    result,
    back,
    load_sems,
    slot_send,
    slot_recv,
    block_send,
    block_recv,
    meta_send,
    meta_recv,
    core_send,
    core_recv,
    back_send,
    back_recv,
):
    hi, rep, lo = sizes
    bf16, f32 = jnp.bfloat16, jnp.float32
    h, r, l = (lax.axis_index(name) for name in WORLD)
    me = h * lo + l
    group = hi * lo
    members, points = slot_rows.shape
    modes, columns = src.shape
    slot_count = owner.shape[0]
    fields = columns // members
    ty = members // TX
    width = slot_count * members
    strip = gy * members
    half = hi * strip
    unit = lo * width

    loads = []
    for k, (a, b) in enumerate(
        [
            (src, coef),
            (slot_rows, slot_in),
            (vander_hbm, vander),
            (test_hbm, test_fn),
            (inv_hbm, inv),
            (trace_hbm, trace),
            (lift_hbm, lift),
        ]
    ):
        copy = pltpu.make_async_copy(a, b, load_sems.at[k])
        copy.start()
        loads.append(copy)

    y, x = h // 2, h % 2
    flip_x = y * 2 + (1 - x)
    flip_y = (1 - y) * 2 + x
    flip_xy = (1 - y) * 2 + (1 - x)
    near = [h, flip_x, flip_y, flip_xy]
    core = (h, 1 - r, l)

    barrier = pltpu.get_barrier_semaphore()
    for o in offsets((hi, 1, lo)):
        pl.semaphore_signal(
            barrier, inc=1, device_id=peer_at((hi, 1, lo), o), device_id_type=MESH
        )
    pl.semaphore_signal(barrier, inc=1, device_id=core, device_id_type=MESH)

    meta[...] = jnp.zeros_like(meta)
    meta[0:slot_count, 0:members] = (owner[...] * members + local_id[...]).astype(f32)
    meta[slot_count : slot_count + 1, 0:members] = jac[...]
    packed = meta[...]
    row = lax.broadcasted_iota(jnp.int32, packed.shape, 0)
    lane = lax.broadcasted_iota(jnp.int32, packed.shape, 1)
    ids = jnp.zeros_like(packed)
    for s in range(slot_count):
        turned = pltpu.roll(packed, s * members, 1) if s else packed
        ids = jnp.where((row == s) & (lane // members == s), turned, ids)
    ids = jnp.sum(ids, axis=0, keepdims=True)
    jacs = jnp.zeros_like(packed)
    for c in range(lo):
        turned = pltpu.roll(packed, c * members, 1) if c else packed
        here = (row == slot_count) & (lane // members == c) & (lane // members == l)
        jacs = jnp.where(here, turned, jacs)
    jacs = jnp.sum(jacs, axis=0, keepdims=True)
    packed = jnp.where(row == 0, ids, jnp.where(row == 1, jacs, 0.0))
    meta[...] = packed
    metas[me] = packed

    loads[1].wait()
    slots[me] = slot_in[...].astype(f32).astype(bf16)
    loads[0].wait()
    rows = lo * members
    r_iota = lax.broadcasted_iota(jnp.int32, (rows, columns), 0)
    c_iota = lax.broadcasted_iota(jnp.int32, (rows, columns), 1)
    for k in range(hi):
        wanted = (r_iota % members) * fields + r_iota // members + k * lo
        perm = (wanted == c_iota).astype(f32).astype(bf16)
        moved = nt(perm, coef[...]).astype(bf16)
        blocks[k * lo : (k + 1) * lo] = moved.reshape(lo, members, modes)
    mine[me] = blocks[me]

    pl.semaphore_wait(barrier, group)

    sent = []

    def slot_copy(at, k, to):
        return pltpu.make_async_remote_copy(
            src_ref=slots.at[at],
            dst_ref=slots.at[at],
            send_sem=slot_send.at[k],
            recv_sem=slot_recv.at[at],
            device_id=to,
            device_id_type=MESH,
        )

    def send_slot(at, to):
        copy = slot_copy(at, len(sent), to)
        sent.append(copy)
        copy.start()

    def wait_slot(at):
        slot_copy(at, 0, core).wait_recv()

    for c in (2, 1, 3):
        send_slot(me, (h, r, (l + c) % lo))
    for to_h in (flip_x, flip_y, flip_xy):
        send_slot(me, (to_h, r, l))

    others = []

    def send_block(k, c):
        to_h, to_l = near[k], (l + c) % lo
        copy = pltpu.make_async_remote_copy(
            src_ref=blocks.at[to_h * lo + to_l],
            dst_ref=mine.at[me],
            send_sem=block_send.at[k * lo + c],
            recv_sem=block_recv.at[me],
            device_id=(to_h, r, to_l),
            device_id_type=MESH,
        )
        copy.start()
        others.append(copy)

    for k, to_h in enumerate(near):
        for c in range(1 if k == 0 else 0, lo):
            to_l = (l + c) % lo
            copy = pltpu.make_async_remote_copy(
                src_ref=meta,
                dst_ref=metas.at[me],
                send_sem=meta_send.at[k * lo + c],
                recv_sem=meta_recv.at[me],
                device_id=(to_h, r, to_l),
                device_id_type=MESH,
            )
            copy.start()
            others.append(copy)

    line = [h * lo + (l + c) % lo for c in (1, 3, 2)]
    for i, at in enumerate(line):
        wait_slot(at)
        send_slot(at, (flip_x, r, l))
        send_block(1, (1, 3, 2)[i])
        send_block(0, (1, 3, 2)[i])
        send_slot(at, (flip_y, r, l))
        send_block(2, (1, 3, 2)[i])
    send_block(1, 0)
    send_block(2, 0)
    for i, at in enumerate(line):
        send_slot(at, (flip_xy, r, l))
        send_block(3, (1, 3, 2, 0)[i])
    send_block(3, 0)

    def wait_block(at):
        pltpu.make_async_remote_copy(
            src_ref=mine.at[at],
            dst_ref=mine.at[at],
            send_sem=block_send.at[0],
            recv_sem=block_recv.at[at],
            device_id=core,
            device_id_type=MESH,
        ).wait_recv()
        pltpu.make_async_remote_copy(
            src_ref=metas.at[at],
            dst_ref=metas.at[at],
            send_sem=meta_send.at[0],
            recv_sem=meta_recv.at[at],
            device_id=core,
            device_id_type=MESH,
        ).wait_recv()

    for copy in loads[2:]:
        copy.wait()
    high, low = split(inv[...])
    inv_hi[...] = high
    inv_lo[...] = low
    traced = nn3(inv[...], trace[...])
    pts = trace.shape[1] // 4
    table[:, : 4 * pts] = traced.astype(bf16)
    face = lax.broadcasted_iota(jnp.int32, traced.shape, 1) // pts
    swapped = jnp.where(
        face % 2 == 0, pltpu.roll(traced, 3 * pts, 1), pltpu.roll(traced, pts, 1)
    )
    table[:, 4 * pts :] = swapped.astype(bf16)
    lift_inv[...] = nn3(lift[...], inv[...]).astype(bf16)

    place = lax.broadcasted_iota(jnp.int32, (half, width), 0)
    place = (place // strip) * (2 * strip) + place % strip

    def gather(from_h, k):
        first = from_h * lo
        source = mine[pl.ds(first, lo)].reshape(lo * members, modes)
        values = nt(source, vander[...]).astype(bf16).astype(f32)
        parts = []
        for c in range(lo):
            where = slots[first + c].astype(f32)
            value = values[c * members : (c + 1) * members]
            for s in range(slot_count):
                parts.append(jnp.where(where == s, value, 0.0).astype(bf16))
        pieces = nn(jnp.concatenate(parts, axis=0), test_fn[...]).astype(bf16)
        for side in range(2):
            shift = (1 - r if side == 0 else r) * strip
            for c in range(lo):
                targets = (metas[first + c][0:1, :]).astype(jnp.int32) - shift
                onehot[side, :, c * width : (c + 1) * width] = (
                    jnp.where(place == targets, 1.0, 0.0).astype(bf16)
                )
        return pieces

    def scatter(pieces, side, first):
        summed = nn(onehot[side], pieces)
        return summed if first else acc[side] + summed

    for k in range(hi):
        from_h = near[k]
        if k:
            for c in range(lo):
                wait_slot(from_h * lo + c)
        for c in range(1 if k == 0 else 0, lo):
            wait_block(from_h * lo + (l + c) % lo)
        pieces = gather(from_h, k)
        if k < hi - 1:
            for side in range(2):
                acc[side] = scatter(pieces, side, k == 0)

    def core_copy(a, b, k):
        return pltpu.make_async_remote_copy(
            src_ref=a,
            dst_ref=b,
            send_sem=core_send.at[k],
            recv_sem=core_recv.at[k],
            device_id=core,
            device_id_type=MESH,
        )

    theirs = scatter(pieces, 0, False).astype(bf16)
    part[...] = theirs
    part_copy = core_copy(part, part_in, 0)
    part_copy.start()
    ours = scatter(pieces, 1, False)
    acc[1] = ours
    swap = table[:, 4 * pts :]
    seen = nn(ours.astype(bf16), swap)
    eye_r = lax.broadcasted_iota(jnp.int32, (strip, strip), 0)
    eye_c = lax.broadcasted_iota(jnp.int32, (strip, strip), 1)
    lanes = lax.broadcasted_iota(jnp.int32, (strip, 4 * pts), 1)
    inverse = []
    for k in range(hi):
        jac_row = metas[k * lo][1:2, :]
        for c in range(1, lo):
            jac_row = jac_row + metas[k * lo + c][1:2, :]
        column = jnp.sum(jnp.where(eye_r == eye_c, jac_row, 0.0), axis=1, keepdims=True)
        column = 1.0 / column
        inverse.append(column)
        edge[k * strip : (k + 1) * strip, :] = jnp.where(
            lanes == 4 * pts - 1, column, seen[k * strip : (k + 1) * strip]
        )
    edge_copy = core_copy(edge, edge_in, 1)
    edge_copy.start()
    seen = nn(theirs, swap)
    beside[0:strip, :] = jnp.zeros((strip, 4 * pts), f32)
    beside[(hi + 1) * strip :, :] = jnp.zeros((strip, 4 * pts), f32)
    part_copy.wait_recv()
    edge_copy.wait_recv()
    for k in range(hi):
        got = edge_in[k * strip : (k + 1) * strip, :]
        column = got[:, 4 * pts - 1 : 4 * pts]
        beside[(k + 1) * strip : (k + 2) * strip, :] = (
            seen[k * strip : (k + 1) * strip] + got
        ) * column

    speed = speeds[me]
    t_row = lax.broadcasted_iota(jnp.int32, (strip, 4 * pts), 0)
    d_row, a_row, b_row = t_row // members, (t_row % members) // ty, t_row % ty
    face = lanes // pts
    moved = lambda v, n: pltpu.roll(v, n % strip, 0)
    for k in range(hi):
        own = slice(k * strip, (k + 1) * strip)
        moments = acc[1, own, :] + part_in[own, :].astype(f32)
        m_hi, m_lo = split(moments)
        both = nn(m_hi, table[...]) * inverse[k]
        mine_t, cur = both[:, : 4 * pts], both[:, 4 * pts :]
        prev = beside[pl.ds(pl.multiple_of((k + r) * strip, strip), strip), :]
        after = beside[pl.ds(pl.multiple_of((k + r + 1) * strip, strip), strip), :]
        last = (TX - 1) * ty
        west = jnp.where(a_row > 0, moved(cur, ty), moved(prev, -last))
        east = jnp.where(a_row < TX - 1, moved(cur, -ty), moved(after, last))
        jump = members - (ty - 1)
        south = jnp.where(b_row > 0, moved(cur, 1), moved(cur, jump))
        south = jnp.where((b_row == 0) & (d_row == 0), 0.0, south)
        north = jnp.where(b_row < ty - 1, moved(cur, -1), moved(cur, -jump))
        north = jnp.where((b_row == ty - 1) & (d_row == gy - 1), 0.0, north)
        other = jnp.where(
            face < 2, jnp.where(face == 0, west, east), jnp.where(face == 2, south, north)
        )
        jumps = ((other - mine_t) * speed).astype(bf16)
        solved = nn(m_hi, inv_hi[...]) + nn(m_lo, inv_hi[...]) + nn(m_hi, inv_lo[...])
        solved = (solved + nn(jumps, lift_inv[...])) * inverse[k]
        result[k * lo : (k + 1) * lo] = solved.astype(bf16).reshape(lo, members, modes)
        for c in range(lo):
            to_l = (l + c) % lo

            def back_copy():
                return pltpu.make_async_remote_copy(
                    src_ref=result.at[k * lo + to_l],
                    dst_ref=back.at[me],
                    send_sem=back_send.at[k * lo + c],
                    recv_sem=back_recv.at[me],
                    device_id=(k, r, to_l),
                    device_id_type=MESH,
                )

            if c == 0:
                pl.when(h != k)(lambda: back_copy().start())
            else:
                back_copy().start()
    back[me] = result[me]

    for at in range(group):

        @pl.when(me != at)
        def _():
            pltpu.make_async_remote_copy(
                src_ref=back.at[at],
                dst_ref=back.at[at],
                send_sem=back_send.at[0],
                recv_sem=back_recv.at[at],
                device_id=core,
                device_id_type=MESH,
            ).wait_recv()

    for at in range(group):
        out[:, at, :] = back[at].astype(f32)

    for copy in sent + others + [part_copy, edge_copy]:
        copy.wait_send()
    for k in range(hi):
        for c in range(lo):

            def leave_wait():
                pltpu.make_async_remote_copy(
                    src_ref=result.at[k * lo],
                    dst_ref=back.at[me],
                    send_sem=back_send.at[k * lo + c],
                    recv_sem=back_recv.at[me],
                    device_id=core,
                    device_id_type=MESH,
                ).wait_send()

            if c == 0:
                pl.when(h != k)(leave_wait)
            else:
                leave_wait()


def fused(sizes, gy, *args):
    src, slot_rows, owner, _, _, vander, test_fn, inv, trace, lift, speeds = args
    hi, rep, lo = sizes
    members, points = slot_rows.shape
    modes, columns = src.shape
    slot_count = owner.shape[0]
    group = hi * lo
    strip = gy * members
    half = hi * strip
    faces = trace.shape[1]
    width = slot_count * members
    bf16, f32 = jnp.bfloat16, jnp.float32
    any_, vmem = pl.BlockSpec(memory_space=pl.ANY), pl.BlockSpec(memory_space=pltpu.VMEM)
    smem = pl.BlockSpec(memory_space=pltpu.SMEM)
    dma = pltpu.SemaphoreType.DMA
    like = lambda a: pltpu.VMEM(a.shape, a.dtype)
    slot_sends = 6 + (lo - 1) * 3
    return pl.pallas_call(
        functools.partial(fused_kernel, sizes, gy),
        out_shape=pltpu.VMEM((members, columns // members, modes), f32),
        in_specs=[any_, any_, vmem, vmem, vmem, any_, any_, any_, any_, any_, smem],
        out_specs=vmem,
        scratch_shapes=[
            like(src),
            like(slot_rows),
            like(vander),
            like(test_fn),
            like(inv),
            like(trace),
            like(lift),
            pltpu.VMEM(inv.shape, bf16),
            pltpu.VMEM(inv.shape, bf16),
            pltpu.VMEM((modes, 2 * faces), bf16),
            pltpu.VMEM(lift.shape, bf16),
            pltpu.VMEM((group, members, modes), bf16),
            pltpu.VMEM((group, members, modes), bf16),
            pltpu.VMEM((group, members, points), bf16),
            pltpu.VMEM((8, width), f32),
            pltpu.VMEM((group, 8, width), f32),
            pltpu.VMEM((2, half, lo * width), bf16),
            pltpu.VMEM((2, half, modes), f32),
            pltpu.VMEM((half, modes), bf16),
            pltpu.VMEM((half, modes), bf16),
            pltpu.VMEM((half, faces), f32),
            pltpu.VMEM((half, faces), f32),
            pltpu.VMEM((half + 2 * strip, faces), f32),
            pltpu.VMEM((group, members, modes), bf16),
            pltpu.VMEM((group, members, modes), bf16),
            dma((7,)),
            dma((slot_sends,)),
            dma((group,)),
            dma((group,)),
            dma((group,)),
            dma((group,)),
            dma((group,)),
            dma((2,)),
            dma((2,)),
            dma((group,)),
            dma((group,)),
        ],
        compiler_params=pltpu.CompilerParams(
            collective_id=2, has_side_effects=True, vmem_limit_bytes=56 << 20
        ),
        name="remap",
    )(*args)


def fused_device(sizes, gy, src_coef, point_slot, tgt_owner, tgt_local, vander, test_fn, inv_mass, jacobian, trace_tab, lift_tab, wave_speed):
    return fused(
        sizes,
        gy,
        src_coef,
        point_slot.T,
        tgt_owner.T,
        tgt_local.T,
        jacobian[None, :],
        vander,
        test_fn,
        inv_mass,
        trace_tab,
        lift_tab,
        wave_speed,
    )


def solution(mesh):
    gx, gy = mesh.shape["gx"], mesh.shape["gy"]
    devices = gx * gy

    def call(*args):
        fields = args[-1].shape[0]
        sizes = (fields // gy, devices // fields, gy)
        body = functools.partial(per_device, gx, gy)
        if sizes == (4, 2, 4):
            body = functools.partial(fused_device, sizes, gy)
        return jax.shard_map(
            body,
            mesh=Mesh(mesh.devices.reshape(sizes), WORLD),
            in_specs=(
                P(None, WORLD),
                P(None, WORLD),
                P(WORLD, None),
                P(WORLD, None),
                P(),
                P(),
                P(),
                P(WORLD),
                P(),
                P(),
                P(),
            ),
            out_specs=P(WORLD, None, None),
            check_vma=False,
        )(*args)

    return call
```

```python
import functools

import jax
import jax.numpy as jnp
from jax import lax
from jax.experimental import pallas as pl
from jax.experimental.pallas import tpu as pltpu
from jax.sharding import Mesh, PartitionSpec as P

TX = 8
MESH = pl.DeviceIdType.MESH
GROUP = ("hi", "lo")
WORLD = ("hi", "rep", "lo")


def dot(a, b, dims, precision=None):
    return lax.dot_general(
        a, b, (dims, ((), ())), precision=precision, preferred_element_type=jnp.float32
    )


def neighbour_traces(traces, gx, gy, tx, ty):
    face_cols = traces.shape[1]
    pts = face_cols // 4
    grid = traces.reshape(gx, gy, tx, ty, face_cols).transpose(0, 2, 1, 3, 4)
    grid = grid.reshape(gx * tx, gy * ty, face_cols)
    face = lambda k: grid[:, :, k * pts : (k + 1) * pts]
    west = jnp.pad(face(1)[:-1], ((1, 0), (0, 0), (0, 0)))
    east = jnp.pad(face(0)[1:], ((0, 1), (0, 0), (0, 0)))
    south = jnp.pad(face(3)[:, :-1], ((0, 0), (1, 0), (0, 0)))
    north = jnp.pad(face(2)[:, 1:], ((0, 0), (0, 1), (0, 0)))
    joined = jnp.concatenate([west, east, south, north], axis=2) - grid
    joined = joined.reshape(gx, tx, gy, ty, face_cols).transpose(0, 2, 1, 3, 4)
    return joined.reshape(gx * gy * tx * ty, face_cols)


def peer_at(sizes, offset):
    return tuple(
        lax.rem(lax.axis_index(name) + step, size) if step else lax.axis_index(name)
        for name, size, step in zip(WORLD, sizes, offset)
    )


def offsets(sizes):
    hi, rep, lo = sizes
    every = [(a, b, c) for a in range(hi) for b in range(rep) for c in range(lo)]
    return every[1:]


def greet(peers):
    barrier = pltpu.get_barrier_semaphore()
    for peer in peers:
        pl.semaphore_signal(barrier, inc=1, device_id=peer, device_id_type=MESH)
    pl.semaphore_wait(barrier, len(peers))


def push(src, dst, send, recv, peer):
    copy = pltpu.make_async_remote_copy(
        src_ref=src, dst_ref=dst, send_sem=send, recv_sem=recv, device_id=peer, device_id_type=MESH
    )
    copy.start()
    return copy


def enter_kernel(
    sizes,
    blocks,
    slot_rows,
    meta,
    vander,
    test_fn,
    part,
    metas,
    mine,
    slots,
    onehot,
    pieces,
    block_sems,
    slot_sems,
    relay_sems,
    meta_sems,
    local_sems,
):
    hi, rep, lo = sizes
    h, r, l = (lax.axis_index(name) for name in WORLD)
    me = h * lo + l
    device = (h * rep + r) * lo + l
    everyone = offsets(sizes)
    group = [o for o in everyone if o[1] == 0]
    local = [
        pltpu.make_async_copy(slot_rows, slots.at[me], local_sems.at[0]),
        pltpu.make_async_copy(blocks.at[me], mine.at[me], local_sems.at[1]),
        pltpu.make_async_copy(meta, metas.at[device], local_sems.at[2]),
    ]
    for copy in local:
        copy.start()
    greet([peer_at(sizes, o) for o in everyone])

    along, relays = [], []
    for c in range(1, lo):
        peer = peer_at(sizes, (0, 0, c))
        along.append(
            push(slot_rows, slots.at[me], slot_sems.at[0, c], slot_sems.at[1, c], peer)
        )
    for a in range(1, hi):
        peer = peer_at(sizes, (a, 0, 0))
        k = a * lo
        relays.append(
            push(slot_rows, slots.at[me], relay_sems.at[0, k], relay_sems.at[1, k], peer)
        )
    arrive, labels = [], []
    for k, o in enumerate(group):
        to_h, _, to_l = peer = peer_at(sizes, o)
        arrive.append(
            push(
                blocks.at[to_h * lo + to_l],
                mine.at[me],
                block_sems.at[0, k],
                block_sems.at[1, k],
                peer,
            )
        )
    for k, o in enumerate(everyone):
        labels.append(
            push(
                meta, metas.at[device], meta_sems.at[0, k], meta_sems.at[1, k], peer_at(sizes, o)
            )
        )
    for c in range(1, lo):
        along[c - 1].wait_recv()
        place = h * lo + lax.rem(l + lo - c, lo)
        for a in range(1, hi):
            k = a * lo + c
            relays.append(
                push(
                    slots.at[place],
                    slots.at[place],
                    relay_sems.at[0, k],
                    relay_sems.at[1, k],
                    peer_at(sizes, (a, 0, 0)),
                )
            )
    for copy in local:
        copy.wait()
    for copy in labels:
        copy.wait_recv()

    width = meta.shape[1]
    rows = 128

    @pl.loop(0, part.shape[0] // rows)
    def _(i):
        start = pl.multiple_of(i * rows, rows)
        target = (lax.broadcasted_iota(jnp.int32, (rows, width), 0) + start).astype(jnp.float32)
        for g in range(hi * lo):
            ids = metas[(g // lo * rep + r) * lo + g % lo][0:1, :]
            onehot[pl.ds(start, rows), g * width : (g + 1) * width] = jnp.where(
                target == ids, 1.0, 0.0
            ).astype(onehot.dtype)

    members = slot_rows.shape[0]
    slot_count = width // members
    for a in range(hi):
        for c in range(lo):
            if a or c:
                arrive[a * lo + c - 1].wait_recv()
            if a:
                relays[(a - 1) if c == 0 else (hi - 1) * c + a - 1].wait_recv()
        from_h = lax.rem(h + hi - a, hi)
        first = from_h * lo
        source = mine[pl.ds(first, lo)].reshape(lo * members, -1)
        values = dot(source, vander[...], ((1,), (1,)))
        parts = []
        for c in range(lo):
            where = slots[first + c].astype(jnp.float32)
            value = values[c * members : (c + 1) * members]
            for s in range(slot_count):
                parts.append(jnp.where(where == s, value, 0.0).astype(jnp.bfloat16))
        masked = jnp.concatenate(parts, axis=0)
        pieces[from_h] = dot(masked, test_fn[...], ((1,), (0,))).astype(jnp.bfloat16)

    every = pieces.shape[0] * pieces.shape[1]
    block = 256

    @pl.loop(0, part.shape[0] // block)
    def _(i):
        start = pl.multiple_of(i * block, block)
        summed = dot(
            onehot[pl.ds(start, block), :], pieces[...].reshape(every, -1), ((1,), (0,))
        )
        part[pl.ds(start, block), :] = summed.astype(part.dtype)

    for copy in along + relays + arrive + labels:
        copy.wait_send()


def enter(sizes, blocks, slot_rows, meta, vander, test_fn):
    hi, rep, lo = sizes
    world = hi * rep * lo
    _, members, modes = blocks.shape
    vmem = pl.BlockSpec(memory_space=pltpu.VMEM)
    dma = pltpu.SemaphoreType.DMA
    return pl.pallas_call(
        functools.partial(enter_kernel, sizes),
        out_shape=(
            jax.ShapeDtypeStruct((world * members, modes), jnp.bfloat16),
            jax.ShapeDtypeStruct((world, *meta.shape), meta.dtype),
        ),
        in_specs=[vmem] * 5,
        out_specs=(vmem,) * 2,
        scratch_shapes=[
            pltpu.VMEM(blocks.shape, blocks.dtype),
            pltpu.VMEM((hi * lo, *slot_rows.shape), slot_rows.dtype),
            pltpu.VMEM((world * members, hi * lo * meta.shape[1]), jnp.bfloat16),
            pltpu.VMEM((hi, lo * meta.shape[1], modes), jnp.bfloat16),
            dma((2, hi * lo)),
            dma((2, lo)),
            dma((2, hi * lo)),
            dma((2, world)),
            dma((3,)),
        ],
        compiler_params=pltpu.CompilerParams(
            collective_id=0, has_side_effects=True, vmem_limit_bytes=44 << 20
        ),
        name="enter",
    )(blocks, slot_rows, meta, vander, test_fn)


def leave_kernel(sizes, blocks, mine, sems, local_sem):
    hi, rep, lo = sizes
    me = lax.axis_index("hi") * lo + lax.axis_index("lo")
    group = [o for o in offsets(sizes) if o[1] == 0]
    local = pltpu.make_async_copy(blocks.at[me], mine.at[me], local_sem)
    local.start()
    greet([peer_at(sizes, o) for o in group])
    copies = []
    for k, o in enumerate(group):
        to_h, _, to_l = peer = peer_at(sizes, o)
        copies.append(
            push(blocks.at[to_h * lo + to_l], mine.at[me], sems.at[0, k], sems.at[1, k], peer)
        )
    for copy in copies:
        copy.wait()
    local.wait()


def leave(sizes, blocks):
    vmem = pl.BlockSpec(memory_space=pltpu.VMEM)
    dma = pltpu.SemaphoreType.DMA
    return pl.pallas_call(
        functools.partial(leave_kernel, sizes),
        out_shape=jax.ShapeDtypeStruct(blocks.shape, blocks.dtype),
        in_specs=[vmem],
        out_specs=vmem,
        scratch_shapes=[dma((2, sizes[0] * sizes[2])), dma],
        compiler_params=pltpu.CompilerParams(
            collective_id=1, has_side_effects=True, vmem_limit_bytes=8 << 20
        ),
        name="leave",
    )(blocks)


def per_device(
    gx,
    gy,
    src_coef,
    point_slot,
    tgt_owner,
    tgt_local,
    vander,
    test_fn,
    inv_mass,
    jacobian,
    trace_tab,
    lift_tab,
    wave_speed,
):
    bf16 = jnp.bfloat16
    high = lax.Precision.HIGH
    modes, columns = src_coef.shape
    members = point_slot.shape[1]
    fields = wave_speed.shape[0]
    reps = lax.axis_size("rep")
    my_rep = lax.axis_index("rep")
    my_field = lax.axis_index("hi") * lax.axis_size("lo") + lax.axis_index("lo")

    row = jnp.arange(columns, dtype=jnp.int32)
    wanted = (row % members) * fields + row // members
    perm = (wanted[:, None] == row[None, :]).astype(bf16)
    by_field = dot(perm, src_coef, ((1,), (1,))).astype(bf16)
    sizes = tuple(lax.axis_size(name) for name in WORLD)
    holders = sizes[0] * sizes[2]
    ids = (tgt_owner * members + tgt_local).T.reshape(1, -1).astype(jnp.float32)
    jac = jnp.pad(jacobian[None, :], ((0, 0), (0, ids.shape[1] - members)))
    meta = jnp.pad(jnp.concatenate([ids, jac], axis=0), ((0, 6), (0, 0)))
    part, metas = enter(
        sizes,
        by_field.reshape(holders, members, modes),
        point_slot.T.astype(bf16),
        meta,
        vander,
        test_fn,
    )
    jac = metas[:, 1, :members].reshape(-1, 1)
    if reps == 2:
        other = lax.ppermute(part, "rep", [(0, 1), (1, 0)])
        moments = part.astype(jnp.float32) + other.astype(jnp.float32)
    else:
        moments = lax.psum(part.astype(jnp.float32), "rep")

    coeffs = dot(moments, inv_mass, ((1,), (0,)), high) / jac
    traces = dot(coeffs, trace_tab, ((1,), (0,)), high)
    jumps = neighbour_traces(traces, gx, gy, TX, members // TX)
    own = lambda x: lax.dynamic_index_in_dim(
        x.reshape(-1, reps, gy * members, x.shape[-1]), my_rep, 1, keepdims=False
    ).reshape(-1, x.shape[-1])
    lift = dot(lift_tab, inv_mass, ((1,), (0,)), high)
    speed = lax.dynamic_index_in_dim(wave_speed, my_field, 0, keepdims=False)
    update = dot(own(jumps), lift, ((1,), (0,)), high) * (speed / own(jac))
    result = (own(coeffs) + update).astype(bf16)
    back = leave(sizes, result.reshape(holders, members, modes))
    back = back.transpose(1, 0, 2)
    return back.astype(jnp.float32)


def nt(a, b):
    return dot(a, b, ((1,), (1,)))


def nn(a, b):
    return dot(a, b, ((1,), (0,)))


def split(x):
    high = x.astype(jnp.bfloat16)
    return high, (x - high.astype(jnp.float32)).astype(jnp.bfloat16)


def nn3(a, b):
    (ah, al), (bh, bl) = split(a), split(b)
    return nn(ah, bh) + nn(al, bh) + nn(ah, bl)


def fused_kernel(
    sizes,
    gy,
    src,
    slot_rows,
    owner,
    local_id,
    jac,
    vander_hbm,
    test_hbm,
    inv_hbm,
    trace_hbm,
    lift_hbm,
    speeds,
    out,
    coef,
    slot_in,
    vander,
    test_fn,
    inv,
    trace,
    lift,
    inv_hi,
    inv_lo,
    table,
    lift_inv,
    blocks,
    mine,
    slots,
    meta,
    metas,
    onehot,
    acc,
    part,
    part_in,
    edge,
    edge_in,
    beside,
    result,
    back,
    load_sems,
    slot_send,
    slot_recv,
    block_send,
    block_recv,
    meta_send,
    meta_recv,
    core_send,
    core_recv,
    back_send,
    back_recv,
):
    hi, rep, lo = sizes
    bf16, f32 = jnp.bfloat16, jnp.float32
    h, r, l = (lax.axis_index(name) for name in WORLD)
    me = h * lo + l
    group = hi * lo
    members, points = slot_rows.shape
    modes, columns = src.shape
    slot_count = owner.shape[0]
    fields = columns // members
    ty = members // TX
    width = slot_count * members
    strip = gy * members
    half = hi * strip

    loads = []
    for k, (a, b) in enumerate(
        [
            (src, coef),
            (slot_rows, slot_in),
            (vander_hbm, vander),
            (test_hbm, test_fn),
            (inv_hbm, inv),
            (trace_hbm, trace),
            (lift_hbm, lift),
        ]
    ):
        copy = pltpu.make_async_copy(a, b, load_sems.at[k])
        copy.start()
        loads.append(copy)

    y, x = h // 2, h % 2
    flip_x = y * 2 + (1 - x)
    flip_y = (1 - y) * 2 + x
    flip_xy = (1 - y) * 2 + (1 - x)
    near = [h, flip_x, flip_y, flip_xy]
    core = (h, 1 - r, l)

    barrier = pltpu.get_barrier_semaphore()
    for o in offsets((hi, 1, lo)):
        pl.semaphore_signal(
            barrier, inc=1, device_id=peer_at((hi, 1, lo), o), device_id_type=MESH
        )
    pl.semaphore_signal(barrier, inc=1, device_id=core, device_id_type=MESH)

    meta[...] = jnp.zeros_like(meta)
    meta[0:slot_count, 0:members] = (owner[...] * members + local_id[...]).astype(f32)
    meta[slot_count : slot_count + 1, 0:members] = jac[...]
    packed = meta[...]
    row = lax.broadcasted_iota(jnp.int32, packed.shape, 0)
    lane = lax.broadcasted_iota(jnp.int32, packed.shape, 1)
    ids = jnp.zeros_like(packed)
    for s in range(slot_count):
        turned = pltpu.roll(packed, s * members, 1) if s else packed
        ids = jnp.where((row == s) & (lane // members == s), turned, ids)
    ids = jnp.sum(ids, axis=0, keepdims=True)
    jacs = jnp.zeros_like(packed)
    for c in range(lo):
        turned = pltpu.roll(packed, c * members, 1) if c else packed
        here = (row == slot_count) & (lane // members == c) & (lane // members == l)
        jacs = jnp.where(here, turned, jacs)
    jacs = jnp.sum(jacs, axis=0, keepdims=True)
    packed = jnp.where(row == 0, ids, jnp.where(row == 1, jacs, 0.0))
    meta[...] = packed
    metas[me] = packed

    loads[1].wait()
    slots[me] = slot_in[...].astype(f32).astype(bf16)
    loads[0].wait()
    rows = lo * members
    r_iota = lax.broadcasted_iota(jnp.int32, (rows, columns), 0)
    c_iota = lax.broadcasted_iota(jnp.int32, (rows, columns), 1)
    for k in range(hi):
        wanted = (r_iota % members) * fields + r_iota // members + k * lo
        perm = (wanted == c_iota).astype(f32).astype(bf16)
        moved = nt(perm, coef[...]).astype(bf16)
        blocks[k * lo : (k + 1) * lo] = moved.reshape(lo, members, modes)
    mine[me] = blocks[me]

    pl.semaphore_wait(barrier, group)

    sent = []

    def slot_copy(at, k, to):
        return pltpu.make_async_remote_copy(
            src_ref=slots.at[at],
            dst_ref=slots.at[at],
            send_sem=slot_send.at[k],
            recv_sem=slot_recv.at[at],
            device_id=to,
            device_id_type=MESH,
        )

    def send_slot(at, to):
        copy = slot_copy(at, len(sent), to)
        sent.append(copy)
        copy.start()

    def wait_slot(at):
        slot_copy(at, 0, core).wait_recv()

    turns = (1, 3, 2)
    for c in turns:
        send_slot(me, (h, r, (l - c + lo) % lo))
    for to_h in near[1:]:
        send_slot(me, (to_h, r, l))

    others = []

    def send_block(k, c):
        to_h, to_l = near[k], (l + c) % lo
        copy = pltpu.make_async_remote_copy(
            src_ref=blocks.at[to_h * lo + to_l],
            dst_ref=mine.at[me],
            send_sem=block_send.at[k * lo + c],
            recv_sem=block_recv.at[me],
            device_id=(to_h, r, to_l),
            device_id_type=MESH,
        )
        copy.start()
        others.append(copy)

    for k, to_h in enumerate(near):
        for c in range(1 if k == 0 else 0, lo):
            to_l = (l + c) % lo
            copy = pltpu.make_async_remote_copy(
                src_ref=meta,
                dst_ref=metas.at[me],
                send_sem=meta_send.at[k * lo + c],
                recv_sem=meta_recv.at[me],
                device_id=(to_h, r, to_l),
                device_id_type=MESH,
            )
            copy.start()
            others.append(copy)

    for k in range(1, hi):
        send_block(k, 0)
    for c in turns:
        at = h * lo + (l + c) % lo
        wait_slot(at)
        for k in (3, 1, 2, 0):
            if k:
                send_slot(at, (near[k], r, l))
            send_block(k, (lo - c) % lo)

    def wait_block(at):
        pltpu.make_async_remote_copy(
            src_ref=mine.at[at],
            dst_ref=mine.at[at],
            send_sem=block_send.at[0],
            recv_sem=block_recv.at[at],
            device_id=core,
            device_id_type=MESH,
        ).wait_recv()
        pltpu.make_async_remote_copy(
            src_ref=metas.at[at],
            dst_ref=metas.at[at],
            send_sem=meta_send.at[0],
            recv_sem=meta_recv.at[at],
            device_id=core,
            device_id_type=MESH,
        ).wait_recv()

    for copy in loads[2:]:
        copy.wait()
    high, low = split(inv[...])
    inv_hi[...] = high
    inv_lo[...] = low
    traced = nn3(inv[...], trace[...])
    pts = trace.shape[1] // 4
    table[:, : 4 * pts] = traced.astype(bf16)
    face = lax.broadcasted_iota(jnp.int32, traced.shape, 1) // pts
    swapped = jnp.where(
        face % 2 == 0, pltpu.roll(traced, 3 * pts, 1), pltpu.roll(traced, pts, 1)
    )
    table[:, 4 * pts :] = swapped.astype(bf16)
    lift_inv[...] = nn3(lift[...], inv[...]).astype(bf16)

    place = lax.broadcasted_iota(jnp.int32, (half, width), 0)
    place = (place // strip) * (2 * strip) + place % strip

    def gather(places):
        source = jnp.concatenate([mine[at] for at in places], axis=0)
        values = nt(source, vander[...]).astype(bf16).astype(f32)
        parts = []
        for c, at in enumerate(places):
            where = slots[at].astype(f32)
            value = values[c * members : (c + 1) * members]
            for s in range(slot_count):
                parts.append(jnp.where(where == s, value, 0.0).astype(bf16))
        pieces = nn(jnp.concatenate(parts, axis=0), test_fn[...]).astype(bf16)
        for side in range(2):
            shift = (1 - r if side == 0 else r) * strip
            for c, at in enumerate(places):
                targets = (metas[at][0:1, :]).astype(jnp.int32) - shift
                onehot[side, :, c * width : (c + 1) * width] = (
                    jnp.where(place == targets, 1.0, 0.0).astype(bf16)
                )
        return pieces

    def scatter(pieces, side, first):
        summed = nn(onehot[side], pieces)
        return summed if first else acc[side] + summed

    for k, c in enumerate((0,) + turns):
        places = [at * lo + (l + c) % lo for at in near]
        for at in places[1:]:
            wait_slot(at)
        for at in places[0 if c else 1 :]:
            wait_block(at)
        pieces = gather(places)
        if k < lo - 1:
            for side in range(2):
                acc[side] = scatter(pieces, side, k == 0)

    def core_copy(a, b, k):
        return pltpu.make_async_remote_copy(
            src_ref=a,
            dst_ref=b,
            send_sem=core_send.at[k],
            recv_sem=core_recv.at[k],
            device_id=core,
            device_id_type=MESH,
        )

    theirs = scatter(pieces, 0, False).astype(bf16)
    part[...] = theirs
    part_copy = core_copy(part, part_in, 0)
    part_copy.start()
    ours = scatter(pieces, 1, False)
    acc[1] = ours
    swap = table[:, 4 * pts :]
    seen = nn(ours.astype(bf16), swap)
    eye_r = lax.broadcasted_iota(jnp.int32, (strip, strip), 0)
    eye_c = lax.broadcasted_iota(jnp.int32, (strip, strip), 1)
    lanes = lax.broadcasted_iota(jnp.int32, (strip, 4 * pts), 1)
    inverse = []
    for k in range(hi):
        jac_row = metas[k * lo][1:2, :]
        for c in range(1, lo):
            jac_row = jac_row + metas[k * lo + c][1:2, :]
        column = jnp.sum(jnp.where(eye_r == eye_c, jac_row, 0.0), axis=1, keepdims=True)
        column = 1.0 / column
        inverse.append(column)
        edge[k * strip : (k + 1) * strip, :] = jnp.where(
            lanes == 4 * pts - 1, column, seen[k * strip : (k + 1) * strip]
        )
    edge_copy = core_copy(edge, edge_in, 1)
    edge_copy.start()
    seen = nn(theirs, swap)
    beside[0:strip, :] = jnp.zeros((strip, 4 * pts), f32)
    beside[(hi + 1) * strip :, :] = jnp.zeros((strip, 4 * pts), f32)
    part_copy.wait_recv()
    edge_copy.wait_recv()
    for k in range(hi):
        got = edge_in[k * strip : (k + 1) * strip, :]
        column = got[:, 4 * pts - 1 : 4 * pts]
        beside[(k + 1) * strip : (k + 2) * strip, :] = (
            seen[k * strip : (k + 1) * strip] + got
        ) * column

    speed = speeds[me]
    t_row = lax.broadcasted_iota(jnp.int32, (strip, 4 * pts), 0)
    d_row, a_row, b_row = t_row // members, (t_row % members) // ty, t_row % ty
    face = lanes // pts
    moved = lambda v, n: pltpu.roll(v, n % strip, 0)
    for k in range(hi):
        own = slice(k * strip, (k + 1) * strip)
        moments = acc[1, own, :] + part_in[own, :].astype(f32)
        m_hi, m_lo = split(moments)
        both = nn(m_hi, table[...]) * inverse[k]
        mine_t, cur = both[:, : 4 * pts], both[:, 4 * pts :]
        prev = beside[pl.ds(pl.multiple_of((k + r) * strip, strip), strip), :]
        after = beside[pl.ds(pl.multiple_of((k + r + 1) * strip, strip), strip), :]
        last = (TX - 1) * ty
        west = jnp.where(a_row > 0, moved(cur, ty), moved(prev, -last))
        east = jnp.where(a_row < TX - 1, moved(cur, -ty), moved(after, last))
        jump = members - (ty - 1)
        south = jnp.where(b_row > 0, moved(cur, 1), moved(cur, jump))
        south = jnp.where((b_row == 0) & (d_row == 0), 0.0, south)
        north = jnp.where(b_row < ty - 1, moved(cur, -1), moved(cur, -jump))
        north = jnp.where((b_row == ty - 1) & (d_row == gy - 1), 0.0, north)
        other = jnp.where(
            face < 2, jnp.where(face == 0, west, east), jnp.where(face == 2, south, north)
        )
        jumps = ((other - mine_t) * speed).astype(bf16)
        solved = nn(m_hi, inv_hi[...]) + nn(m_lo, inv_hi[...]) + nn(m_hi, inv_lo[...])
        solved = (solved + nn(jumps, lift_inv[...])) * inverse[k]
        result[k * lo : (k + 1) * lo] = solved.astype(bf16).reshape(lo, members, modes)
        for c in range(lo):
            to_l = (l + c) % lo

            def back_copy():
                return pltpu.make_async_remote_copy(
                    src_ref=result.at[k * lo + to_l],
                    dst_ref=back.at[me],
                    send_sem=back_send.at[k * lo + c],
                    recv_sem=back_recv.at[me],
                    device_id=(k, r, to_l),
                    device_id_type=MESH,
                )

            if c == 0:
                pl.when(h != k)(lambda: back_copy().start())
            else:
                back_copy().start()
    back[me] = result[me]

    for at in range(group):

        @pl.when(me != at)
        def _():
            pltpu.make_async_remote_copy(
                src_ref=back.at[at],
                dst_ref=back.at[at],
                send_sem=back_send.at[0],
                recv_sem=back_recv.at[at],
                device_id=core,
                device_id_type=MESH,
            ).wait_recv()

    for at in range(group):
        out[:, at, :] = back[at].astype(f32)

    for copy in sent + others + [part_copy, edge_copy]:
        copy.wait_send()
    for k in range(hi):
        for c in range(lo):

            def leave_wait():
                pltpu.make_async_remote_copy(
                    src_ref=result.at[k * lo],
                    dst_ref=back.at[me],
                    send_sem=back_send.at[k * lo + c],
                    recv_sem=back_recv.at[me],
                    device_id=core,
                    device_id_type=MESH,
                ).wait_send()

            if c == 0:
                pl.when(h != k)(leave_wait)
            else:
                leave_wait()


def fused(sizes, gy, *args):
    src, slot_rows, owner, _, _, vander, test_fn, inv, trace, lift, speeds = args
    hi, rep, lo = sizes
    members, points = slot_rows.shape
    modes, columns = src.shape
    slot_count = owner.shape[0]
    group = hi * lo
    strip = gy * members
    half = hi * strip
    faces = trace.shape[1]
    width = slot_count * members
    bf16, f32 = jnp.bfloat16, jnp.float32
    any_, vmem = pl.BlockSpec(memory_space=pl.ANY), pl.BlockSpec(memory_space=pltpu.VMEM)
    smem = pl.BlockSpec(memory_space=pltpu.SMEM)
    dma = pltpu.SemaphoreType.DMA
    like = lambda a: pltpu.VMEM(a.shape, a.dtype)
    slot_sends = 6 + (lo - 1) * 3
    return pl.pallas_call(
        functools.partial(fused_kernel, sizes, gy),
        out_shape=pltpu.VMEM((members, columns // members, modes), f32),
        in_specs=[any_, any_, vmem, vmem, vmem, any_, any_, any_, any_, any_, smem],
        out_specs=vmem,
        scratch_shapes=[
            like(src),
            like(slot_rows),
            like(vander),
            like(test_fn),
            like(inv),
            like(trace),
            like(lift),
            pltpu.VMEM(inv.shape, bf16),
            pltpu.VMEM(inv.shape, bf16),
            pltpu.VMEM((modes, 2 * faces), bf16),
            pltpu.VMEM(lift.shape, bf16),
            pltpu.VMEM((group, members, modes), bf16),
            pltpu.VMEM((group, members, modes), bf16),
            pltpu.VMEM((group, members, points), bf16),
            pltpu.VMEM((8, width), f32),
            pltpu.VMEM((group, 8, width), f32),
            pltpu.VMEM((2, half, hi * width), bf16),
            pltpu.VMEM((2, half, modes), f32),
            pltpu.VMEM((half, modes), bf16),
            pltpu.VMEM((half, modes), bf16),
            pltpu.VMEM((half, faces), f32),
            pltpu.VMEM((half, faces), f32),
            pltpu.VMEM((half + 2 * strip, faces), f32),
            pltpu.VMEM((group, members, modes), bf16),
            pltpu.VMEM((group, members, modes), bf16),
            dma((7,)),
            dma((slot_sends,)),
            dma((group,)),
            dma((group,)),
            dma((group,)),
            dma((group,)),
            dma((group,)),
            dma((2,)),
            dma((2,)),
            dma((group,)),
            dma((group,)),
        ],
        compiler_params=pltpu.CompilerParams(
            collective_id=2, has_side_effects=True, vmem_limit_bytes=56 << 20
        ),
        name="remap",
    )(*args)


def fused_device(sizes, gy, src_coef, point_slot, tgt_owner, tgt_local, vander, test_fn, inv_mass, jacobian, trace_tab, lift_tab, wave_speed):
    return fused(
        sizes,
        gy,
        src_coef,
        point_slot.T,
        tgt_owner.T,
        tgt_local.T,
        jacobian[None, :],
        vander,
        test_fn,
        inv_mass,
        trace_tab,
        lift_tab,
        wave_speed,
    )


def solution(mesh):
    gx, gy = mesh.shape["gx"], mesh.shape["gy"]
    devices = gx * gy

    def call(*args):
        fields = args[-1].shape[0]
        sizes = (fields // gy, devices // fields, gy)
        body = functools.partial(per_device, gx, gy)
        if sizes == (4, 2, 4):
            body = functools.partial(fused_device, sizes, gy)
        return jax.shard_map(
            body,
            mesh=Mesh(mesh.devices.reshape(sizes), WORLD),
            in_specs=(
                P(None, WORLD),
                P(None, WORLD),
                P(WORLD, None),
                P(WORLD, None),
                P(),
                P(),
                P(),
                P(WORLD),
                P(),
                P(),
                P(),
            ),
            out_specs=P(WORLD, None, None),
            check_vma=False,
        )(*args)

    return call
```

```python
import functools

import jax
import jax.numpy as jnp
from jax import lax
from jax.experimental import pallas as pl
from jax.experimental.pallas import tpu as pltpu
from jax.sharding import Mesh, PartitionSpec as P

TX = 8
MESH = pl.DeviceIdType.MESH
GROUP = ("hi", "lo")
WORLD = ("hi", "rep", "lo")


def dot(a, b, dims, precision=None):
    return lax.dot_general(
        a, b, (dims, ((), ())), precision=precision, preferred_element_type=jnp.float32
    )


def neighbour_traces(traces, gx, gy, tx, ty):
    face_cols = traces.shape[1]
    pts = face_cols // 4
    grid = traces.reshape(gx, gy, tx, ty, face_cols).transpose(0, 2, 1, 3, 4)
    grid = grid.reshape(gx * tx, gy * ty, face_cols)
    face = lambda k: grid[:, :, k * pts : (k + 1) * pts]
    west = jnp.pad(face(1)[:-1], ((1, 0), (0, 0), (0, 0)))
    east = jnp.pad(face(0)[1:], ((0, 1), (0, 0), (0, 0)))
    south = jnp.pad(face(3)[:, :-1], ((0, 0), (1, 0), (0, 0)))
    north = jnp.pad(face(2)[:, 1:], ((0, 0), (0, 1), (0, 0)))
    joined = jnp.concatenate([west, east, south, north], axis=2) - grid
    joined = joined.reshape(gx, tx, gy, ty, face_cols).transpose(0, 2, 1, 3, 4)
    return joined.reshape(gx * gy * tx * ty, face_cols)


def peer_at(sizes, offset):
    return tuple(
        lax.rem(lax.axis_index(name) + step, size) if step else lax.axis_index(name)
        for name, size, step in zip(WORLD, sizes, offset)
    )


def offsets(sizes):
    hi, rep, lo = sizes
    every = [(a, b, c) for a in range(hi) for b in range(rep) for c in range(lo)]
    return every[1:]


def greet(peers):
    barrier = pltpu.get_barrier_semaphore()
    for peer in peers:
        pl.semaphore_signal(barrier, inc=1, device_id=peer, device_id_type=MESH)
    pl.semaphore_wait(barrier, len(peers))


def push(src, dst, send, recv, peer):
    copy = pltpu.make_async_remote_copy(
        src_ref=src, dst_ref=dst, send_sem=send, recv_sem=recv, device_id=peer, device_id_type=MESH
    )
    copy.start()
    return copy


def enter_kernel(
    sizes,
    blocks,
    slot_rows,
    meta,
    vander,
    test_fn,
    part,
    metas,
    mine,
    slots,
    onehot,
    pieces,
    block_sems,
    slot_sems,
    relay_sems,
    meta_sems,
    local_sems,
):
    hi, rep, lo = sizes
    h, r, l = (lax.axis_index(name) for name in WORLD)
    me = h * lo + l
    device = (h * rep + r) * lo + l
    everyone = offsets(sizes)
    group = [o for o in everyone if o[1] == 0]
    local = [
        pltpu.make_async_copy(slot_rows, slots.at[me], local_sems.at[0]),
        pltpu.make_async_copy(blocks.at[me], mine.at[me], local_sems.at[1]),
        pltpu.make_async_copy(meta, metas.at[device], local_sems.at[2]),
    ]
    for copy in local:
        copy.start()
    greet([peer_at(sizes, o) for o in everyone])

    along, relays = [], []
    for c in range(1, lo):
        peer = peer_at(sizes, (0, 0, c))
        along.append(
            push(slot_rows, slots.at[me], slot_sems.at[0, c], slot_sems.at[1, c], peer)
        )
    for a in range(1, hi):
        peer = peer_at(sizes, (a, 0, 0))
        k = a * lo
        relays.append(
            push(slot_rows, slots.at[me], relay_sems.at[0, k], relay_sems.at[1, k], peer)
        )
    arrive, labels = [], []
    for k, o in enumerate(group):
        to_h, _, to_l = peer = peer_at(sizes, o)
        arrive.append(
            push(
                blocks.at[to_h * lo + to_l],
                mine.at[me],
                block_sems.at[0, k],
                block_sems.at[1, k],
                peer,
            )
        )
    for k, o in enumerate(everyone):
        labels.append(
            push(
                meta, metas.at[device], meta_sems.at[0, k], meta_sems.at[1, k], peer_at(sizes, o)
            )
        )
    for c in range(1, lo):
        along[c - 1].wait_recv()
        place = h * lo + lax.rem(l + lo - c, lo)
        for a in range(1, hi):
            k = a * lo + c
            relays.append(
                push(
                    slots.at[place],
                    slots.at[place],
                    relay_sems.at[0, k],
                    relay_sems.at[1, k],
                    peer_at(sizes, (a, 0, 0)),
                )
            )
    for copy in local:
        copy.wait()
    for copy in labels:
        copy.wait_recv()

    width = meta.shape[1]
    rows = 128

    @pl.loop(0, part.shape[0] // rows)
    def _(i):
        start = pl.multiple_of(i * rows, rows)
        target = (lax.broadcasted_iota(jnp.int32, (rows, width), 0) + start).astype(jnp.float32)
        for g in range(hi * lo):
            ids = metas[(g // lo * rep + r) * lo + g % lo][0:1, :]
            onehot[pl.ds(start, rows), g * width : (g + 1) * width] = jnp.where(
                target == ids, 1.0, 0.0
            ).astype(onehot.dtype)

    members = slot_rows.shape[0]
    slot_count = width // members
    for a in range(hi):
        for c in range(lo):
            if a or c:
                arrive[a * lo + c - 1].wait_recv()
            if a:
                relays[(a - 1) if c == 0 else (hi - 1) * c + a - 1].wait_recv()
        from_h = lax.rem(h + hi - a, hi)
        first = from_h * lo
        source = mine[pl.ds(first, lo)].reshape(lo * members, -1)
        values = dot(source, vander[...], ((1,), (1,)))
        parts = []
        for c in range(lo):
            where = slots[first + c].astype(jnp.float32)
            value = values[c * members : (c + 1) * members]
            for s in range(slot_count):
                parts.append(jnp.where(where == s, value, 0.0).astype(jnp.bfloat16))
        masked = jnp.concatenate(parts, axis=0)
        pieces[from_h] = dot(masked, test_fn[...], ((1,), (0,))).astype(jnp.bfloat16)

    every = pieces.shape[0] * pieces.shape[1]
    block = 256

    @pl.loop(0, part.shape[0] // block)
    def _(i):
        start = pl.multiple_of(i * block, block)
        summed = dot(
            onehot[pl.ds(start, block), :], pieces[...].reshape(every, -1), ((1,), (0,))
        )
        part[pl.ds(start, block), :] = summed.astype(part.dtype)

    for copy in along + relays + arrive + labels:
        copy.wait_send()


def enter(sizes, blocks, slot_rows, meta, vander, test_fn):
    hi, rep, lo = sizes
    world = hi * rep * lo
    _, members, modes = blocks.shape
    vmem = pl.BlockSpec(memory_space=pltpu.VMEM)
    dma = pltpu.SemaphoreType.DMA
    return pl.pallas_call(
        functools.partial(enter_kernel, sizes),
        out_shape=(
            jax.ShapeDtypeStruct((world * members, modes), jnp.bfloat16),
            jax.ShapeDtypeStruct((world, *meta.shape), meta.dtype),
        ),
        in_specs=[vmem] * 5,
        out_specs=(vmem,) * 2,
        scratch_shapes=[
            pltpu.VMEM(blocks.shape, blocks.dtype),
            pltpu.VMEM((hi * lo, *slot_rows.shape), slot_rows.dtype),
            pltpu.VMEM((world * members, hi * lo * meta.shape[1]), jnp.bfloat16),
            pltpu.VMEM((hi, lo * meta.shape[1], modes), jnp.bfloat16),
            dma((2, hi * lo)),
            dma((2, lo)),
            dma((2, hi * lo)),
            dma((2, world)),
            dma((3,)),
        ],
        compiler_params=pltpu.CompilerParams(
            collective_id=0, has_side_effects=True, vmem_limit_bytes=44 << 20
        ),
        name="enter",
    )(blocks, slot_rows, meta, vander, test_fn)


def leave_kernel(sizes, blocks, mine, sems, local_sem):
    hi, rep, lo = sizes
    me = lax.axis_index("hi") * lo + lax.axis_index("lo")
    group = [o for o in offsets(sizes) if o[1] == 0]
    local = pltpu.make_async_copy(blocks.at[me], mine.at[me], local_sem)
    local.start()
    greet([peer_at(sizes, o) for o in group])
    copies = []
    for k, o in enumerate(group):
        to_h, _, to_l = peer = peer_at(sizes, o)
        copies.append(
            push(blocks.at[to_h * lo + to_l], mine.at[me], sems.at[0, k], sems.at[1, k], peer)
        )
    for copy in copies:
        copy.wait()
    local.wait()


def leave(sizes, blocks):
    vmem = pl.BlockSpec(memory_space=pltpu.VMEM)
    dma = pltpu.SemaphoreType.DMA
    return pl.pallas_call(
        functools.partial(leave_kernel, sizes),
        out_shape=jax.ShapeDtypeStruct(blocks.shape, blocks.dtype),
        in_specs=[vmem],
        out_specs=vmem,
        scratch_shapes=[dma((2, sizes[0] * sizes[2])), dma],
        compiler_params=pltpu.CompilerParams(
            collective_id=1, has_side_effects=True, vmem_limit_bytes=8 << 20
        ),
        name="leave",
    )(blocks)


def per_device(
    gx,
    gy,
    src_coef,
    point_slot,
    tgt_owner,
    tgt_local,
    vander,
    test_fn,
    inv_mass,
    jacobian,
    trace_tab,
    lift_tab,
    wave_speed,
):
    bf16 = jnp.bfloat16
    high = lax.Precision.HIGH
    modes, columns = src_coef.shape
    members = point_slot.shape[1]
    fields = wave_speed.shape[0]
    reps = lax.axis_size("rep")
    my_rep = lax.axis_index("rep")
    my_field = lax.axis_index("hi") * lax.axis_size("lo") + lax.axis_index("lo")

    row = jnp.arange(columns, dtype=jnp.int32)
    wanted = (row % members) * fields + row // members
    perm = (wanted[:, None] == row[None, :]).astype(bf16)
    by_field = dot(perm, src_coef, ((1,), (1,))).astype(bf16)
    sizes = tuple(lax.axis_size(name) for name in WORLD)
    holders = sizes[0] * sizes[2]
    ids = (tgt_owner * members + tgt_local).T.reshape(1, -1).astype(jnp.float32)
    jac = jnp.pad(jacobian[None, :], ((0, 0), (0, ids.shape[1] - members)))
    meta = jnp.pad(jnp.concatenate([ids, jac], axis=0), ((0, 6), (0, 0)))
    part, metas = enter(
        sizes,
        by_field.reshape(holders, members, modes),
        point_slot.T.astype(bf16),
        meta,
        vander,
        test_fn,
    )
    jac = metas[:, 1, :members].reshape(-1, 1)
    if reps == 2:
        other = lax.ppermute(part, "rep", [(0, 1), (1, 0)])
        moments = part.astype(jnp.float32) + other.astype(jnp.float32)
    else:
        moments = lax.psum(part.astype(jnp.float32), "rep")

    coeffs = dot(moments, inv_mass, ((1,), (0,)), high) / jac
    traces = dot(coeffs, trace_tab, ((1,), (0,)), high)
    jumps = neighbour_traces(traces, gx, gy, TX, members // TX)
    own = lambda x: lax.dynamic_index_in_dim(
        x.reshape(-1, reps, gy * members, x.shape[-1]), my_rep, 1, keepdims=False
    ).reshape(-1, x.shape[-1])
    lift = dot(lift_tab, inv_mass, ((1,), (0,)), high)
    speed = lax.dynamic_index_in_dim(wave_speed, my_field, 0, keepdims=False)
    update = dot(own(jumps), lift, ((1,), (0,)), high) * (speed / own(jac))
    result = (own(coeffs) + update).astype(bf16)
    back = leave(sizes, result.reshape(holders, members, modes))
    back = back.transpose(1, 0, 2)
    return back.astype(jnp.float32)


def nt(a, b):
    return dot(a, b, ((1,), (1,)))


def nn(a, b):
    return dot(a, b, ((1,), (0,)))


def split(x):
    high = x.astype(jnp.bfloat16)
    return high, (x - high.astype(jnp.float32)).astype(jnp.bfloat16)


def nn3(a, b):
    (ah, al), (bh, bl) = split(a), split(b)
    return nn(ah, bh) + nn(al, bh) + nn(ah, bl)


def fused_kernel(
    sizes,
    gy,
    src,
    slot_rows,
    owner,
    local_id,
    jac,
    vander_hbm,
    test_hbm,
    inv_hbm,
    trace_hbm,
    lift_hbm,
    speeds,
    out,
    coef,
    slot_in,
    vander,
    test_fn,
    inv,
    trace,
    lift,
    inv_hi,
    inv_lo,
    table,
    lift_inv,
    blocks,
    mine,
    slots,
    meta,
    metas,
    onehot,
    acc,
    part,
    part_in,
    edge,
    edge_in,
    beside,
    result,
    back,
    load_sems,
    slot_send,
    slot_recv,
    block_send,
    block_recv,
    meta_send,
    meta_recv,
    core_send,
    core_recv,
    back_send,
    back_recv,
):
    hi, rep, lo = sizes
    bf16, f32 = jnp.bfloat16, jnp.float32
    h, r, l = (lax.axis_index(name) for name in WORLD)
    me = h * lo + l
    group = hi * lo
    members, points = slot_rows.shape
    modes, columns = src.shape
    slot_count = owner.shape[0]
    fields = columns // members
    ty = members // TX
    width = slot_count * members
    strip = gy * members
    half = hi * strip

    y, x = h // 2, h % 2
    flip_x = y * 2 + (1 - x)
    flip_y = (1 - y) * 2 + x
    flip_xy = (1 - y) * 2 + (1 - x)
    near = [h, flip_x, flip_y, flip_xy]
    core = (h, 1 - r, l)

    barrier = pltpu.get_barrier_semaphore()
    for o in offsets((hi, 1, lo)):
        pl.semaphore_signal(
            barrier, inc=1, device_id=peer_at((hi, 1, lo), o), device_id_type=MESH
        )
    pl.semaphore_signal(barrier, inc=1, device_id=core, device_id_type=MESH)

    loads = []
    for k, (a, b) in enumerate(
        [
            (src, coef),
            (slot_rows, slot_in),
            (vander_hbm, vander),
            (test_hbm, test_fn),
            (inv_hbm, inv),
            (trace_hbm, trace),
            (lift_hbm, lift),
        ]
    ):
        copy = pltpu.make_async_copy(a, b, load_sems.at[k])
        copy.start()
        loads.append(copy)

    loads[1].wait()
    slots[me] = slot_in[...].astype(f32).astype(bf16)
    pl.semaphore_wait(barrier, group)

    sent = []

    def slot_copy(at, k, to):
        return pltpu.make_async_remote_copy(
            src_ref=slots.at[at],
            dst_ref=slots.at[at],
            send_sem=slot_send.at[k],
            recv_sem=slot_recv.at[at],
            device_id=to,
            device_id_type=MESH,
        )

    def send_slot(at, to):
        copy = slot_copy(at, len(sent), to)
        sent.append((copy, None))
        copy.start()

    def wait_slot(at):
        slot_copy(at, 0, core).wait_recv()

    partner = l + 1 - 2 * (l % 2)
    lower = l < 2
    near_z = jnp.where(lower, 2, 1)
    far_z = jnp.where(lower, 3, 0)
    inner = (l == 1) | (l == 2)
    outer = jnp.where(lower, 0, 3)
    line = [l, partner, near_z, far_z]

    send_slot(me, (h, r, near_z))
    send_slot(me, (h, r, partner))
    for to_h in near[1:]:
        send_slot(me, (to_h, r, l))

    others = []

    def send_block(k, c):
        to_h, to_l = near[k], line[c]
        copy = pltpu.make_async_remote_copy(
            src_ref=blocks.at[to_h * lo + to_l],
            dst_ref=mine.at[me],
            send_sem=block_send.at[k * lo + c],
            recv_sem=block_recv.at[me],
            device_id=(to_h, r, to_l),
            device_id_type=MESH,
        )
        copy.start()
        others.append(copy)

    meta[...] = jnp.zeros_like(meta)
    meta[0:slot_count, 0:members] = (owner[...] * members + local_id[...]).astype(f32)
    meta[slot_count : slot_count + 1, 0:members] = jac[...]
    packed = meta[...]
    row = lax.broadcasted_iota(jnp.int32, packed.shape, 0)
    lane = lax.broadcasted_iota(jnp.int32, packed.shape, 1)
    ids = jnp.zeros_like(packed)
    for s in range(slot_count):
        turned = pltpu.roll(packed, s * members, 1) if s else packed
        ids = jnp.where((row == s) & (lane // members == s), turned, ids)
    ids = jnp.sum(ids, axis=0, keepdims=True)
    jacs = jnp.zeros_like(packed)
    for c in range(lo):
        turned = pltpu.roll(packed, c * members, 1) if c else packed
        here = (row == slot_count) & (lane // members == c) & (lane // members == l)
        jacs = jnp.where(here, turned, jacs)
    jacs = jnp.sum(jacs, axis=0, keepdims=True)
    packed = jnp.where(row == 0, ids, jnp.where(row == 1, jacs, 0.0))
    meta[...] = packed
    metas[me] = packed

    for k, to_h in enumerate(near):
        for c in range(1 if k == 0 else 0, lo):
            to_l = (l + c) % lo
            copy = pltpu.make_async_remote_copy(
                src_ref=meta,
                dst_ref=metas.at[me],
                send_sem=meta_send.at[k * lo + c],
                recv_sem=meta_recv.at[me],
                device_id=(to_h, r, to_l),
                device_id_type=MESH,
            )
            copy.start()
            others.append(copy)

    loads[0].wait()
    rows = lo * members
    r_iota = lax.broadcasted_iota(jnp.int32, (rows, columns), 0)
    c_iota = lax.broadcasted_iota(jnp.int32, (rows, columns), 1)
    r_iota = (r_iota % members) * fields + r_iota // members
    for k in (1, 2, 3, 0):
        first = near[k] * lo
        perm = (r_iota + first == c_iota).astype(f32).astype(bf16)
        moved = nt(perm, coef[...]).astype(bf16)
        blocks[pl.ds(first, lo)] = moved.reshape(lo, members, modes)
        if k:
            send_block(k, 0)
    mine[me] = blocks[me]


    for i in range(1, lo):
        z = line[i]
        at = h * lo + z
        wait_slot(at)
        if i > 1:
            copy = slot_copy(at, len(sent), (h, r, outer))
            sent.append((copy, inner))
            pl.when(inner)(copy.start)
        for k in (3, 1, 2, 0):
            if k in (1, 2, 3):
                send_slot(at, (near[k], r, l))
            send_block(k, i)

    def wait_block(at):
        pltpu.make_async_remote_copy(
            src_ref=mine.at[at],
            dst_ref=mine.at[at],
            send_sem=block_send.at[0],
            recv_sem=block_recv.at[at],
            device_id=core,
            device_id_type=MESH,
        ).wait_recv()
        pltpu.make_async_remote_copy(
            src_ref=metas.at[at],
            dst_ref=metas.at[at],
            send_sem=meta_send.at[0],
            recv_sem=meta_recv.at[at],
            device_id=core,
            device_id_type=MESH,
        ).wait_recv()

    for copy in loads[2:]:
        copy.wait()
    high, low = split(inv[...])
    inv_hi[...] = high
    inv_lo[...] = low
    traced = nn3(inv[...], trace[...])
    pts = trace.shape[1] // 4
    table[:, : 4 * pts] = traced.astype(bf16)
    face = lax.broadcasted_iota(jnp.int32, traced.shape, 1) // pts
    swapped = jnp.where(
        face % 2 == 0, pltpu.roll(traced, 3 * pts, 1), pltpu.roll(traced, pts, 1)
    )
    table[:, 4 * pts :] = swapped.astype(bf16)
    lift_inv[...] = nn3(lift[...], inv[...]).astype(bf16)

    place = lax.broadcasted_iota(jnp.int32, (half, width), 0)
    place = (place // strip) * (2 * strip) + place % strip

    def gather(places):
        source = jnp.concatenate([mine[at] for at in places], axis=0)
        values = nt(source, vander[...]).astype(bf16).astype(f32)
        parts = []
        for c, at in enumerate(places):
            where = slots[at].astype(f32)
            value = values[c * members : (c + 1) * members]
            for s in range(slot_count):
                parts.append(jnp.where(where == s, value, 0.0).astype(bf16))
        pieces = nn(jnp.concatenate(parts, axis=0), test_fn[...]).astype(bf16)
        for side in range(2):
            shift = (1 - r if side == 0 else r) * strip
            for c, at in enumerate(places):
                targets = (metas[at][0:1, :]).astype(jnp.int32) - shift
                onehot[side, :, c * width : (c + 1) * width] = (
                    jnp.where(place == targets, 1.0, 0.0).astype(bf16)
                )
        return pieces

    def scatter(pieces, side, first):
        summed = nn(onehot[side], pieces)
        return summed if first else acc[side] + summed

    for k, z in enumerate(line):
        places = [at * lo + z for at in near]
        for at in places[1:]:
            wait_slot(at)
        for at in places[0 if k else 1 :]:
            wait_block(at)
        pieces = gather(places)
        if k < lo - 1:
            for side in range(2):
                acc[side] = scatter(pieces, side, k == 0)

    def core_copy(a, b, k):
        return pltpu.make_async_remote_copy(
            src_ref=a,
            dst_ref=b,
            send_sem=core_send.at[k],
            recv_sem=core_recv.at[k],
            device_id=core,
            device_id_type=MESH,
        )

    theirs = scatter(pieces, 0, False).astype(bf16)
    part[...] = theirs
    part_copy = core_copy(part, part_in, 0)
    part_copy.start()
    ours = scatter(pieces, 1, False)
    acc[1] = ours
    swap = table[:, 4 * pts :]
    seen = nn(ours.astype(bf16), swap)
    eye_r = lax.broadcasted_iota(jnp.int32, (strip, strip), 0)
    eye_c = lax.broadcasted_iota(jnp.int32, (strip, strip), 1)
    lanes = lax.broadcasted_iota(jnp.int32, (strip, 4 * pts), 1)
    inverse = []
    for k in range(hi):
        jac_row = metas[k * lo][1:2, :]
        for c in range(1, lo):
            jac_row = jac_row + metas[k * lo + c][1:2, :]
        column = jnp.sum(jnp.where(eye_r == eye_c, jac_row, 0.0), axis=1, keepdims=True)
        column = 1.0 / column
        inverse.append(column)
        edge[k * strip : (k + 1) * strip, :] = jnp.where(
            lanes == 4 * pts - 1, column, seen[k * strip : (k + 1) * strip]
        )
    edge_copy = core_copy(edge, edge_in, 1)
    edge_copy.start()
    seen = nn(theirs, swap)
    beside[0:strip, :] = jnp.zeros((strip, 4 * pts), f32)
    beside[(hi + 1) * strip :, :] = jnp.zeros((strip, 4 * pts), f32)
    part_copy.wait_recv()
    edge_copy.wait_recv()
    for k in range(hi):
        got = edge_in[k * strip : (k + 1) * strip, :]
        column = got[:, 4 * pts - 1 : 4 * pts]
        beside[(k + 1) * strip : (k + 2) * strip, :] = (
            seen[k * strip : (k + 1) * strip] + got
        ) * column

    speed = speeds[me]
    t_row = lax.broadcasted_iota(jnp.int32, (strip, 4 * pts), 0)
    d_row, a_row, b_row = t_row // members, (t_row % members) // ty, t_row % ty
    face = lanes // pts
    moved = lambda v, n: pltpu.roll(v, n % strip, 0)
    for k in range(hi):
        own = slice(k * strip, (k + 1) * strip)
        moments = acc[1, own, :] + part_in[own, :].astype(f32)
        m_hi, m_lo = split(moments)
        both = nn(m_hi, table[...]) * inverse[k]
        mine_t, cur = both[:, : 4 * pts], both[:, 4 * pts :]
        prev = beside[pl.ds(pl.multiple_of((k + r) * strip, strip), strip), :]
        after = beside[pl.ds(pl.multiple_of((k + r + 1) * strip, strip), strip), :]
        last = (TX - 1) * ty
        west = jnp.where(a_row > 0, moved(cur, ty), moved(prev, -last))
        east = jnp.where(a_row < TX - 1, moved(cur, -ty), moved(after, last))
        jump = members - (ty - 1)
        south = jnp.where(b_row > 0, moved(cur, 1), moved(cur, jump))
        south = jnp.where((b_row == 0) & (d_row == 0), 0.0, south)
        north = jnp.where(b_row < ty - 1, moved(cur, -1), moved(cur, -jump))
        north = jnp.where((b_row == ty - 1) & (d_row == gy - 1), 0.0, north)
        other = jnp.where(
            face < 2, jnp.where(face == 0, west, east), jnp.where(face == 2, south, north)
        )
        jumps = ((other - mine_t) * speed).astype(bf16)
        solved = nn(m_hi, inv_hi[...]) + nn(m_lo, inv_hi[...]) + nn(m_hi, inv_lo[...])
        solved = (solved + nn(jumps, lift_inv[...])) * inverse[k]
        result[k * lo : (k + 1) * lo] = solved.astype(bf16).reshape(lo, members, modes)
        for c in range(lo):
            to_l = (l + c) % lo

            def back_copy():
                return pltpu.make_async_remote_copy(
                    src_ref=result.at[k * lo + to_l],
                    dst_ref=back.at[me],
                    send_sem=back_send.at[k * lo + c],
                    recv_sem=back_recv.at[me],
                    device_id=(k, r, to_l),
                    device_id_type=MESH,
                )

            if c == 0:
                pl.when(h != k)(lambda: back_copy().start())
            else:
                back_copy().start()
    back[me] = result[me]

    for at in range(group):

        @pl.when(me != at)
        def _():
            pltpu.make_async_remote_copy(
                src_ref=back.at[at],
                dst_ref=back.at[at],
                send_sem=back_send.at[0],
                recv_sem=back_recv.at[at],
                device_id=core,
                device_id_type=MESH,
            ).wait_recv()

    for at in range(group):
        out[:, at, :] = back[at].astype(f32)

    for copy, when in sent:
        if when is None:
            copy.wait_send()
        else:
            pl.when(when)(copy.wait_send)
    for copy in others + [part_copy, edge_copy]:
        copy.wait_send()
    for k in range(hi):
        for c in range(lo):

            def leave_wait():
                pltpu.make_async_remote_copy(
                    src_ref=result.at[k * lo],
                    dst_ref=back.at[me],
                    send_sem=back_send.at[k * lo + c],
                    recv_sem=back_recv.at[me],
                    device_id=core,
                    device_id_type=MESH,
                ).wait_send()

            if c == 0:
                pl.when(h != k)(leave_wait)
            else:
                leave_wait()


def fused(sizes, gy, *args):
    src, slot_rows, owner, _, _, vander, test_fn, inv, trace, lift, speeds = args
    hi, rep, lo = sizes
    members, points = slot_rows.shape
    modes, columns = src.shape
    slot_count = owner.shape[0]
    group = hi * lo
    strip = gy * members
    half = hi * strip
    faces = trace.shape[1]
    width = slot_count * members
    bf16, f32 = jnp.bfloat16, jnp.float32
    any_, vmem = pl.BlockSpec(memory_space=pl.ANY), pl.BlockSpec(memory_space=pltpu.VMEM)
    smem = pl.BlockSpec(memory_space=pltpu.SMEM)
    dma = pltpu.SemaphoreType.DMA
    like = lambda a: pltpu.VMEM(a.shape, a.dtype)
    slot_sends = 8 + lo * 5
    return pl.pallas_call(
        functools.partial(fused_kernel, sizes, gy),
        out_shape=pltpu.VMEM((members, columns // members, modes), f32),
        in_specs=[any_, any_, vmem, vmem, vmem, any_, any_, any_, any_, any_, smem],
        out_specs=vmem,
        scratch_shapes=[
            like(src),
            like(slot_rows),
            like(vander),
            like(test_fn),
            like(inv),
            like(trace),
            like(lift),
            pltpu.VMEM(inv.shape, bf16),
            pltpu.VMEM(inv.shape, bf16),
            pltpu.VMEM((modes, 2 * faces), bf16),
            pltpu.VMEM(lift.shape, bf16),
            pltpu.VMEM((group, members, modes), bf16),
            pltpu.VMEM((group, members, modes), bf16),
            pltpu.VMEM((group, members, points), bf16),
            pltpu.VMEM((8, width), f32),
            pltpu.VMEM((group, 8, width), f32),
            pltpu.VMEM((2, half, hi * width), bf16),
            pltpu.VMEM((2, half, modes), f32),
            pltpu.VMEM((half, modes), bf16),
            pltpu.VMEM((half, modes), bf16),
            pltpu.VMEM((half, faces), f32),
            pltpu.VMEM((half, faces), f32),
            pltpu.VMEM((half + 2 * strip, faces), f32),
            pltpu.VMEM((group, members, modes), bf16),
            pltpu.VMEM((group, members, modes), bf16),
            dma((7,)),
            dma((slot_sends,)),
            dma((group,)),
            dma((group,)),
            dma((group,)),
            dma((group,)),
            dma((group,)),
            dma((2,)),
            dma((2,)),
            dma((group,)),
            dma((group,)),
        ],
        compiler_params=pltpu.CompilerParams(
            collective_id=2, has_side_effects=True, vmem_limit_bytes=56 << 20
        ),
        name="remap",
    )(*args)


def fused_device(sizes, gy, src_coef, point_slot, tgt_owner, tgt_local, vander, test_fn, inv_mass, jacobian, trace_tab, lift_tab, wave_speed):
    return fused(
        sizes,
        gy,
        src_coef,
        point_slot.T,
        tgt_owner.T,
        tgt_local.T,
        jacobian[None, :],
        vander,
        test_fn,
        inv_mass,
        trace_tab,
        lift_tab,
        wave_speed,
    )


def solution(mesh):
    gx, gy = mesh.shape["gx"], mesh.shape["gy"]
    devices = gx * gy

    def call(*args):
        fields = args[-1].shape[0]
        sizes = (fields // gy, devices // fields, gy)
        body = functools.partial(per_device, gx, gy)
        if sizes == (4, 2, 4):
            body = functools.partial(fused_device, sizes, gy)
        return jax.shard_map(
            body,
            mesh=Mesh(mesh.devices.reshape(sizes), WORLD),
            in_specs=(
                P(None, WORLD),
                P(None, WORLD),
                P(WORLD, None),
                P(WORLD, None),
                P(),
                P(),
                P(),
                P(WORLD),
                P(),
                P(),
                P(),
            ),
            out_specs=P(WORLD, None, None),
            check_vma=False,
        )(*args)

    return call
```

```python
import functools

import jax
import jax.numpy as jnp
from jax import lax
from jax.experimental import pallas as pl
from jax.experimental.pallas import tpu as pltpu
from jax.sharding import Mesh, PartitionSpec as P

TX = 8
MESH = pl.DeviceIdType.MESH
GROUP = ("hi", "lo")
WORLD = ("hi", "rep", "lo")


def dot(a, b, dims, precision=None):
    return lax.dot_general(
        a, b, (dims, ((), ())), precision=precision, preferred_element_type=jnp.float32
    )


def neighbour_traces(traces, gx, gy, tx, ty):
    face_cols = traces.shape[1]
    pts = face_cols // 4
    grid = traces.reshape(gx, gy, tx, ty, face_cols).transpose(0, 2, 1, 3, 4)
    grid = grid.reshape(gx * tx, gy * ty, face_cols)
    face = lambda k: grid[:, :, k * pts : (k + 1) * pts]
    west = jnp.pad(face(1)[:-1], ((1, 0), (0, 0), (0, 0)))
    east = jnp.pad(face(0)[1:], ((0, 1), (0, 0), (0, 0)))
    south = jnp.pad(face(3)[:, :-1], ((0, 0), (1, 0), (0, 0)))
    north = jnp.pad(face(2)[:, 1:], ((0, 0), (0, 1), (0, 0)))
    joined = jnp.concatenate([west, east, south, north], axis=2) - grid
    joined = joined.reshape(gx, tx, gy, ty, face_cols).transpose(0, 2, 1, 3, 4)
    return joined.reshape(gx * gy * tx * ty, face_cols)


def peer_at(sizes, offset):
    return tuple(
        lax.rem(lax.axis_index(name) + step, size) if step else lax.axis_index(name)
        for name, size, step in zip(WORLD, sizes, offset)
    )


def offsets(sizes):
    hi, rep, lo = sizes
    every = [(a, b, c) for a in range(hi) for b in range(rep) for c in range(lo)]
    return every[1:]


def greet(peers):
    barrier = pltpu.get_barrier_semaphore()
    for peer in peers:
        pl.semaphore_signal(barrier, inc=1, device_id=peer, device_id_type=MESH)
    pl.semaphore_wait(barrier, len(peers))


def push(src, dst, send, recv, peer):
    copy = pltpu.make_async_remote_copy(
        src_ref=src, dst_ref=dst, send_sem=send, recv_sem=recv, device_id=peer, device_id_type=MESH
    )
    copy.start()
    return copy


def enter_kernel(
    sizes,
    blocks,
    slot_rows,
    meta,
    vander,
    test_fn,
    part,
    metas,
    mine,
    slots,
    onehot,
    pieces,
    block_sems,
    slot_sems,
    relay_sems,
    meta_sems,
    local_sems,
):
    hi, rep, lo = sizes
    h, r, l = (lax.axis_index(name) for name in WORLD)
    me = h * lo + l
    device = (h * rep + r) * lo + l
    everyone = offsets(sizes)
    group = [o for o in everyone if o[1] == 0]
    local = [
        pltpu.make_async_copy(slot_rows, slots.at[me], local_sems.at[0]),
        pltpu.make_async_copy(blocks.at[me], mine.at[me], local_sems.at[1]),
        pltpu.make_async_copy(meta, metas.at[device], local_sems.at[2]),
    ]
    for copy in local:
        copy.start()
    greet([peer_at(sizes, o) for o in everyone])

    along, relays = [], []
    for c in range(1, lo):
        peer = peer_at(sizes, (0, 0, c))
        along.append(
            push(slot_rows, slots.at[me], slot_sems.at[0, c], slot_sems.at[1, c], peer)
        )
    for a in range(1, hi):
        peer = peer_at(sizes, (a, 0, 0))
        k = a * lo
        relays.append(
            push(slot_rows, slots.at[me], relay_sems.at[0, k], relay_sems.at[1, k], peer)
        )
    arrive, labels = [], []
    for k, o in enumerate(group):
        to_h, _, to_l = peer = peer_at(sizes, o)
        arrive.append(
            push(
                blocks.at[to_h * lo + to_l],
                mine.at[me],
                block_sems.at[0, k],
                block_sems.at[1, k],
                peer,
            )
        )
    for k, o in enumerate(everyone):
        labels.append(
            push(
                meta, metas.at[device], meta_sems.at[0, k], meta_sems.at[1, k], peer_at(sizes, o)
            )
        )
    for c in range(1, lo):
        along[c - 1].wait_recv()
        place = h * lo + lax.rem(l + lo - c, lo)
        for a in range(1, hi):
            k = a * lo + c
            relays.append(
                push(
                    slots.at[place],
                    slots.at[place],
                    relay_sems.at[0, k],
                    relay_sems.at[1, k],
                    peer_at(sizes, (a, 0, 0)),
                )
            )
    for copy in local:
        copy.wait()
    for copy in labels:
        copy.wait_recv()

    width = meta.shape[1]
    rows = 128

    @pl.loop(0, part.shape[0] // rows)
    def _(i):
        start = pl.multiple_of(i * rows, rows)
        target = (lax.broadcasted_iota(jnp.int32, (rows, width), 0) + start).astype(jnp.float32)
        for g in range(hi * lo):
            ids = metas[(g // lo * rep + r) * lo + g % lo][0:1, :]
            onehot[pl.ds(start, rows), g * width : (g + 1) * width] = jnp.where(
                target == ids, 1.0, 0.0
            ).astype(onehot.dtype)

    members = slot_rows.shape[0]
    slot_count = width // members
    for a in range(hi):
        for c in range(lo):
            if a or c:
                arrive[a * lo + c - 1].wait_recv()
            if a:
                relays[(a - 1) if c == 0 else (hi - 1) * c + a - 1].wait_recv()
        from_h = lax.rem(h + hi - a, hi)
        first = from_h * lo
        source = mine[pl.ds(first, lo)].reshape(lo * members, -1)
        values = dot(source, vander[...], ((1,), (1,)))
        parts = []
        for c in range(lo):
            where = slots[first + c].astype(jnp.float32)
            value = values[c * members : (c + 1) * members]
            for s in range(slot_count):
                parts.append(jnp.where(where == s, value, 0.0).astype(jnp.bfloat16))
        masked = jnp.concatenate(parts, axis=0)
        pieces[from_h] = dot(masked, test_fn[...], ((1,), (0,))).astype(jnp.bfloat16)

    every = pieces.shape[0] * pieces.shape[1]
    block = 256

    @pl.loop(0, part.shape[0] // block)
    def _(i):
        start = pl.multiple_of(i * block, block)
        summed = dot(
            onehot[pl.ds(start, block), :], pieces[...].reshape(every, -1), ((1,), (0,))
        )
        part[pl.ds(start, block), :] = summed.astype(part.dtype)

    for copy in along + relays + arrive + labels:
        copy.wait_send()


def enter(sizes, blocks, slot_rows, meta, vander, test_fn):
    hi, rep, lo = sizes
    world = hi * rep * lo
    _, members, modes = blocks.shape
    vmem = pl.BlockSpec(memory_space=pltpu.VMEM)
    dma = pltpu.SemaphoreType.DMA
    return pl.pallas_call(
        functools.partial(enter_kernel, sizes),
        out_shape=(
            jax.ShapeDtypeStruct((world * members, modes), jnp.bfloat16),
            jax.ShapeDtypeStruct((world, *meta.shape), meta.dtype),
        ),
        in_specs=[vmem] * 5,
        out_specs=(vmem,) * 2,
        scratch_shapes=[
            pltpu.VMEM(blocks.shape, blocks.dtype),
            pltpu.VMEM((hi * lo, *slot_rows.shape), slot_rows.dtype),
            pltpu.VMEM((world * members, hi * lo * meta.shape[1]), jnp.bfloat16),
            pltpu.VMEM((hi, lo * meta.shape[1], modes), jnp.bfloat16),
            dma((2, hi * lo)),
            dma((2, lo)),
            dma((2, hi * lo)),
            dma((2, world)),
            dma((3,)),
        ],
        compiler_params=pltpu.CompilerParams(
            collective_id=0, has_side_effects=True, vmem_limit_bytes=44 << 20
        ),
        name="enter",
    )(blocks, slot_rows, meta, vander, test_fn)


def leave_kernel(sizes, blocks, mine, sems, local_sem):
    hi, rep, lo = sizes
    me = lax.axis_index("hi") * lo + lax.axis_index("lo")
    group = [o for o in offsets(sizes) if o[1] == 0]
    local = pltpu.make_async_copy(blocks.at[me], mine.at[me], local_sem)
    local.start()
    greet([peer_at(sizes, o) for o in group])
    copies = []
    for k, o in enumerate(group):
        to_h, _, to_l = peer = peer_at(sizes, o)
        copies.append(
            push(blocks.at[to_h * lo + to_l], mine.at[me], sems.at[0, k], sems.at[1, k], peer)
        )
    for copy in copies:
        copy.wait()
    local.wait()


def leave(sizes, blocks):
    vmem = pl.BlockSpec(memory_space=pltpu.VMEM)
    dma = pltpu.SemaphoreType.DMA
    return pl.pallas_call(
        functools.partial(leave_kernel, sizes),
        out_shape=jax.ShapeDtypeStruct(blocks.shape, blocks.dtype),
        in_specs=[vmem],
        out_specs=vmem,
        scratch_shapes=[dma((2, sizes[0] * sizes[2])), dma],
        compiler_params=pltpu.CompilerParams(
            collective_id=1, has_side_effects=True, vmem_limit_bytes=8 << 20
        ),
        name="leave",
    )(blocks)


def per_device(
    gx,
    gy,
    src_coef,
    point_slot,
    tgt_owner,
    tgt_local,
    vander,
    test_fn,
    inv_mass,
    jacobian,
    trace_tab,
    lift_tab,
    wave_speed,
):
    bf16 = jnp.bfloat16
    high = lax.Precision.HIGH
    modes, columns = src_coef.shape
    members = point_slot.shape[1]
    fields = wave_speed.shape[0]
    reps = lax.axis_size("rep")
    my_rep = lax.axis_index("rep")
    my_field = lax.axis_index("hi") * lax.axis_size("lo") + lax.axis_index("lo")

    row = jnp.arange(columns, dtype=jnp.int32)
    wanted = (row % members) * fields + row // members
    perm = (wanted[:, None] == row[None, :]).astype(bf16)
    by_field = dot(perm, src_coef, ((1,), (1,))).astype(bf16)
    sizes = tuple(lax.axis_size(name) for name in WORLD)
    holders = sizes[0] * sizes[2]
    ids = (tgt_owner * members + tgt_local).T.reshape(1, -1).astype(jnp.float32)
    jac = jnp.pad(jacobian[None, :], ((0, 0), (0, ids.shape[1] - members)))
    meta = jnp.pad(jnp.concatenate([ids, jac], axis=0), ((0, 6), (0, 0)))
    part, metas = enter(
        sizes,
        by_field.reshape(holders, members, modes),
        point_slot.T.astype(bf16),
        meta,
        vander,
        test_fn,
    )
    jac = metas[:, 1, :members].reshape(-1, 1)
    if reps == 2:
        other = lax.ppermute(part, "rep", [(0, 1), (1, 0)])
        moments = part.astype(jnp.float32) + other.astype(jnp.float32)
    else:
        moments = lax.psum(part.astype(jnp.float32), "rep")

    coeffs = dot(moments, inv_mass, ((1,), (0,)), high) / jac
    traces = dot(coeffs, trace_tab, ((1,), (0,)), high)
    jumps = neighbour_traces(traces, gx, gy, TX, members // TX)
    own = lambda x: lax.dynamic_index_in_dim(
        x.reshape(-1, reps, gy * members, x.shape[-1]), my_rep, 1, keepdims=False
    ).reshape(-1, x.shape[-1])
    lift = dot(lift_tab, inv_mass, ((1,), (0,)), high)
    speed = lax.dynamic_index_in_dim(wave_speed, my_field, 0, keepdims=False)
    update = dot(own(jumps), lift, ((1,), (0,)), high) * (speed / own(jac))
    result = (own(coeffs) + update).astype(bf16)
    back = leave(sizes, result.reshape(holders, members, modes))
    back = back.transpose(1, 0, 2)
    return back.astype(jnp.float32)


def nt(a, b):
    return dot(a, b, ((1,), (1,)))


def nn(a, b):
    return dot(a, b, ((1,), (0,)))


def split(x):
    high = x.astype(jnp.bfloat16)
    return high, (x - high.astype(jnp.float32)).astype(jnp.bfloat16)


def nn3(a, b):
    (ah, al), (bh, bl) = split(a), split(b)
    return nn(ah, bh) + nn(al, bh) + nn(ah, bl)


def fused_kernel(
    sizes,
    gy,
    src,
    slot_rows,
    owner,
    local_id,
    jac,
    vander_hbm,
    test_hbm,
    inv_hbm,
    trace_hbm,
    lift_hbm,
    speeds,
    out,
    coef,
    slot_in,
    vander,
    test_fn,
    inv,
    trace,
    lift,
    inv_hi,
    inv_lo,
    table,
    lift_inv,
    blocks,
    mine,
    slots,
    meta,
    metas,
    onehot,
    acc,
    part,
    part_in,
    edge,
    edge_in,
    beside,
    result,
    back,
    load_sems,
    slot_send,
    slot_recv,
    block_send,
    block_recv,
    meta_send,
    meta_recv,
    core_send,
    core_recv,
    back_send,
    back_recv,
):
    hi, rep, lo = sizes
    bf16, f32 = jnp.bfloat16, jnp.float32
    h, r, l = (lax.axis_index(name) for name in WORLD)
    me = h * lo + l
    group = hi * lo
    members, points = slot_rows.shape
    modes, columns = src.shape
    slot_count = owner.shape[0]
    fields = columns // members
    ty = members // TX
    width = slot_count * members
    strip = gy * members
    half = hi * strip

    y, x = h // 2, h % 2
    flip_x = y * 2 + (1 - x)
    flip_y = (1 - y) * 2 + x
    flip_xy = (1 - y) * 2 + (1 - x)
    near = [h, flip_x, flip_y, flip_xy]
    core = (h, 1 - r, l)

    barrier = pltpu.get_barrier_semaphore()
    for o in offsets((hi, 1, lo)):
        pl.semaphore_signal(
            barrier, inc=1, device_id=peer_at((hi, 1, lo), o), device_id_type=MESH
        )
    pl.semaphore_signal(barrier, inc=1, device_id=core, device_id_type=MESH)

    loads = []
    for k, (a, b) in enumerate(
        [
            (src, coef),
            (slot_rows, slot_in),
            (vander_hbm, vander),
            (test_hbm, test_fn),
            (inv_hbm, inv),
            (trace_hbm, trace),
            (lift_hbm, lift),
        ]
    ):
        copy = pltpu.make_async_copy(a, b, load_sems.at[k])
        copy.start()
        loads.append(copy)

    loads[1].wait()
    slots[me] = slot_in[...].astype(f32).astype(bf16)
    pl.semaphore_wait(barrier, group)

    sent = []

    def slot_copy(at, k, to):
        return pltpu.make_async_remote_copy(
            src_ref=slots.at[at],
            dst_ref=slots.at[at],
            send_sem=slot_send.at[k],
            recv_sem=slot_recv.at[at],
            device_id=to,
            device_id_type=MESH,
        )

    def send_slot(at, to):
        copy = slot_copy(at, len(sent), to)
        sent.append((copy, None))
        copy.start()

    def wait_slot(at):
        slot_copy(at, 0, core).wait_recv()

    partner = l + 1 - 2 * (l % 2)
    lower = l < 2
    near_z = jnp.where(lower, 2, 1)
    far_z = jnp.where(lower, 3, 0)
    inner = (l == 1) | (l == 2)
    outer = jnp.where(lower, 0, 3)
    line = [l, partner, near_z, far_z]

    send_slot(me, (h, r, near_z))
    send_slot(me, (h, r, partner))
    for to_h in near[1:]:
        send_slot(me, (to_h, r, l))

    others = []

    def send_block(k, c):
        to_h, to_l = near[k], line[c]
        copy = pltpu.make_async_remote_copy(
            src_ref=blocks.at[to_h * lo + to_l],
            dst_ref=mine.at[me],
            send_sem=block_send.at[k * lo + c],
            recv_sem=block_recv.at[me],
            device_id=(to_h, r, to_l),
            device_id_type=MESH,
        )
        copy.start()
        others.append(copy)

    meta[...] = jnp.zeros_like(meta)
    meta[0:slot_count, 0:members] = (owner[...] * members + local_id[...]).astype(f32)
    meta[slot_count : slot_count + 1, 0:members] = jac[...]
    packed = meta[...]
    row = lax.broadcasted_iota(jnp.int32, packed.shape, 0)
    lane = lax.broadcasted_iota(jnp.int32, packed.shape, 1)
    ids = jnp.zeros_like(packed)
    for s in range(slot_count):
        turned = pltpu.roll(packed, s * members, 1) if s else packed
        ids = jnp.where((row == s) & (lane // members == s), turned, ids)
    ids = jnp.sum(ids, axis=0, keepdims=True)
    jacs = jnp.zeros_like(packed)
    for c in range(lo):
        turned = pltpu.roll(packed, c * members, 1) if c else packed
        here = (row == slot_count) & (lane // members == c) & (lane // members == l)
        jacs = jnp.where(here, turned, jacs)
    jacs = jnp.sum(jacs, axis=0, keepdims=True)
    packed = jnp.where(row == 0, ids, jnp.where(row == 1, jacs, 0.0))
    meta[...] = packed
    metas[me] = packed

    for k, to_h in enumerate(near):
        for c in range(1 if k == 0 else 0, lo):
            to_l = (l + c) % lo
            copy = pltpu.make_async_remote_copy(
                src_ref=meta,
                dst_ref=metas.at[me],
                send_sem=meta_send.at[k * lo + c],
                recv_sem=meta_recv.at[me],
                device_id=(to_h, r, to_l),
                device_id_type=MESH,
            )
            copy.start()
            others.append(copy)

    loads[0].wait()
    rows = lo * members
    r_iota = lax.broadcasted_iota(jnp.int32, (rows, columns), 0)
    c_iota = lax.broadcasted_iota(jnp.int32, (rows, columns), 1)
    r_iota = (r_iota % members) * fields + r_iota // members
    for k in (1, 2, 3, 0):
        first = near[k] * lo
        perm = (r_iota + first == c_iota).astype(f32).astype(bf16)
        moved = nt(perm, coef[...]).astype(bf16)
        blocks[pl.ds(first, lo)] = moved.reshape(lo, members, modes)
        if k:
            send_block(k, 0)
    mine[me] = blocks[me]


    for i in range(1, lo):
        z = line[i]
        at = h * lo + z
        wait_slot(at)
        if i > 1:
            copy = slot_copy(at, len(sent), (h, r, outer))
            sent.append((copy, inner))
            pl.when(inner)(copy.start)
        for k in (3, 1, 2, 0):
            if k in (1, 2, 3):
                send_slot(at, (near[k], r, l))
            send_block(k, i)

    def wait_block(at):
        pltpu.make_async_remote_copy(
            src_ref=mine.at[at],
            dst_ref=mine.at[at],
            send_sem=block_send.at[0],
            recv_sem=block_recv.at[at],
            device_id=core,
            device_id_type=MESH,
        ).wait_recv()
        pltpu.make_async_remote_copy(
            src_ref=metas.at[at],
            dst_ref=metas.at[at],
            send_sem=meta_send.at[0],
            recv_sem=meta_recv.at[at],
            device_id=core,
            device_id_type=MESH,
        ).wait_recv()

    for copy in loads[2:]:
        copy.wait()
    high, low = split(inv[...])
    inv_hi[...] = high
    inv_lo[...] = low
    traced = nn3(inv[...], trace[...])
    pts = trace.shape[1] // 4
    table[:, : 4 * pts] = traced.astype(bf16)
    face = lax.broadcasted_iota(jnp.int32, traced.shape, 1) // pts
    swapped = jnp.where(
        face % 2 == 0, pltpu.roll(traced, 3 * pts, 1), pltpu.roll(traced, pts, 1)
    )
    table[:, 4 * pts :] = swapped.astype(bf16)
    lift_inv[...] = nn3(lift[...], inv[...]).astype(bf16)

    place = lax.broadcasted_iota(jnp.int32, (half, width), 0)
    place = (place // strip) * (2 * strip) + place % strip

    def gather(places):
        source = jnp.concatenate([mine[at] for at in places], axis=0)
        values = nt(source, vander[...]).astype(bf16).astype(f32)
        parts = []
        for c, at in enumerate(places):
            where = slots[at].astype(f32)
            value = values[c * members : (c + 1) * members]
            for s in range(slot_count):
                parts.append(jnp.where(where == s, value, 0.0).astype(bf16))
        pieces = nn(jnp.concatenate(parts, axis=0), test_fn[...]).astype(bf16)
        for side in range(2):
            shift = (1 - r if side == 0 else r) * strip
            for c, at in enumerate(places):
                targets = (metas[at][0:1, :]).astype(jnp.int32) - shift
                onehot[side, :, c * width : (c + 1) * width] = (
                    jnp.where(place == targets, 1.0, 0.0).astype(bf16)
                )
        return pieces

    def scatter(pieces, side, first):
        summed = nn(onehot[side], pieces)
        return summed if first else acc[side] + summed

    for k, z in enumerate(line):
        places = [at * lo + z for at in near]
        for at in places[1:]:
            wait_slot(at)
        for at in places[0 if k else 1 :]:
            wait_block(at)
        pieces = gather(places)
        if k < lo - 1:
            for side in range(2):
                acc[side] = scatter(pieces, side, k == 0)

    def core_copy(a, b, k):
        return pltpu.make_async_remote_copy(
            src_ref=a,
            dst_ref=b,
            send_sem=core_send.at[k],
            recv_sem=core_recv.at[k],
            device_id=core,
            device_id_type=MESH,
        )

    theirs = scatter(pieces, 0, False).astype(bf16)
    part[...] = theirs
    part_copy = core_copy(part, part_in, 0)
    part_copy.start()
    ours = scatter(pieces, 1, False)
    acc[1] = ours
    swap = table[:, 4 * pts :]
    seen = nn(ours.astype(bf16), swap)
    eye_r = lax.broadcasted_iota(jnp.int32, (strip, strip), 0)
    eye_c = lax.broadcasted_iota(jnp.int32, (strip, strip), 1)
    lanes = lax.broadcasted_iota(jnp.int32, (strip, 4 * pts), 1)
    inverse = []
    for k in range(hi):
        jac_row = metas[k * lo][1:2, :]
        for c in range(1, lo):
            jac_row = jac_row + metas[k * lo + c][1:2, :]
        column = jnp.sum(jnp.where(eye_r == eye_c, jac_row, 0.0), axis=1, keepdims=True)
        column = 1.0 / column
        inverse.append(column)
        edge[k * strip : (k + 1) * strip, :] = jnp.where(
            lanes == 4 * pts - 1, column, seen[k * strip : (k + 1) * strip]
        )
    edge_copy = core_copy(edge, edge_in, 1)
    edge_copy.start()
    seen = nn(theirs, swap)
    beside[0:strip, :] = jnp.zeros((strip, 4 * pts), f32)
    beside[(hi + 1) * strip :, :] = jnp.zeros((strip, 4 * pts), f32)
    part_copy.wait_recv()
    edge_copy.wait_recv()
    for k in range(hi):
        got = edge_in[k * strip : (k + 1) * strip, :]
        column = got[:, 4 * pts - 1 : 4 * pts]
        beside[(k + 1) * strip : (k + 2) * strip, :] = (
            seen[k * strip : (k + 1) * strip] + got
        ) * column

    speed = speeds[me]
    t_row = lax.broadcasted_iota(jnp.int32, (strip, 4 * pts), 0)
    d_row, a_row, b_row = t_row // members, (t_row % members) // ty, t_row % ty
    face = lanes // pts
    moved = lambda v, n: pltpu.roll(v, n % strip, 0)
    for k in range(hi):
        own = slice(k * strip, (k + 1) * strip)
        moments = acc[1, own, :] + part_in[own, :].astype(f32)
        m_hi, m_lo = split(moments)
        both = nn(m_hi, table[...]) * inverse[k]
        mine_t, cur = both[:, : 4 * pts], both[:, 4 * pts :]
        prev = beside[pl.ds(pl.multiple_of((k + r) * strip, strip), strip), :]
        after = beside[pl.ds(pl.multiple_of((k + r + 1) * strip, strip), strip), :]
        last = (TX - 1) * ty
        west = jnp.where(a_row > 0, moved(cur, ty), moved(prev, -last))
        east = jnp.where(a_row < TX - 1, moved(cur, -ty), moved(after, last))
        jump = members - (ty - 1)
        south = jnp.where(b_row > 0, moved(cur, 1), moved(cur, jump))
        south = jnp.where((b_row == 0) & (d_row == 0), 0.0, south)
        north = jnp.where(b_row < ty - 1, moved(cur, -1), moved(cur, -jump))
        north = jnp.where((b_row == ty - 1) & (d_row == gy - 1), 0.0, north)
        other = jnp.where(
            face < 2, jnp.where(face == 0, west, east), jnp.where(face == 2, south, north)
        )
        jumps = ((other - mine_t) * speed).astype(bf16)
        solved = nn(m_hi, inv_hi[...]) + nn(m_lo, inv_hi[...]) + nn(m_hi, inv_lo[...])
        solved = (solved + nn(jumps, lift_inv[...])) * inverse[k]
        result[k * lo : (k + 1) * lo] = solved.astype(bf16).reshape(lo, members, modes)
        for c in range(lo):
            to_l = (l + c) % lo

            def back_copy():
                return pltpu.make_async_remote_copy(
                    src_ref=result.at[k * lo + to_l],
                    dst_ref=back.at[me],
                    send_sem=back_send.at[k * lo + c],
                    recv_sem=back_recv.at[me],
                    device_id=(k, r, to_l),
                    device_id_type=MESH,
                )

            if c == 0:
                pl.when(h != k)(lambda: back_copy().start())
            else:
                back_copy().start()
    back[me] = result[me]

    for copy, when in sent:
        if when is None:
            copy.wait_send()
        else:
            pl.when(when)(copy.wait_send)
    for copy in others + [part_copy, edge_copy]:
        copy.wait_send()
    for k in range(hi):
        for c in range(lo):

            def leave_wait():
                pltpu.make_async_remote_copy(
                    src_ref=result.at[k * lo],
                    dst_ref=back.at[me],
                    send_sem=back_send.at[k * lo + c],
                    recv_sem=back_recv.at[me],
                    device_id=core,
                    device_id_type=MESH,
                ).wait_send()

            if c == 0:
                pl.when(h != k)(leave_wait)
            else:
                leave_wait()

    for at in range(group):

        @pl.when(me != at)
        def _():
            pltpu.make_async_remote_copy(
                src_ref=back.at[at],
                dst_ref=back.at[at],
                send_sem=back_send.at[0],
                recv_sem=back_recv.at[at],
                device_id=core,
                device_id_type=MESH,
            ).wait_recv()

    for at in range(group):
        out[:, at, :] = back[at].astype(f32)


def fused(sizes, gy, *args):
    src, slot_rows, owner, _, _, vander, test_fn, inv, trace, lift, speeds = args
    hi, rep, lo = sizes
    members, points = slot_rows.shape
    modes, columns = src.shape
    slot_count = owner.shape[0]
    group = hi * lo
    strip = gy * members
    half = hi * strip
    faces = trace.shape[1]
    width = slot_count * members
    bf16, f32 = jnp.bfloat16, jnp.float32
    any_, vmem = pl.BlockSpec(memory_space=pl.ANY), pl.BlockSpec(memory_space=pltpu.VMEM)
    smem = pl.BlockSpec(memory_space=pltpu.SMEM)
    dma = pltpu.SemaphoreType.DMA
    like = lambda a: pltpu.VMEM(a.shape, a.dtype)
    slot_sends = 8 + lo * 5
    return pl.pallas_call(
        functools.partial(fused_kernel, sizes, gy),
        out_shape=pltpu.VMEM((members, columns // members, modes), f32),
        in_specs=[any_, any_, vmem, vmem, vmem, any_, any_, any_, any_, any_, smem],
        out_specs=vmem,
        scratch_shapes=[
            like(src),
            like(slot_rows),
            like(vander),
            like(test_fn),
            like(inv),
            like(trace),
            like(lift),
            pltpu.VMEM(inv.shape, bf16),
            pltpu.VMEM(inv.shape, bf16),
            pltpu.VMEM((modes, 2 * faces), bf16),
            pltpu.VMEM(lift.shape, bf16),
            pltpu.VMEM((group, members, modes), bf16),
            pltpu.VMEM((group, members, modes), bf16),
            pltpu.VMEM((group, members, points), bf16),
            pltpu.VMEM((8, width), f32),
            pltpu.VMEM((group, 8, width), f32),
            pltpu.VMEM((2, half, hi * width), bf16),
            pltpu.VMEM((2, half, modes), f32),
            pltpu.VMEM((half, modes), bf16),
            pltpu.VMEM((half, modes), bf16),
            pltpu.VMEM((half, faces), f32),
            pltpu.VMEM((half, faces), f32),
            pltpu.VMEM((half + 2 * strip, faces), f32),
            pltpu.VMEM((group, members, modes), bf16),
            pltpu.VMEM((group, members, modes), bf16),
            dma((7,)),
            dma((slot_sends,)),
            dma((group,)),
            dma((group,)),
            dma((group,)),
            dma((group,)),
            dma((group,)),
            dma((2,)),
            dma((2,)),
            dma((group,)),
            dma((group,)),
        ],
        compiler_params=pltpu.CompilerParams(
            collective_id=2, has_side_effects=True, vmem_limit_bytes=56 << 20
        ),
        name="remap",
    )(*args)


def fused_device(sizes, gy, src_coef, point_slot, tgt_owner, tgt_local, vander, test_fn, inv_mass, jacobian, trace_tab, lift_tab, wave_speed):
    return fused(
        sizes,
        gy,
        src_coef,
        point_slot.T,
        tgt_owner.T,
        tgt_local.T,
        jacobian[None, :],
        vander,
        test_fn,
        inv_mass,
        trace_tab,
        lift_tab,
        wave_speed,
    )


def solution(mesh):
    gx, gy = mesh.shape["gx"], mesh.shape["gy"]
    devices = gx * gy

    def call(*args):
        fields = args[-1].shape[0]
        sizes = (fields // gy, devices // fields, gy)
        body = functools.partial(per_device, gx, gy)
        if sizes == (4, 2, 4):
            body = functools.partial(fused_device, sizes, gy)
        return jax.shard_map(
            body,
            mesh=Mesh(mesh.devices.reshape(sizes), WORLD),
            in_specs=(
                P(None, WORLD),
                P(None, WORLD),
                P(WORLD, None),
                P(WORLD, None),
                P(),
                P(),
                P(),
                P(WORLD),
                P(),
                P(),
                P(),
            ),
            out_specs=P(WORLD, None, None),
            check_vma=False,
        )(*args)

    return call
```

```python
import functools

import jax
import jax.numpy as jnp
from jax import lax
from jax.experimental import pallas as pl
from jax.experimental.pallas import tpu as pltpu
from jax.sharding import Mesh, PartitionSpec as P

TX = 8
MESH = pl.DeviceIdType.MESH
GROUP = ("hi", "lo")
WORLD = ("hi", "rep", "lo")


def dot(a, b, dims, precision=None):
    return lax.dot_general(
        a, b, (dims, ((), ())), precision=precision, preferred_element_type=jnp.float32
    )


def neighbour_traces(traces, gx, gy, tx, ty):
    face_cols = traces.shape[1]
    pts = face_cols // 4
    grid = traces.reshape(gx, gy, tx, ty, face_cols).transpose(0, 2, 1, 3, 4)
    grid = grid.reshape(gx * tx, gy * ty, face_cols)
    face = lambda k: grid[:, :, k * pts : (k + 1) * pts]
    west = jnp.pad(face(1)[:-1], ((1, 0), (0, 0), (0, 0)))
    east = jnp.pad(face(0)[1:], ((0, 1), (0, 0), (0, 0)))
    south = jnp.pad(face(3)[:, :-1], ((0, 0), (1, 0), (0, 0)))
    north = jnp.pad(face(2)[:, 1:], ((0, 0), (0, 1), (0, 0)))
    joined = jnp.concatenate([west, east, south, north], axis=2) - grid
    joined = joined.reshape(gx, tx, gy, ty, face_cols).transpose(0, 2, 1, 3, 4)
    return joined.reshape(gx * gy * tx * ty, face_cols)


def peer_at(sizes, offset):
    return tuple(
        lax.rem(lax.axis_index(name) + step, size) if step else lax.axis_index(name)
        for name, size, step in zip(WORLD, sizes, offset)
    )


def offsets(sizes):
    hi, rep, lo = sizes
    every = [(a, b, c) for a in range(hi) for b in range(rep) for c in range(lo)]
    return every[1:]


def greet(peers):
    barrier = pltpu.get_barrier_semaphore()
    for peer in peers:
        pl.semaphore_signal(barrier, inc=1, device_id=peer, device_id_type=MESH)
    pl.semaphore_wait(barrier, len(peers))


def push(src, dst, send, recv, peer):
    copy = pltpu.make_async_remote_copy(
        src_ref=src, dst_ref=dst, send_sem=send, recv_sem=recv, device_id=peer, device_id_type=MESH
    )
    copy.start()
    return copy


def enter_kernel(
    sizes,
    blocks,
    slot_rows,
    meta,
    vander,
    test_fn,
    part,
    metas,
    mine,
    slots,
    onehot,
    pieces,
    block_sems,
    slot_sems,
    relay_sems,
    meta_sems,
    local_sems,
):
    hi, rep, lo = sizes
    h, r, l = (lax.axis_index(name) for name in WORLD)
    me = h * lo + l
    device = (h * rep + r) * lo + l
    everyone = offsets(sizes)
    group = [o for o in everyone if o[1] == 0]
    local = [
        pltpu.make_async_copy(slot_rows, slots.at[me], local_sems.at[0]),
        pltpu.make_async_copy(blocks.at[me], mine.at[me], local_sems.at[1]),
        pltpu.make_async_copy(meta, metas.at[device], local_sems.at[2]),
    ]
    for copy in local:
        copy.start()
    greet([peer_at(sizes, o) for o in everyone])

    along, relays = [], []
    for c in range(1, lo):
        peer = peer_at(sizes, (0, 0, c))
        along.append(
            push(slot_rows, slots.at[me], slot_sems.at[0, c], slot_sems.at[1, c], peer)
        )
    for a in range(1, hi):
        peer = peer_at(sizes, (a, 0, 0))
        k = a * lo
        relays.append(
            push(slot_rows, slots.at[me], relay_sems.at[0, k], relay_sems.at[1, k], peer)
        )
    arrive, labels = [], []
    for k, o in enumerate(group):
        to_h, _, to_l = peer = peer_at(sizes, o)
        arrive.append(
            push(
                blocks.at[to_h * lo + to_l],
                mine.at[me],
                block_sems.at[0, k],
                block_sems.at[1, k],
                peer,
            )
        )
    for k, o in enumerate(everyone):
        labels.append(
            push(
                meta, metas.at[device], meta_sems.at[0, k], meta_sems.at[1, k], peer_at(sizes, o)
            )
        )
    for c in range(1, lo):
        along[c - 1].wait_recv()
        place = h * lo + lax.rem(l + lo - c, lo)
        for a in range(1, hi):
            k = a * lo + c
            relays.append(
                push(
                    slots.at[place],
                    slots.at[place],
                    relay_sems.at[0, k],
                    relay_sems.at[1, k],
                    peer_at(sizes, (a, 0, 0)),
                )
            )
    for copy in local:
        copy.wait()
    for copy in labels:
        copy.wait_recv()

    width = meta.shape[1]
    rows = 128

    @pl.loop(0, part.shape[0] // rows)
    def _(i):
        start = pl.multiple_of(i * rows, rows)
        target = (lax.broadcasted_iota(jnp.int32, (rows, width), 0) + start).astype(jnp.float32)
        for g in range(hi * lo):
            ids = metas[(g // lo * rep + r) * lo + g % lo][0:1, :]
            onehot[pl.ds(start, rows), g * width : (g + 1) * width] = jnp.where(
                target == ids, 1.0, 0.0
            ).astype(onehot.dtype)

    members = slot_rows.shape[0]
    slot_count = width // members
    for a in range(hi):
        for c in range(lo):
            if a or c:
                arrive[a * lo + c - 1].wait_recv()
            if a:
                relays[(a - 1) if c == 0 else (hi - 1) * c + a - 1].wait_recv()
        from_h = lax.rem(h + hi - a, hi)
        first = from_h * lo
        source = mine[pl.ds(first, lo)].reshape(lo * members, -1)
        values = dot(source, vander[...], ((1,), (1,)))
        parts = []
        for c in range(lo):
            where = slots[first + c].astype(jnp.float32)
            value = values[c * members : (c + 1) * members]
            for s in range(slot_count):
                parts.append(jnp.where(where == s, value, 0.0).astype(jnp.bfloat16))
        masked = jnp.concatenate(parts, axis=0)
        pieces[from_h] = dot(masked, test_fn[...], ((1,), (0,))).astype(jnp.bfloat16)

    every = pieces.shape[0] * pieces.shape[1]
    block = 256

    @pl.loop(0, part.shape[0] // block)
    def _(i):
        start = pl.multiple_of(i * block, block)
        summed = dot(
            onehot[pl.ds(start, block), :], pieces[...].reshape(every, -1), ((1,), (0,))
        )
        part[pl.ds(start, block), :] = summed.astype(part.dtype)

    for copy in along + relays + arrive + labels:
        copy.wait_send()


def enter(sizes, blocks, slot_rows, meta, vander, test_fn):
    hi, rep, lo = sizes
    world = hi * rep * lo
    _, members, modes = blocks.shape
    vmem = pl.BlockSpec(memory_space=pltpu.VMEM)
    dma = pltpu.SemaphoreType.DMA
    return pl.pallas_call(
        functools.partial(enter_kernel, sizes),
        out_shape=(
            jax.ShapeDtypeStruct((world * members, modes), jnp.bfloat16),
            jax.ShapeDtypeStruct((world, *meta.shape), meta.dtype),
        ),
        in_specs=[vmem] * 5,
        out_specs=(vmem,) * 2,
        scratch_shapes=[
            pltpu.VMEM(blocks.shape, blocks.dtype),
            pltpu.VMEM((hi * lo, *slot_rows.shape), slot_rows.dtype),
            pltpu.VMEM((world * members, hi * lo * meta.shape[1]), jnp.bfloat16),
            pltpu.VMEM((hi, lo * meta.shape[1], modes), jnp.bfloat16),
            dma((2, hi * lo)),
            dma((2, lo)),
            dma((2, hi * lo)),
            dma((2, world)),
            dma((3,)),
        ],
        compiler_params=pltpu.CompilerParams(
            collective_id=0, has_side_effects=True, vmem_limit_bytes=44 << 20
        ),
        name="enter",
    )(blocks, slot_rows, meta, vander, test_fn)


def leave_kernel(sizes, blocks, mine, sems, local_sem):
    hi, rep, lo = sizes
    me = lax.axis_index("hi") * lo + lax.axis_index("lo")
    group = [o for o in offsets(sizes) if o[1] == 0]
    local = pltpu.make_async_copy(blocks.at[me], mine.at[me], local_sem)
    local.start()
    greet([peer_at(sizes, o) for o in group])
    copies = []
    for k, o in enumerate(group):
        to_h, _, to_l = peer = peer_at(sizes, o)
        copies.append(
            push(blocks.at[to_h * lo + to_l], mine.at[me], sems.at[0, k], sems.at[1, k], peer)
        )
    for copy in copies:
        copy.wait()
    local.wait()


def leave(sizes, blocks):
    vmem = pl.BlockSpec(memory_space=pltpu.VMEM)
    dma = pltpu.SemaphoreType.DMA
    return pl.pallas_call(
        functools.partial(leave_kernel, sizes),
        out_shape=jax.ShapeDtypeStruct(blocks.shape, blocks.dtype),
        in_specs=[vmem],
        out_specs=vmem,
        scratch_shapes=[dma((2, sizes[0] * sizes[2])), dma],
        compiler_params=pltpu.CompilerParams(
            collective_id=1, has_side_effects=True, vmem_limit_bytes=8 << 20
        ),
        name="leave",
    )(blocks)


def per_device(
    gx,
    gy,
    src_coef,
    point_slot,
    tgt_owner,
    tgt_local,
    vander,
    test_fn,
    inv_mass,
    jacobian,
    trace_tab,
    lift_tab,
    wave_speed,
):
    bf16 = jnp.bfloat16
    high = lax.Precision.HIGH
    modes, columns = src_coef.shape
    members = point_slot.shape[1]
    fields = wave_speed.shape[0]
    reps = lax.axis_size("rep")
    my_rep = lax.axis_index("rep")
    my_field = lax.axis_index("hi") * lax.axis_size("lo") + lax.axis_index("lo")

    row = jnp.arange(columns, dtype=jnp.int32)
    wanted = (row % members) * fields + row // members
    perm = (wanted[:, None] == row[None, :]).astype(bf16)
    by_field = dot(perm, src_coef, ((1,), (1,))).astype(bf16)
    sizes = tuple(lax.axis_size(name) for name in WORLD)
    holders = sizes[0] * sizes[2]
    ids = (tgt_owner * members + tgt_local).T.reshape(1, -1).astype(jnp.float32)
    jac = jnp.pad(jacobian[None, :], ((0, 0), (0, ids.shape[1] - members)))
    meta = jnp.pad(jnp.concatenate([ids, jac], axis=0), ((0, 6), (0, 0)))
    part, metas = enter(
        sizes,
        by_field.reshape(holders, members, modes),
        point_slot.T.astype(bf16),
        meta,
        vander,
        test_fn,
    )
    jac = metas[:, 1, :members].reshape(-1, 1)
    if reps == 2:
        other = lax.ppermute(part, "rep", [(0, 1), (1, 0)])
        moments = part.astype(jnp.float32) + other.astype(jnp.float32)
    else:
        moments = lax.psum(part.astype(jnp.float32), "rep")

    coeffs = dot(moments, inv_mass, ((1,), (0,)), high) / jac
    traces = dot(coeffs, trace_tab, ((1,), (0,)), high)
    jumps = neighbour_traces(traces, gx, gy, TX, members // TX)
    own = lambda x: lax.dynamic_index_in_dim(
        x.reshape(-1, reps, gy * members, x.shape[-1]), my_rep, 1, keepdims=False
    ).reshape(-1, x.shape[-1])
    lift = dot(lift_tab, inv_mass, ((1,), (0,)), high)
    speed = lax.dynamic_index_in_dim(wave_speed, my_field, 0, keepdims=False)
    update = dot(own(jumps), lift, ((1,), (0,)), high) * (speed / own(jac))
    result = (own(coeffs) + update).astype(bf16)
    back = leave(sizes, result.reshape(holders, members, modes))
    back = back.transpose(1, 0, 2)
    return back.astype(jnp.float32)


def nt(a, b):
    return dot(a, b, ((1,), (1,)))


def nn(a, b):
    return dot(a, b, ((1,), (0,)))


def split(x):
    high = x.astype(jnp.bfloat16)
    return high, (x - high.astype(jnp.float32)).astype(jnp.bfloat16)


def nn3(a, b):
    (ah, al), (bh, bl) = split(a), split(b)
    return nn(ah, bh) + nn(al, bh) + nn(ah, bl)


def fused_kernel(
    sizes,
    gy,
    src,
    slot_rows,
    owner,
    local_id,
    jac,
    vander_hbm,
    test_hbm,
    inv_hbm,
    trace_hbm,
    lift_hbm,
    speeds,
    out,
    coef,
    slot_in,
    vander,
    test_fn,
    inv,
    trace,
    lift,
    inv_hi,
    inv_lo,
    table,
    lift_inv,
    blocks,
    mine,
    slots,
    meta,
    metas,
    onehot,
    acc,
    part,
    part_in,
    edge,
    edge_in,
    beside,
    result,
    back,
    load_sems,
    slot_send,
    slot_recv,
    block_send,
    block_recv,
    meta_send,
    meta_recv,
    core_send,
    core_recv,
    back_send,
    back_recv,
):
    hi, rep, lo = sizes
    bf16, f32 = jnp.bfloat16, jnp.float32
    h, r, l = (lax.axis_index(name) for name in WORLD)
    me = h * lo + l
    group = hi * lo
    members, points = slot_rows.shape
    modes, columns = src.shape
    slot_count = owner.shape[0]
    fields = columns // members
    ty = members // TX
    width = slot_count * members
    strip = gy * members
    half = hi * strip

    y, x = h // 2, h % 2
    flip_x = y * 2 + (1 - x)
    flip_y = (1 - y) * 2 + x
    flip_xy = (1 - y) * 2 + (1 - x)
    near = [h, flip_x, flip_y, flip_xy]
    core = (h, 1 - r, l)

    barrier = pltpu.get_barrier_semaphore()
    for o in offsets((hi, 1, lo)):
        pl.semaphore_signal(
            barrier, inc=1, device_id=peer_at((hi, 1, lo), o), device_id_type=MESH
        )
    pl.semaphore_signal(barrier, inc=1, device_id=core, device_id_type=MESH)

    loads = []
    for k, (a, b) in enumerate(
        [
            (src, coef),
            (slot_rows, slot_in),
            (vander_hbm, vander),
            (test_hbm, test_fn),
            (inv_hbm, inv),
            (trace_hbm, trace),
            (lift_hbm, lift),
        ]
    ):
        copy = pltpu.make_async_copy(a, b, load_sems.at[k])
        copy.start()
        loads.append(copy)

    loads[1].wait()
    slots[me] = slot_in[...].astype(f32).astype(bf16)
    pl.semaphore_wait(barrier, group)

    sent = []

    def slot_copy(at, k, to):
        return pltpu.make_async_remote_copy(
            src_ref=slots.at[at],
            dst_ref=slots.at[at],
            send_sem=slot_send.at[k],
            recv_sem=slot_recv.at[at],
            device_id=to,
            device_id_type=MESH,
        )

    def send_slot(at, to):
        copy = slot_copy(at, len(sent), to)
        sent.append((copy, None))
        copy.start()

    def wait_slot(at):
        slot_copy(at, 0, core).wait_recv()

    partner = l + 1 - 2 * (l % 2)
    lower = l < 2
    near_z = jnp.where(lower, 2, 1)
    far_z = jnp.where(lower, 3, 0)
    inner = (l == 1) | (l == 2)
    outer = jnp.where(lower, 0, 3)
    line = [l, partner, near_z, far_z]

    send_slot(me, (h, r, near_z))
    send_slot(me, (h, r, partner))
    for to_h in near[1:]:
        send_slot(me, (to_h, r, l))

    others = []

    def send_block(k, c):
        to_h, to_l = near[k], line[c]
        copy = pltpu.make_async_remote_copy(
            src_ref=blocks.at[to_h * lo + to_l],
            dst_ref=mine.at[me],
            send_sem=block_send.at[k * lo + c],
            recv_sem=block_recv.at[me],
            device_id=(to_h, r, to_l),
            device_id_type=MESH,
        )
        copy.start()
        others.append(copy)

    meta[...] = jnp.zeros_like(meta)
    meta[0:slot_count, 0:members] = (owner[...] * members + local_id[...]).astype(f32)
    meta[slot_count : slot_count + 1, 0:members] = jac[...]
    packed = meta[...]
    row = lax.broadcasted_iota(jnp.int32, packed.shape, 0)
    lane = lax.broadcasted_iota(jnp.int32, packed.shape, 1)
    ids = jnp.zeros_like(packed)
    for s in range(slot_count):
        turned = pltpu.roll(packed, s * members, 1) if s else packed
        ids = jnp.where((row == s) & (lane // members == s), turned, ids)
    ids = jnp.sum(ids, axis=0, keepdims=True)
    jacs = jnp.zeros_like(packed)
    for c in range(lo):
        turned = pltpu.roll(packed, c * members, 1) if c else packed
        here = (row == slot_count) & (lane // members == c) & (lane // members == l)
        jacs = jnp.where(here, turned, jacs)
    jacs = jnp.sum(jacs, axis=0, keepdims=True)
    packed = jnp.where(row == 0, ids, jnp.where(row == 1, jacs, 0.0))
    meta[...] = packed
    metas[me] = packed

    for k, to_h in enumerate(near):
        for c in range(1 if k == 0 else 0, lo):
            to_l = (l + c) % lo
            copy = pltpu.make_async_remote_copy(
                src_ref=meta,
                dst_ref=metas.at[me],
                send_sem=meta_send.at[k * lo + c],
                recv_sem=meta_recv.at[me],
                device_id=(to_h, r, to_l),
                device_id_type=MESH,
            )
            copy.start()
            others.append(copy)

    loads[0].wait()
    rows = lo * members
    r_iota = lax.broadcasted_iota(jnp.int32, (rows, columns), 0)
    c_iota = lax.broadcasted_iota(jnp.int32, (rows, columns), 1)
    r_iota = (r_iota % members) * fields + r_iota // members
    for k in (1, 2, 3, 0):
        first = near[k] * lo
        perm = (r_iota + first == c_iota).astype(f32).astype(bf16)
        moved = nt(perm, coef[...]).astype(bf16)
        blocks[pl.ds(first, lo)] = moved.reshape(lo, members, modes)
        if k:
            send_block(k, 0)
    mine[me] = blocks[me]


    for k in (0, 3, 1, 2):
        send_block(k, 2)
    for k in (0, 3, 1, 2):
        send_block(k, 3)
    at = h * lo + line[2]
    wait_slot(at)
    copy = slot_copy(at, len(sent), (h, r, outer))
    sent.append((copy, inner))
    pl.when(inner)(copy.start)
    send_slot(at, (near[3], r, l))
    send_slot(at, (near[1], r, l))
    send_slot(at, (near[2], r, l))
    at = h * lo + line[3]
    wait_slot(at)
    copy = slot_copy(at, len(sent), (h, r, outer))
    sent.append((copy, inner))
    pl.when(inner)(copy.start)
    send_slot(at, (near[3], r, l))
    send_slot(at, (near[1], r, l))
    send_slot(at, (near[2], r, l))
    at = h * lo + line[1]
    wait_slot(at)
    send_slot(at, (near[3], r, l))
    send_slot(at, (near[1], r, l))
    send_slot(at, (near[2], r, l))
    for k in (0, 3, 1, 2):
        send_block(k, 1)

    def wait_block(at):
        pltpu.make_async_remote_copy(
            src_ref=mine.at[at],
            dst_ref=mine.at[at],
            send_sem=block_send.at[0],
            recv_sem=block_recv.at[at],
            device_id=core,
            device_id_type=MESH,
        ).wait_recv()
        pltpu.make_async_remote_copy(
            src_ref=metas.at[at],
            dst_ref=metas.at[at],
            send_sem=meta_send.at[0],
            recv_sem=meta_recv.at[at],
            device_id=core,
            device_id_type=MESH,
        ).wait_recv()

    for copy in loads[2:]:
        copy.wait()
    high, low = split(inv[...])
    inv_hi[...] = high
    inv_lo[...] = low
    traced = nn3(inv[...], trace[...])
    pts = trace.shape[1] // 4
    table[:, : 4 * pts] = traced.astype(bf16)
    face = lax.broadcasted_iota(jnp.int32, traced.shape, 1) // pts
    swapped = jnp.where(
        face % 2 == 0, pltpu.roll(traced, 3 * pts, 1), pltpu.roll(traced, pts, 1)
    )
    table[:, 4 * pts :] = swapped.astype(bf16)
    lift_inv[...] = nn3(lift[...], inv[...]).astype(bf16)

    place = lax.broadcasted_iota(jnp.int32, (half, width), 0)
    place = (place // strip) * (2 * strip) + place % strip

    def gather(places):
        source = jnp.concatenate([mine[at] for at in places], axis=0)
        values = nt(source, vander[...]).astype(bf16)
        parts = []
        for c, at in enumerate(places):
            where = slots[at]
            value = values[c * members : (c + 1) * members]
            for s in range(slot_count):
                parts.append(jnp.where(where == bf16(s), value, bf16(0)))
        pieces = nn(jnp.concatenate(parts, axis=0), test_fn[...]).astype(bf16)
        for side in range(2):
            shift = (1 - r if side == 0 else r) * strip
            for c, at in enumerate(places):
                targets = (metas[at][0:1, :]).astype(jnp.int32) - shift
                onehot[side, :, c * width : (c + 1) * width] = (
                    jnp.where(place == targets, 1.0, 0.0).astype(bf16)
                )
        return pieces

    def scatter(pieces, side, first):
        summed = nn(onehot[side], pieces)
        return summed if first else acc[side] + summed

    for k, c in enumerate((0, 2, 3, 1)):
        z = line[c]
        places = [at * lo + z for at in near]
        for at in places[1:]:
            wait_slot(at)
        for at in places[0 if k else 1 :]:
            wait_block(at)
        pieces = gather(places)
        if k < lo - 1:
            for side in range(2):
                acc[side] = scatter(pieces, side, k == 0)

    def core_copy(a, b, k):
        return pltpu.make_async_remote_copy(
            src_ref=a,
            dst_ref=b,
            send_sem=core_send.at[k],
            recv_sem=core_recv.at[k],
            device_id=core,
            device_id_type=MESH,
        )

    theirs = scatter(pieces, 0, False).astype(bf16)
    part[...] = theirs
    part_copy = core_copy(part, part_in, 0)
    part_copy.start()
    ours = scatter(pieces, 1, False)
    acc[1] = ours
    swap = table[:, 4 * pts :]
    seen = nn(ours.astype(bf16), swap)
    eye_r = lax.broadcasted_iota(jnp.int32, (strip, strip), 0)
    eye_c = lax.broadcasted_iota(jnp.int32, (strip, strip), 1)
    lanes = lax.broadcasted_iota(jnp.int32, (strip, 4 * pts), 1)
    inverse = []
    for k in range(hi):
        jac_row = metas[k * lo][1:2, :]
        for c in range(1, lo):
            jac_row = jac_row + metas[k * lo + c][1:2, :]
        column = jnp.sum(jnp.where(eye_r == eye_c, jac_row, 0.0), axis=1, keepdims=True)
        column = 1.0 / column
        inverse.append(column)
        edge[k * strip : (k + 1) * strip, :] = jnp.where(
            lanes == 4 * pts - 1, column, seen[k * strip : (k + 1) * strip]
        )
    edge_copy = core_copy(edge, edge_in, 1)
    edge_copy.start()
    seen = nn(theirs, swap)
    beside[0:strip, :] = jnp.zeros((strip, 4 * pts), f32)
    beside[(hi + 1) * strip :, :] = jnp.zeros((strip, 4 * pts), f32)
    part_copy.wait_recv()
    edge_copy.wait_recv()
    for k in range(hi):
        got = edge_in[k * strip : (k + 1) * strip, :]
        column = got[:, 4 * pts - 1 : 4 * pts]
        beside[(k + 1) * strip : (k + 2) * strip, :] = (
            seen[k * strip : (k + 1) * strip] + got
        ) * column

    speed = speeds[me]
    t_row = lax.broadcasted_iota(jnp.int32, (strip, 4 * pts), 0)
    d_row, a_row, b_row = t_row // members, (t_row % members) // ty, t_row % ty
    face = lanes // pts
    moved = lambda v, n: pltpu.roll(v, n % strip, 0)
    for k in range(hi):
        own = slice(k * strip, (k + 1) * strip)
        moments = acc[1, own, :] + part_in[own, :].astype(f32)
        m_hi, m_lo = split(moments)
        both = nn(m_hi, table[...]) * inverse[k]
        mine_t, cur = both[:, : 4 * pts], both[:, 4 * pts :]
        prev = beside[pl.ds(pl.multiple_of((k + r) * strip, strip), strip), :]
        after = beside[pl.ds(pl.multiple_of((k + r + 1) * strip, strip), strip), :]
        last = (TX - 1) * ty
        west = jnp.where(a_row > 0, moved(cur, ty), moved(prev, -last))
        east = jnp.where(a_row < TX - 1, moved(cur, -ty), moved(after, last))
        jump = members - (ty - 1)
        south = jnp.where(b_row > 0, moved(cur, 1), moved(cur, jump))
        south = jnp.where((b_row == 0) & (d_row == 0), 0.0, south)
        north = jnp.where(b_row < ty - 1, moved(cur, -1), moved(cur, -jump))
        north = jnp.where((b_row == ty - 1) & (d_row == gy - 1), 0.0, north)
        other = jnp.where(
            face < 2, jnp.where(face == 0, west, east), jnp.where(face == 2, south, north)
        )
        jumps = ((other - mine_t) * speed).astype(bf16)
        solved = nn(m_hi, inv_hi[...]) + nn(m_lo, inv_hi[...]) + nn(m_hi, inv_lo[...])
        solved = (solved + nn(jumps, lift_inv[...])) * inverse[k]
        result[k * lo : (k + 1) * lo] = solved.astype(bf16).reshape(lo, members, modes)
        for c in range(lo):
            to_l = (l + c) % lo

            def back_copy():
                return pltpu.make_async_remote_copy(
                    src_ref=result.at[k * lo + to_l],
                    dst_ref=back.at[me],
                    send_sem=back_send.at[k * lo + c],
                    recv_sem=back_recv.at[me],
                    device_id=(k, r, to_l),
                    device_id_type=MESH,
                )

            if c == 0:
                pl.when(h != k)(lambda: back_copy().start())
            else:
                back_copy().start()
    back[me] = result[me]

    for copy, when in sent:
        if when is None:
            copy.wait_send()
        else:
            pl.when(when)(copy.wait_send)
    for copy in others + [part_copy, edge_copy]:
        copy.wait_send()
    for k in range(hi):
        for c in range(lo):

            def leave_wait():
                pltpu.make_async_remote_copy(
                    src_ref=result.at[k * lo],
                    dst_ref=back.at[me],
                    send_sem=back_send.at[k * lo + c],
                    recv_sem=back_recv.at[me],
                    device_id=core,
                    device_id_type=MESH,
                ).wait_send()

            if c == 0:
                pl.when(h != k)(leave_wait)
            else:
                leave_wait()

    for at in range(group):

        @pl.when(me != at)
        def _():
            pltpu.make_async_remote_copy(
                src_ref=back.at[at],
                dst_ref=back.at[at],
                send_sem=back_send.at[0],
                recv_sem=back_recv.at[at],
                device_id=core,
                device_id_type=MESH,
            ).wait_recv()

    for at in range(group):
        out[:, at, :] = back[at].astype(f32)


def fused(sizes, gy, *args):
    src, slot_rows, owner, _, _, vander, test_fn, inv, trace, lift, speeds = args
    hi, rep, lo = sizes
    members, points = slot_rows.shape
    modes, columns = src.shape
    slot_count = owner.shape[0]
    group = hi * lo
    strip = gy * members
    half = hi * strip
    faces = trace.shape[1]
    width = slot_count * members
    bf16, f32 = jnp.bfloat16, jnp.float32
    any_, vmem = pl.BlockSpec(memory_space=pl.ANY), pl.BlockSpec(memory_space=pltpu.VMEM)
    smem = pl.BlockSpec(memory_space=pltpu.SMEM)
    dma = pltpu.SemaphoreType.DMA
    like = lambda a: pltpu.VMEM(a.shape, a.dtype)
    slot_sends = 8 + lo * 5
    return pl.pallas_call(
        functools.partial(fused_kernel, sizes, gy),
        out_shape=pltpu.VMEM((members, columns // members, modes), f32),
        in_specs=[any_, any_, vmem, vmem, vmem, any_, any_, any_, any_, any_, smem],
        out_specs=vmem,
        scratch_shapes=[
            like(src),
            like(slot_rows),
            like(vander),
            like(test_fn),
            like(inv),
            like(trace),
            like(lift),
            pltpu.VMEM(inv.shape, bf16),
            pltpu.VMEM(inv.shape, bf16),
            pltpu.VMEM((modes, 2 * faces), bf16),
            pltpu.VMEM(lift.shape, bf16),
            pltpu.VMEM((group, members, modes), bf16),
            pltpu.VMEM((group, members, modes), bf16),
            pltpu.VMEM((group, members, points), bf16),
            pltpu.VMEM((8, width), f32),
            pltpu.VMEM((group, 8, width), f32),
            pltpu.VMEM((2, half, hi * width), bf16),
            pltpu.VMEM((2, half, modes), f32),
            pltpu.VMEM((half, modes), bf16),
            pltpu.VMEM((half, modes), bf16),
            pltpu.VMEM((half, faces), f32),
            pltpu.VMEM((half, faces), f32),
            pltpu.VMEM((half + 2 * strip, faces), f32),
            pltpu.VMEM((group, members, modes), bf16),
            pltpu.VMEM((group, members, modes), bf16),
            dma((7,)),
            dma((slot_sends,)),
            dma((group,)),
            dma((group,)),
            dma((group,)),
            dma((group,)),
            dma((group,)),
            dma((2,)),
            dma((2,)),
            dma((group,)),
            dma((group,)),
        ],
        compiler_params=pltpu.CompilerParams(
            collective_id=2, has_side_effects=True, vmem_limit_bytes=56 << 20
        ),
        name="remap",
    )(*args)


def fused_device(sizes, gy, src_coef, point_slot, tgt_owner, tgt_local, vander, test_fn, inv_mass, jacobian, trace_tab, lift_tab, wave_speed):
    return fused(
        sizes,
        gy,
        src_coef,
        point_slot.T,
        tgt_owner.T,
        tgt_local.T,
        jacobian[None, :],
        vander,
        test_fn,
        inv_mass,
        trace_tab,
        lift_tab,
        wave_speed,
    )


def solution(mesh):
    gx, gy = mesh.shape["gx"], mesh.shape["gy"]
    devices = gx * gy

    def call(*args):
        fields = args[-1].shape[0]
        sizes = (fields // gy, devices // fields, gy)
        body = functools.partial(per_device, gx, gy)
        if sizes == (4, 2, 4):
            body = functools.partial(fused_device, sizes, gy)
        return jax.shard_map(
            body,
            mesh=Mesh(mesh.devices.reshape(sizes), WORLD),
            in_specs=(
                P(None, WORLD),
                P(None, WORLD),
                P(WORLD, None),
                P(WORLD, None),
                P(),
                P(),
                P(),
                P(WORLD),
                P(),
                P(),
                P(),
            ),
            out_specs=P(WORLD, None, None),
            check_vma=False,
        )(*args)

    return call
```

```python
import functools

import jax
import jax.numpy as jnp
from jax import lax
from jax.experimental import pallas as pl
from jax.experimental.pallas import tpu as pltpu
from jax.sharding import Mesh, PartitionSpec as P

TX = 8
MESH = pl.DeviceIdType.MESH
GROUP = ("hi", "lo")
WORLD = ("hi", "rep", "lo")


def dot(a, b, dims, precision=None):
    return lax.dot_general(
        a, b, (dims, ((), ())), precision=precision, preferred_element_type=jnp.float32
    )


def neighbour_traces(traces, gx, gy, tx, ty):
    face_cols = traces.shape[1]
    pts = face_cols // 4
    grid = traces.reshape(gx, gy, tx, ty, face_cols).transpose(0, 2, 1, 3, 4)
    grid = grid.reshape(gx * tx, gy * ty, face_cols)
    face = lambda k: grid[:, :, k * pts : (k + 1) * pts]
    west = jnp.pad(face(1)[:-1], ((1, 0), (0, 0), (0, 0)))
    east = jnp.pad(face(0)[1:], ((0, 1), (0, 0), (0, 0)))
    south = jnp.pad(face(3)[:, :-1], ((0, 0), (1, 0), (0, 0)))
    north = jnp.pad(face(2)[:, 1:], ((0, 0), (0, 1), (0, 0)))
    joined = jnp.concatenate([west, east, south, north], axis=2) - grid
    joined = joined.reshape(gx, tx, gy, ty, face_cols).transpose(0, 2, 1, 3, 4)
    return joined.reshape(gx * gy * tx * ty, face_cols)


def peer_at(sizes, offset):
    return tuple(
        lax.rem(lax.axis_index(name) + step, size) if step else lax.axis_index(name)
        for name, size, step in zip(WORLD, sizes, offset)
    )


def offsets(sizes):
    hi, rep, lo = sizes
    every = [(a, b, c) for a in range(hi) for b in range(rep) for c in range(lo)]
    return every[1:]


def greet(peers):
    barrier = pltpu.get_barrier_semaphore()
    for peer in peers:
        pl.semaphore_signal(barrier, inc=1, device_id=peer, device_id_type=MESH)
    pl.semaphore_wait(barrier, len(peers))


def push(src, dst, send, recv, peer):
    copy = pltpu.make_async_remote_copy(
        src_ref=src, dst_ref=dst, send_sem=send, recv_sem=recv, device_id=peer, device_id_type=MESH
    )
    copy.start()
    return copy


def enter_kernel(
    sizes,
    blocks,
    slot_rows,
    meta,
    vander,
    test_fn,
    part,
    metas,
    mine,
    slots,
    onehot,
    pieces,
    block_sems,
    slot_sems,
    relay_sems,
    meta_sems,
    local_sems,
):
    hi, rep, lo = sizes
    h, r, l = (lax.axis_index(name) for name in WORLD)
    me = h * lo + l
    device = (h * rep + r) * lo + l
    everyone = offsets(sizes)
    group = [o for o in everyone if o[1] == 0]
    local = [
        pltpu.make_async_copy(slot_rows, slots.at[me], local_sems.at[0]),
        pltpu.make_async_copy(blocks.at[me], mine.at[me], local_sems.at[1]),
        pltpu.make_async_copy(meta, metas.at[device], local_sems.at[2]),
    ]
    for copy in local:
        copy.start()
    greet([peer_at(sizes, o) for o in everyone])

    along, relays = [], []
    for c in range(1, lo):
        peer = peer_at(sizes, (0, 0, c))
        along.append(
            push(slot_rows, slots.at[me], slot_sems.at[0, c], slot_sems.at[1, c], peer)
        )
    for a in range(1, hi):
        peer = peer_at(sizes, (a, 0, 0))
        k = a * lo
        relays.append(
            push(slot_rows, slots.at[me], relay_sems.at[0, k], relay_sems.at[1, k], peer)
        )
    arrive, labels = [], []
    for k, o in enumerate(group):
        to_h, _, to_l = peer = peer_at(sizes, o)
        arrive.append(
            push(
                blocks.at[to_h * lo + to_l],
                mine.at[me],
                block_sems.at[0, k],
                block_sems.at[1, k],
                peer,
            )
        )
    for k, o in enumerate(everyone):
        labels.append(
            push(
                meta, metas.at[device], meta_sems.at[0, k], meta_sems.at[1, k], peer_at(sizes, o)
            )
        )
    for c in range(1, lo):
        along[c - 1].wait_recv()
        place = h * lo + lax.rem(l + lo - c, lo)
        for a in range(1, hi):
            k = a * lo + c
            relays.append(
                push(
                    slots.at[place],
                    slots.at[place],
                    relay_sems.at[0, k],
                    relay_sems.at[1, k],
                    peer_at(sizes, (a, 0, 0)),
                )
            )
    for copy in local:
        copy.wait()
    for copy in labels:
        copy.wait_recv()

    width = meta.shape[1]
    rows = 128

    @pl.loop(0, part.shape[0] // rows)
    def _(i):
        start = pl.multiple_of(i * rows, rows)
        target = (lax.broadcasted_iota(jnp.int32, (rows, width), 0) + start).astype(jnp.float32)
        for g in range(hi * lo):
            ids = metas[(g // lo * rep + r) * lo + g % lo][0:1, :]
            onehot[pl.ds(start, rows), g * width : (g + 1) * width] = jnp.where(
                target == ids, 1.0, 0.0
            ).astype(onehot.dtype)

    members = slot_rows.shape[0]
    slot_count = width // members
    for a in range(hi):
        for c in range(lo):
            if a or c:
                arrive[a * lo + c - 1].wait_recv()
            if a:
                relays[(a - 1) if c == 0 else (hi - 1) * c + a - 1].wait_recv()
        from_h = lax.rem(h + hi - a, hi)
        first = from_h * lo
        source = mine[pl.ds(first, lo)].reshape(lo * members, -1)
        values = dot(source, vander[...], ((1,), (1,)))
        parts = []
        for c in range(lo):
            where = slots[first + c].astype(jnp.float32)
            value = values[c * members : (c + 1) * members]
            for s in range(slot_count):
                parts.append(jnp.where(where == s, value, 0.0).astype(jnp.bfloat16))
        masked = jnp.concatenate(parts, axis=0)
        pieces[from_h] = dot(masked, test_fn[...], ((1,), (0,))).astype(jnp.bfloat16)

    every = pieces.shape[0] * pieces.shape[1]
    block = 256

    @pl.loop(0, part.shape[0] // block)
    def _(i):
        start = pl.multiple_of(i * block, block)
        summed = dot(
            onehot[pl.ds(start, block), :], pieces[...].reshape(every, -1), ((1,), (0,))
        )
        part[pl.ds(start, block), :] = summed.astype(part.dtype)

    for copy in along + relays + arrive + labels:
        copy.wait_send()


def enter(sizes, blocks, slot_rows, meta, vander, test_fn):
    hi, rep, lo = sizes
    world = hi * rep * lo
    _, members, modes = blocks.shape
    vmem = pl.BlockSpec(memory_space=pltpu.VMEM)
    dma = pltpu.SemaphoreType.DMA
    return pl.pallas_call(
        functools.partial(enter_kernel, sizes),
        out_shape=(
            jax.ShapeDtypeStruct((world * members, modes), jnp.bfloat16),
            jax.ShapeDtypeStruct((world, *meta.shape), meta.dtype),
        ),
        in_specs=[vmem] * 5,
        out_specs=(vmem,) * 2,
        scratch_shapes=[
            pltpu.VMEM(blocks.shape, blocks.dtype),
            pltpu.VMEM((hi * lo, *slot_rows.shape), slot_rows.dtype),
            pltpu.VMEM((world * members, hi * lo * meta.shape[1]), jnp.bfloat16),
            pltpu.VMEM((hi, lo * meta.shape[1], modes), jnp.bfloat16),
            dma((2, hi * lo)),
            dma((2, lo)),
            dma((2, hi * lo)),
            dma((2, world)),
            dma((3,)),
        ],
        compiler_params=pltpu.CompilerParams(
            collective_id=0, has_side_effects=True, vmem_limit_bytes=44 << 20
        ),
        name="enter",
    )(blocks, slot_rows, meta, vander, test_fn)


def leave_kernel(sizes, blocks, mine, sems, local_sem):
    hi, rep, lo = sizes
    me = lax.axis_index("hi") * lo + lax.axis_index("lo")
    group = [o for o in offsets(sizes) if o[1] == 0]
    local = pltpu.make_async_copy(blocks.at[me], mine.at[me], local_sem)
    local.start()
    greet([peer_at(sizes, o) for o in group])
    copies = []
    for k, o in enumerate(group):
        to_h, _, to_l = peer = peer_at(sizes, o)
        copies.append(
            push(blocks.at[to_h * lo + to_l], mine.at[me], sems.at[0, k], sems.at[1, k], peer)
        )
    for copy in copies:
        copy.wait()
    local.wait()


def leave(sizes, blocks):
    vmem = pl.BlockSpec(memory_space=pltpu.VMEM)
    dma = pltpu.SemaphoreType.DMA
    return pl.pallas_call(
        functools.partial(leave_kernel, sizes),
        out_shape=jax.ShapeDtypeStruct(blocks.shape, blocks.dtype),
        in_specs=[vmem],
        out_specs=vmem,
        scratch_shapes=[dma((2, sizes[0] * sizes[2])), dma],
        compiler_params=pltpu.CompilerParams(
            collective_id=1, has_side_effects=True, vmem_limit_bytes=8 << 20
        ),
        name="leave",
    )(blocks)


def per_device(
    gx,
    gy,
    src_coef,
    point_slot,
    tgt_owner,
    tgt_local,
    vander,
    test_fn,
    inv_mass,
    jacobian,
    trace_tab,
    lift_tab,
    wave_speed,
):
    bf16 = jnp.bfloat16
    high = lax.Precision.HIGH
    modes, columns = src_coef.shape
    members = point_slot.shape[1]
    fields = wave_speed.shape[0]
    reps = lax.axis_size("rep")
    my_rep = lax.axis_index("rep")
    my_field = lax.axis_index("hi") * lax.axis_size("lo") + lax.axis_index("lo")

    row = jnp.arange(columns, dtype=jnp.int32)
    wanted = (row % members) * fields + row // members
    perm = (wanted[:, None] == row[None, :]).astype(bf16)
    by_field = dot(perm, src_coef, ((1,), (1,))).astype(bf16)
    sizes = tuple(lax.axis_size(name) for name in WORLD)
    holders = sizes[0] * sizes[2]
    ids = (tgt_owner * members + tgt_local).T.reshape(1, -1).astype(jnp.float32)
    jac = jnp.pad(jacobian[None, :], ((0, 0), (0, ids.shape[1] - members)))
    meta = jnp.pad(jnp.concatenate([ids, jac], axis=0), ((0, 6), (0, 0)))
    part, metas = enter(
        sizes,
        by_field.reshape(holders, members, modes),
        point_slot.T.astype(bf16),
        meta,
        vander,
        test_fn,
    )
    jac = metas[:, 1, :members].reshape(-1, 1)
    if reps == 2:
        other = lax.ppermute(part, "rep", [(0, 1), (1, 0)])
        moments = part.astype(jnp.float32) + other.astype(jnp.float32)
    else:
        moments = lax.psum(part.astype(jnp.float32), "rep")

    coeffs = dot(moments, inv_mass, ((1,), (0,)), high) / jac
    traces = dot(coeffs, trace_tab, ((1,), (0,)), high)
    jumps = neighbour_traces(traces, gx, gy, TX, members // TX)
    own = lambda x: lax.dynamic_index_in_dim(
        x.reshape(-1, reps, gy * members, x.shape[-1]), my_rep, 1, keepdims=False
    ).reshape(-1, x.shape[-1])
    lift = dot(lift_tab, inv_mass, ((1,), (0,)), high)
    speed = lax.dynamic_index_in_dim(wave_speed, my_field, 0, keepdims=False)
    update = dot(own(jumps), lift, ((1,), (0,)), high) * (speed / own(jac))
    result = (own(coeffs) + update).astype(bf16)
    back = leave(sizes, result.reshape(holders, members, modes))
    back = back.transpose(1, 0, 2)
    return back.astype(jnp.float32)


def nt(a, b):
    return dot(a, b, ((1,), (1,)))


def nn(a, b):
    return dot(a, b, ((1,), (0,)))


def split(x):
    high = x.astype(jnp.bfloat16)
    return high, (x - high.astype(jnp.float32)).astype(jnp.bfloat16)


def nn3(a, b):
    (ah, al), (bh, bl) = split(a), split(b)
    return nn(ah, bh) + nn(al, bh) + nn(ah, bl)


def fused_kernel(
    sizes,
    gy,
    src,
    slot_rows,
    owner,
    local_id,
    jac,
    vander_hbm,
    test_hbm,
    inv_hbm,
    trace_hbm,
    lift_hbm,
    speeds,
    out,
    coef,
    slot_in,
    vander,
    test_fn,
    inv,
    trace,
    lift,
    inv_hi,
    inv_lo,
    table,
    lift_inv,
    blocks,
    mine,
    slots,
    meta,
    metas,
    onehot,
    acc,
    part,
    part_in,
    edge,
    edge_in,
    beside,
    result,
    back,
    load_sems,
    slot_send,
    slot_recv,
    block_send,
    block_recv,
    meta_send,
    meta_recv,
    core_send,
    core_recv,
    back_send,
    back_recv,
):
    hi, rep, lo = sizes
    bf16, f32 = jnp.bfloat16, jnp.float32
    h, r, l = (lax.axis_index(name) for name in WORLD)
    me = h * lo + l
    group = hi * lo
    members, points = slot_rows.shape
    modes, columns = src.shape
    slot_count = owner.shape[0]
    fields = columns // members
    ty = members // TX
    width = slot_count * members
    strip = gy * members
    half = hi * strip

    y, x = h // 2, h % 2
    flip_x = y * 2 + (1 - x)
    flip_y = (1 - y) * 2 + x
    flip_xy = (1 - y) * 2 + (1 - x)
    near = [h, flip_x, flip_y, flip_xy]
    core = (h, 1 - r, l)

    barrier = pltpu.get_barrier_semaphore()
    for o in offsets((hi, 1, lo)):
        pl.semaphore_signal(
            barrier, inc=1, device_id=peer_at((hi, 1, lo), o), device_id_type=MESH
        )
    pl.semaphore_signal(barrier, inc=1, device_id=core, device_id_type=MESH)

    loads = []
    for k, (a, b) in enumerate(
        [
            (src, coef),
            (slot_rows, slot_in),
            (vander_hbm, vander),
            (test_hbm, test_fn),
            (inv_hbm, inv),
            (trace_hbm, trace),
            (lift_hbm, lift),
        ]
    ):
        copy = pltpu.make_async_copy(a, b, load_sems.at[k])
        copy.start()
        loads.append(copy)

    loads[1].wait()
    slots[me] = slot_in[...].astype(f32).astype(bf16)
    pl.semaphore_wait(barrier, group)

    sent = []

    def slot_copy(at, k, to):
        return pltpu.make_async_remote_copy(
            src_ref=slots.at[at],
            dst_ref=slots.at[at],
            send_sem=slot_send.at[k],
            recv_sem=slot_recv.at[at],
            device_id=to,
            device_id_type=MESH,
        )

    def send_slot(at, to):
        copy = slot_copy(at, len(sent), to)
        sent.append((copy, None))
        copy.start()

    def wait_slot(at):
        slot_copy(at, 0, core).wait_recv()

    partner = l + 1 - 2 * (l % 2)
    lower = l < 2
    near_z = jnp.where(lower, 2, 1)
    far_z = jnp.where(lower, 3, 0)
    inner = (l == 1) | (l == 2)
    outer = jnp.where(lower, 0, 3)
    line = [l, partner, near_z, far_z]

    send_slot(me, (h, r, near_z))
    send_slot(me, (h, r, partner))
    for to_h in near[1:]:
        send_slot(me, (to_h, r, l))

    others = []

    def send_block(k, c):
        to_h, to_l = near[k], line[c]
        copy = pltpu.make_async_remote_copy(
            src_ref=blocks.at[to_h * lo + to_l],
            dst_ref=mine.at[me],
            send_sem=block_send.at[k * lo + c],
            recv_sem=block_recv.at[me],
            device_id=(to_h, r, to_l),
            device_id_type=MESH,
        )
        copy.start()
        others.append(copy)

    meta[...] = jnp.zeros_like(meta)
    meta[0:slot_count, 0:members] = (owner[...] * members + local_id[...]).astype(f32)
    meta[slot_count : slot_count + 1, 0:members] = jac[...]
    packed = meta[...]
    row = lax.broadcasted_iota(jnp.int32, packed.shape, 0)
    lane = lax.broadcasted_iota(jnp.int32, packed.shape, 1)
    ids = jnp.zeros_like(packed)
    for s in range(slot_count):
        turned = pltpu.roll(packed, s * members, 1) if s else packed
        ids = jnp.where((row == s) & (lane // members == s), turned, ids)
    ids = jnp.sum(ids, axis=0, keepdims=True)
    jacs = jnp.zeros_like(packed)
    for c in range(lo):
        turned = pltpu.roll(packed, c * members, 1) if c else packed
        here = (row == slot_count) & (lane // members == c) & (lane // members == l)
        jacs = jnp.where(here, turned, jacs)
    jacs = jnp.sum(jacs, axis=0, keepdims=True)
    packed = jnp.where(row == 0, ids, jnp.where(row == 1, jacs, 0.0))
    meta[...] = packed
    metas[me] = packed

    for k, to_h in enumerate(near):
        for c in range(1 if k == 0 else 0, lo):
            to_l = (l + c) % lo
            copy = pltpu.make_async_remote_copy(
                src_ref=meta,
                dst_ref=metas.at[me],
                send_sem=meta_send.at[k * lo + c],
                recv_sem=meta_recv.at[me],
                device_id=(to_h, r, to_l),
                device_id_type=MESH,
            )
            copy.start()
            others.append(copy)

    loads[0].wait()
    rows = lo * members
    r_iota = lax.broadcasted_iota(jnp.int32, (rows, columns), 0)
    c_iota = lax.broadcasted_iota(jnp.int32, (rows, columns), 1)
    r_iota = (r_iota % members) * fields + r_iota // members
    for k in (1, 2, 3, 0):
        first = near[k] * lo
        perm = (r_iota + first == c_iota).astype(f32).astype(bf16)
        moved = nt(perm, coef[...]).astype(bf16)
        blocks[pl.ds(first, lo)] = moved.reshape(lo, members, modes)
        if k:
            send_block(k, 0)
    mine[me] = blocks[me]


    for k in (0, 3, 1, 2):
        send_block(k, 2)
    for k in (0, 3, 1, 2):
        send_block(k, 3)
    at = h * lo + line[2]
    wait_slot(at)
    copy = slot_copy(at, len(sent), (h, r, outer))
    sent.append((copy, inner))
    pl.when(inner)(copy.start)
    send_slot(at, (near[3], r, l))
    send_slot(at, (near[1], r, l))
    send_slot(at, (near[2], r, l))
    at = h * lo + line[3]
    wait_slot(at)
    copy = slot_copy(at, len(sent), (h, r, outer))
    sent.append((copy, inner))
    pl.when(inner)(copy.start)
    send_slot(at, (near[3], r, l))
    send_slot(at, (near[1], r, l))
    send_slot(at, (near[2], r, l))
    at = h * lo + line[1]
    wait_slot(at)
    send_slot(at, (near[3], r, l))
    send_slot(at, (near[1], r, l))
    send_slot(at, (near[2], r, l))
    for k in (0, 3, 1, 2):
        send_block(k, 1)

    def wait_block(at):
        pltpu.make_async_remote_copy(
            src_ref=mine.at[at],
            dst_ref=mine.at[at],
            send_sem=block_send.at[0],
            recv_sem=block_recv.at[at],
            device_id=core,
            device_id_type=MESH,
        ).wait_recv()

    def wait_meta(at):
        pltpu.make_async_remote_copy(
            src_ref=metas.at[at],
            dst_ref=metas.at[at],
            send_sem=meta_send.at[0],
            recv_sem=meta_recv.at[at],
            device_id=core,
            device_id_type=MESH,
        ).wait_recv()

    for copy in loads[2:]:
        copy.wait()
    high, low = split(inv[...])
    inv_hi[...] = high
    inv_lo[...] = low
    traced = nn3(inv[...], trace[...])
    pts = trace.shape[1] // 4
    table[:, : 4 * pts] = traced.astype(bf16)
    face = lax.broadcasted_iota(jnp.int32, traced.shape, 1) // pts
    swapped = jnp.where(
        face % 2 == 0, pltpu.roll(traced, 3 * pts, 1), pltpu.roll(traced, pts, 1)
    )
    table[:, 4 * pts :] = swapped.astype(bf16)
    lift_inv[...] = nn3(lift[...], inv[...]).astype(bf16)

    place = lax.broadcasted_iota(jnp.int32, (half, width), 0)
    place = (place // strip) * (2 * strip) + place % strip

    def gather(places):
        source = jnp.concatenate([mine[at] for at in places], axis=0)
        values = nt(source, vander[...]).astype(bf16)
        parts = []
        for c, at in enumerate(places):
            where = slots[at]
            value = values[c * members : (c + 1) * members]
            for s in range(slot_count):
                parts.append(jnp.where(where == bf16(s), value, bf16(0)))
        pieces = nn(jnp.concatenate(parts, axis=0), test_fn[...]).astype(bf16)
        for side in range(2):
            shift = (1 - r if side == 0 else r) * strip
            for c, at in enumerate(places):
                targets = (metas[at][0:1, :]).astype(jnp.int32) - shift
                onehot[side, :, c * width : (c + 1) * width] = (
                    jnp.where(place == targets, 1.0, 0.0).astype(bf16)
                )
        return pieces

    def scatter(pieces, side, first):
        summed = nn(onehot[side], pieces)
        return summed if first else acc[side] + summed

    for k, z in enumerate(line):
        for at_h in near[0 if k else 1 :]:
            wait_meta(at_h * lo + z)
    for k, c in enumerate((0, 2, 3, 1)):
        z = line[c]
        places = [at * lo + z for at in near]
        for at in places[1:]:
            wait_slot(at)
        for at in places[0 if k else 1 :]:
            wait_block(at)
        pieces = gather(places)
        if k < lo - 1:
            for side in range(2):
                acc[side] = scatter(pieces, side, k == 0)

    def core_copy(a, b, k):
        return pltpu.make_async_remote_copy(
            src_ref=a,
            dst_ref=b,
            send_sem=core_send.at[k],
            recv_sem=core_recv.at[k],
            device_id=core,
            device_id_type=MESH,
        )

    theirs = scatter(pieces, 0, False).astype(bf16)
    part[...] = theirs
    part_copy = core_copy(part, part_in, 0)
    part_copy.start()
    ours = scatter(pieces, 1, False)
    acc[1] = ours
    swap = table[:, 4 * pts :]
    seen = nn(ours.astype(bf16), swap)
    eye_r = lax.broadcasted_iota(jnp.int32, (strip, strip), 0)
    eye_c = lax.broadcasted_iota(jnp.int32, (strip, strip), 1)
    lanes = lax.broadcasted_iota(jnp.int32, (strip, 4 * pts), 1)
    inverse = []
    for k in range(hi):
        jac_row = metas[k * lo][1:2, :]
        for c in range(1, lo):
            jac_row = jac_row + metas[k * lo + c][1:2, :]
        column = jnp.sum(jnp.where(eye_r == eye_c, jac_row, 0.0), axis=1, keepdims=True)
        column = 1.0 / column
        inverse.append(column)
        edge[k * strip : (k + 1) * strip, :] = jnp.where(
            lanes == 4 * pts - 1, column, seen[k * strip : (k + 1) * strip]
        )
    edge_copy = core_copy(edge, edge_in, 1)
    edge_copy.start()
    seen = nn(theirs, swap)
    beside[0:strip, :] = jnp.zeros((strip, 4 * pts), f32)
    beside[(hi + 1) * strip :, :] = jnp.zeros((strip, 4 * pts), f32)
    part_copy.wait_recv()
    edge_copy.wait_recv()
    for k in range(hi):
        got = edge_in[k * strip : (k + 1) * strip, :]
        column = got[:, 4 * pts - 1 : 4 * pts]
        beside[(k + 1) * strip : (k + 2) * strip, :] = (
            seen[k * strip : (k + 1) * strip] + got
        ) * column

    speed = speeds[me]
    t_row = lax.broadcasted_iota(jnp.int32, (strip, 4 * pts), 0)
    d_row, a_row, b_row = t_row // members, (t_row % members) // ty, t_row % ty
    face = lanes // pts
    moved = lambda v, n: pltpu.roll(v, n % strip, 0)
    for k in range(hi):
        own = slice(k * strip, (k + 1) * strip)
        moments = acc[1, own, :] + part_in[own, :].astype(f32)
        m_hi, m_lo = split(moments)
        both = nn(m_hi, table[...]) * inverse[k]
        mine_t, cur = both[:, : 4 * pts], both[:, 4 * pts :]
        prev = beside[pl.ds(pl.multiple_of((k + r) * strip, strip), strip), :]
        after = beside[pl.ds(pl.multiple_of((k + r + 1) * strip, strip), strip), :]
        last = (TX - 1) * ty
        west = jnp.where(a_row > 0, moved(cur, ty), moved(prev, -last))
        east = jnp.where(a_row < TX - 1, moved(cur, -ty), moved(after, last))
        jump = members - (ty - 1)
        south = jnp.where(b_row > 0, moved(cur, 1), moved(cur, jump))
        south = jnp.where((b_row == 0) & (d_row == 0), 0.0, south)
        north = jnp.where(b_row < ty - 1, moved(cur, -1), moved(cur, -jump))
        north = jnp.where((b_row == ty - 1) & (d_row == gy - 1), 0.0, north)
        other = jnp.where(
            face < 2, jnp.where(face == 0, west, east), jnp.where(face == 2, south, north)
        )
        jumps = ((other - mine_t) * speed).astype(bf16)
        solved = nn(m_hi, inv_hi[...]) + nn(m_lo, inv_hi[...]) + nn(m_hi, inv_lo[...])
        solved = (solved + nn(jumps, lift_inv[...])) * inverse[k]
        result[k * lo : (k + 1) * lo] = solved.astype(bf16).reshape(lo, members, modes)
        for c in range(lo):
            to_l = (l + c) % lo

            def back_copy():
                return pltpu.make_async_remote_copy(
                    src_ref=result.at[k * lo + to_l],
                    dst_ref=back.at[me],
                    send_sem=back_send.at[k * lo + c],
                    recv_sem=back_recv.at[me],
                    device_id=(k, r, to_l),
                    device_id_type=MESH,
                )

            if c == 0:
                pl.when(h != k)(lambda: back_copy().start())
            else:
                back_copy().start()
    back[me] = result[me]

    for copy, when in sent:
        if when is None:
            copy.wait_send()
        else:
            pl.when(when)(copy.wait_send)
    for copy in others + [part_copy, edge_copy]:
        copy.wait_send()
    for k in range(hi):
        for c in range(lo):

            def leave_wait():
                pltpu.make_async_remote_copy(
                    src_ref=result.at[k * lo],
                    dst_ref=back.at[me],
                    send_sem=back_send.at[k * lo + c],
                    recv_sem=back_recv.at[me],
                    device_id=core,
                    device_id_type=MESH,
                ).wait_send()

            if c == 0:
                pl.when(h != k)(leave_wait)
            else:
                leave_wait()

    for at in range(group):

        @pl.when(me != at)
        def _():
            pltpu.make_async_remote_copy(
                src_ref=back.at[at],
                dst_ref=back.at[at],
                send_sem=back_send.at[0],
                recv_sem=back_recv.at[at],
                device_id=core,
                device_id_type=MESH,
            ).wait_recv()

    for at in range(group):
        out[:, at, :] = back[at].astype(f32)


def fused(sizes, gy, *args):
    src, slot_rows, owner, _, _, vander, test_fn, inv, trace, lift, speeds = args
    hi, rep, lo = sizes
    members, points = slot_rows.shape
    modes, columns = src.shape
    slot_count = owner.shape[0]
    group = hi * lo
    strip = gy * members
    half = hi * strip
    faces = trace.shape[1]
    width = slot_count * members
    bf16, f32 = jnp.bfloat16, jnp.float32
    any_, vmem = pl.BlockSpec(memory_space=pl.ANY), pl.BlockSpec(memory_space=pltpu.VMEM)
    smem = pl.BlockSpec(memory_space=pltpu.SMEM)
    dma = pltpu.SemaphoreType.DMA
    like = lambda a: pltpu.VMEM(a.shape, a.dtype)
    slot_sends = 8 + lo * 5
    return pl.pallas_call(
        functools.partial(fused_kernel, sizes, gy),
        out_shape=pltpu.VMEM((members, columns // members, modes), f32),
        in_specs=[any_, any_, vmem, vmem, vmem, any_, any_, any_, any_, any_, smem],
        out_specs=vmem,
        scratch_shapes=[
            like(src),
            like(slot_rows),
            like(vander),
            like(test_fn),
            like(inv),
            like(trace),
            like(lift),
            pltpu.VMEM(inv.shape, bf16),
            pltpu.VMEM(inv.shape, bf16),
            pltpu.VMEM((modes, 2 * faces), bf16),
            pltpu.VMEM(lift.shape, bf16),
            pltpu.VMEM((group, members, modes), bf16),
            pltpu.VMEM((group, members, modes), bf16),
            pltpu.VMEM((group, members, points), bf16),
            pltpu.VMEM((8, width), f32),
            pltpu.VMEM((group, 8, width), f32),
            pltpu.VMEM((2, half, hi * width), bf16),
            pltpu.VMEM((2, half, modes), f32),
            pltpu.VMEM((half, modes), bf16),
            pltpu.VMEM((half, modes), bf16),
            pltpu.VMEM((half, faces), f32),
            pltpu.VMEM((half, faces), f32),
            pltpu.VMEM((half + 2 * strip, faces), f32),
            pltpu.VMEM((group, members, modes), bf16),
            pltpu.VMEM((group, members, modes), bf16),
            dma((7,)),
            dma((slot_sends,)),
            dma((group,)),
            dma((group,)),
            dma((group,)),
            dma((group,)),
            dma((group,)),
            dma((2,)),
            dma((2,)),
            dma((group,)),
            dma((group,)),
        ],
        compiler_params=pltpu.CompilerParams(
            collective_id=2, has_side_effects=True, vmem_limit_bytes=56 << 20
        ),
        name="remap",
    )(*args)


def fused_device(sizes, gy, src_coef, point_slot, tgt_owner, tgt_local, vander, test_fn, inv_mass, jacobian, trace_tab, lift_tab, wave_speed):
    return fused(
        sizes,
        gy,
        src_coef,
        point_slot.T,
        tgt_owner.T,
        tgt_local.T,
        jacobian[None, :],
        vander,
        test_fn,
        inv_mass,
        trace_tab,
        lift_tab,
        wave_speed,
    )


def solution(mesh):
    gx, gy = mesh.shape["gx"], mesh.shape["gy"]
    devices = gx * gy

    def call(*args):
        fields = args[-1].shape[0]
        sizes = (fields // gy, devices // fields, gy)
        body = functools.partial(per_device, gx, gy)
        if sizes == (4, 2, 4):
            body = functools.partial(fused_device, sizes, gy)
        return jax.shard_map(
            body,
            mesh=Mesh(mesh.devices.reshape(sizes), WORLD),
            in_specs=(
                P(None, WORLD),
                P(None, WORLD),
                P(WORLD, None),
                P(WORLD, None),
                P(),
                P(),
                P(),
                P(WORLD),
                P(),
                P(),
                P(),
            ),
            out_specs=P(WORLD, None, None),
            check_vma=False,
        )(*args)

    return call
```
